32 devices in a mesh: fsdp: 4 (over y, core), ctx: 4 (over z), tp: 2 (over x).
Axes of the slice: x: 2, y: 2, z: 4, core: 2. Of those that a mesh axis runs over, the one named last changes fastest.
Arguments:
- inputs: bfloat16 [16, 320, 1024], P('fsdp', 'ctx'), may hold values from -6 to 6
- lengths: int32 [16], P('fsdp'), may hold values from 224 to 320, as said below
- ln1_gain: bfloat16 [1024], P('fsdp'), may hold values from 0.5 to 1.5
- ln1_bias: bfloat16 [1024], P('fsdp'), may hold values from -3 to 3
- w_qkv: bfloat16 [1024, 3, 1024], P('fsdp', None, 'tp'), may hold values from -0.1875 to 0.1875
- qv_bias: bfloat16 [2, 1024], P(None, 'fsdp'), may hold values from -3 to 3
- w_out: bfloat16 [1024, 1024], P('tp', 'fsdp'), may hold values from -1.5 to 1.5
- out_bias: bfloat16 [1024], P('fsdp'), may hold values from -3 to 3
- ln2_gain: bfloat16 [1024], P('fsdp'), may hold values from 0.5 to 1.5
- ln2_bias: bfloat16 [1024], P('fsdp'), may hold values from -3 to 3
- w_up: bfloat16 [1024, 4096], P('fsdp', 'tp'), may hold values from -0.1875 to 0.1875
- up_bias: bfloat16 [4096], P('fsdp'), may hold values from -3 to 3
- w_down: bfloat16 [4096, 1024], P('tp', 'fsdp'), may hold values from -0.09375 to 0.09375
- down_bias: bfloat16 [1024], P('fsdp'), may hold values from -3 to 3
- cotangent: bfloat16 [16, 320, 1024], P('fsdp', 'ctx'), may hold values from -6 to 6
Outputs:
- output: bfloat16 [16, 320, 1024], P('fsdp', 'ctx')
- grad_inputs: float32 [16, 320, 1024], P('fsdp', 'ctx')
- grad_ln1_gain: float32 [1024], P('fsdp')
- grad_ln1_bias: float32 [1024], P('fsdp')
- grad_w_qkv: float32 [1024, 3, 1024], P('fsdp', None, 'tp')
- grad_qv_bias: float32 [2, 1024], P(None, 'fsdp')
- grad_w_out: float32 [1024, 1024], P('tp', 'fsdp')
- grad_out_bias: float32 [1024], P('fsdp')
- grad_ln2_gain: float32 [1024], P('fsdp')
- grad_ln2_bias: float32 [1024], P('fsdp')
- grad_w_up: float32 [1024, 4096], P('fsdp', 'tp')
- grad_up_bias: float32 [4096], P('fsdp')
- grad_w_down: float32 [4096, 1024], P('tp', 'fsdp')
- grad_down_bias: float32 [1024], P('fsdp')
The draws below stay inside these ranges and needn't reach their ends.
Inputs may be any that keep to these rules, and one draw needn't show every extreme that they name: `lengths`: among the 4 images of each index of fsdp one has length 320; some image has length 224.
All inputs are finite; a program needn't handle non-finite values.
Results may differ from the reference program's by a relative error of at most 0.02.
Values may be sent and summed in bfloat16 or wider, within the bound.
No kernel may reach another device: no remote copies, remote signals or barrier semaphores. Data moves between devices by JAX's collectives and lax.ppermute only.
A program may use at most 128 MiB of HBM per device.

```python
import math
import jax
import jax.numpy as jnp
from jax import lax

D = 1024
HEADS = 16
HD = 64
FF = 4096
SLOTS = 320
MIN_LEN = 224
IMG_DEV = 4
IMAGES = 16


def draw_lengths(key, part):
    key = jax.random.fold_in(key, 11)
    subkeys = jax.random.split(key, 4)
    groups = IMAGES // IMG_DEV
    base = jax.random.randint(subkeys[0], (IMAGES,), MIN_LEN, SLOTS + 1)
    longest = jax.random.randint(subkeys[1], (groups,), 0, IMG_DEV)
    index = jnp.arange(IMAGES)
    position = index % IMG_DEV
    group_id = index // IMG_DEV
    is_long = position == longest[group_id]
    short_group = jax.random.randint(subkeys[2], (), 0, groups)
    offset = 1 + jax.random.randint(subkeys[3], (), 0, max(IMG_DEV - 1, 1))
    short_place = (longest[short_group] + offset) % IMG_DEV
    is_short = (group_id == short_group) & (position == short_place) & jnp.logical_not(is_long)
    return jnp.where(is_long, SLOTS, jnp.where(is_short, MIN_LEN, base)).astype(jnp.int32)


def level_of(rng, shape, cuts, low, top_value):
    factor_of, own = 1.0, jax.random.fold_in(rng, 6)
    for dim, blocks in cuts:
        draws = jnp.exp(jax.random.uniform(jax.random.fold_in(own, dim), (blocks,), jnp.float32, low / len(cuts), top_value / len(cuts)))
        factor_of = factor_of * jnp.repeat(draws, shape[dim] // blocks).reshape([-1 if axis == dim else 1 for axis in range(len(shape))])
    return factor_of


def scatter_about(key, dims, width, bound, pieces=(), dtype=jnp.bfloat16):
    array = width * jax.random.normal(key, dims, jnp.float32)
    if pieces:
        array = array * level_of(key, dims, pieces, -0.22, 0.18)
    return jnp.clip(array, -bound, bound).astype(dtype)


def setup_inputs(seed: int = 0) -> dict:
    keys = jax.random.split(jax.random.key(seed), 16)
    inputs = scatter_about(keys[0], (IMAGES, SLOTS, D), 1.0, 6.0, ((0, 4), (1, 4)))
    lengths = draw_lengths(jax.random.fold_in(keys[15], 71), 0)
    ln1_gain = jnp.clip(1.0 + 0.1 * jax.random.normal(keys[2], (D,), jnp.float32), 0.5, 1.5).astype(jnp.bfloat16)
    ln1_bias = scatter_about(keys[3], (D,), 0.5, 3.0, ((0, 4),))
    w_qkv = scatter_about(keys[4], (D, 3, D), D ** -0.5, 0.1875, ((0, 4), (2, 2)))
    qv_bias = scatter_about(keys[5], (2, D), 0.5, 3.0, ((1, 4),))
    w_out = scatter_about(keys[6], (D, D), (D // 64) ** -0.5, 1.5, ((0, 2), (1, 4)))
    out_bias = scatter_about(keys[7], (D,), 0.5, 3.0, ((0, 4),))
    ln2_gain = jnp.clip(1.0 + 0.1 * jax.random.normal(keys[8], (D,), jnp.float32), 0.5, 1.5).astype(jnp.bfloat16)
    ln2_bias = scatter_about(keys[9], (D,), 0.5, 3.0, ((0, 4),))
    w_up = scatter_about(keys[10], (D, FF), D ** -0.5, 0.1875, ((0, 4), (1, 2)))
    up_bias = scatter_about(keys[11], (FF,), 0.5, 3.0, ((0, 4),))
    w_down = scatter_about(keys[12], (FF, D), FF ** -0.5, 0.09375, ((0, 2), (1, 4)))
    down_bias = scatter_about(keys[13], (D,), 0.5, 3.0, ((0, 4),))
    cotangent = scatter_about(keys[14], (IMAGES, SLOTS, D), 1.0, 6.0, ((0, 4), (1, 4)))
    return {"inputs": inputs, "lengths": lengths, "ln1_gain": ln1_gain, "ln1_bias": ln1_bias, "w_qkv": w_qkv, "qv_bias": qv_bias, "w_out": w_out, "out_bias": out_bias, "ln2_gain": ln2_gain, "ln2_bias": ln2_bias, "w_up": w_up, "up_bias": up_bias, "w_down": w_down, "down_bias": down_bias, "cotangent": cotangent}


@jax.custom_vjp
def low(v):
    return lax.optimization_barrier(v.astype(jnp.bfloat16)).astype(jnp.float32)

@jax.custom_vjp
def low_back(v):
    return v

def low_keep(v):
    return (low(v), None)

def low_pass(kept, grad):
    return (grad,)

def back_keep(v):
    return (v, None)

def back_low(kept, grad):
    return (low(grad),)
low.defvjp(low_keep, low_pass)
low_back.defvjp(back_keep, back_low)
epsilon = 1e-06
exact = lax.Precision.HIGHEST

def layer_norm(values, gain, shift):
    center = values - lax.optimization_barrier(jnp.mean(values, axis=-1, keepdims=True))
    spread = lax.optimization_barrier(jnp.mean(center * center, axis=-1, keepdims=True))
    return center * lax.rsqrt(spread + epsilon) * gain + shift

def encoder_block(tokens, image_lengths, params):
    gain_one, shift_one, w_qkv, qv_bias, w_out, out_bias, gain_two, shift_two, w_up, up_bias, w_down, down_bias = params
    count = tokens.shape[0]
    live = (jnp.arange(SLOTS)[None, :] < image_lengths[:, None]).astype(jnp.float32)
    masked = tokens * live[:, :, None]
    normed = low(layer_norm(masked, gain_one, shift_one))
    project = jnp.einsum('gsd,dke->gske', normed, w_qkv, precision=exact)
    queries = low(low_back(project[:, :, 0] + qv_bias[0]))
    keys_all = low(low_back(project[:, :, 1]))
    values_all = low(low_back(project[:, :, 2] + qv_bias[1]))
    head_shape = (count, SLOTS, HEADS, HD)
    raw = jnp.einsum('gqhe,gkhe->ghqk', queries.reshape(head_shape), keys_all.reshape(head_shape), precision=exact) * HD ** (-0.5)
    raw = low_back(raw)
    scores = jnp.where(live[:, None, None, :] > 0, raw, -1e+30)
    highest = lax.optimization_barrier(jnp.max(scores, axis=-1, keepdims=True))
    expo = jnp.exp(scores - highest)
    attn_prob = expo / lax.optimization_barrier(jnp.sum(expo, axis=-1, keepdims=True))
    mixed = jnp.einsum('ghqk,gkhe->gqhe', low(attn_prob), values_all.reshape(head_shape), precision=exact)
    mixed = low(low_back(mixed.reshape(count, SLOTS, HEADS * HD)))
    branch = low_back(jnp.einsum('gsk,kd->gsd', mixed, w_out, precision=exact) + out_bias)
    middle = masked + branch
    normed_two = low(layer_norm(middle, gain_two, shift_two))
    hidden = low_back(jnp.einsum('gsd,df->gsf', normed_two, w_up, precision=exact) + up_bias)
    active = low(jax.nn.gelu(hidden))
    ffn_out = low_back(jnp.einsum('gsf,fd->gsd', active, w_down, precision=exact) + down_bias)
    return (middle + ffn_out) * live[:, :, None]

def reference(inputs, lengths, ln1_gain, ln1_bias, w_qkv, qv_bias, w_out, out_bias, ln2_gain, ln2_bias, w_up, up_bias, w_down, down_bias, cotangent):
    params = tuple((weight_arg.astype(jnp.float32) for weight_arg in (ln1_gain, ln1_bias, w_qkv, qv_bias, w_out, out_bias, ln2_gain, ln2_bias, w_up, up_bias, w_down, down_bias)))
    group = math.gcd(IMAGES, 8)
    blocks = IMAGES // group

    def forward(values, weights):

        def per_group(pair_entry):
            return encoder_block(pair_entry[0], pair_entry[1], weights)
        result = lax.map(jax.checkpoint(per_group), (values.reshape(blocks, group, SLOTS, D), lengths.reshape(blocks, group)))
        return result.reshape(IMAGES, SLOTS, D)
    result, pull = jax.vjp(forward, inputs.astype(jnp.float32), params)
    grad_inputs, grads = pull(cotangent.astype(jnp.float32))
    return (result.astype(jnp.bfloat16), grad_inputs, grads[0], grads[1], grads[2], grads[3], grads[4], grads[5], grads[6], grads[7], grads[8], grads[9], grads[10], grads[11])
```

```python
import functools

import jax
import jax.numpy as jnp
from jax import lax
from jax.sharding import PartitionSpec as P

HD = 64
epsilon = 1e-06
f32 = jnp.float32
bf16 = jnp.bfloat16


def bits_of(n):
    out, bit = [], 1
    while bit < n:
        out.append(bit)
        bit *= 2
    return out


def bitrev(n):
    order = [0]
    for bit in reversed(bits_of(n)):
        order = order + [j | bit for j in order]
    return order


def swap(x, axis, bit):
    return lax.ppermute(x, axis, [(i, i ^ bit) for i in range(lax.axis_size(axis))])


def gather(piece, axis, dim):
    for bit in reversed(bits_of(lax.axis_size(axis))):
        piece = jnp.concatenate([piece, swap(piece, axis, bit)], axis=dim)
    return piece


def halves(x, dim):
    return jnp.split(x, 2, axis=dim)


def scatter_sum(make, axis, dim):
    bits = bits_of(lax.axis_size(axis))
    got = swap(make(1).astype(bf16), axis, bits[0])
    total = (make(0) + got.astype(f32)).astype(bf16)
    for bit in bits[1:]:
        low, high = halves(total, dim)
        total = (low.astype(f32) + swap(high, axis, bit).astype(f32)).astype(bf16)
    return total


def line_sum(x, axis):
    n = lax.axis_size(axis)
    me = lax.axis_index(axis)
    half = n // 2
    for k in range(half - 1):
        got = lax.ppermute(x, axis, [(k, k + 1), (n - 1 - k, n - 2 - k)])
        x = (x.astype(f32) + got.astype(f32)).astype(bf16)
    got = lax.ppermute(x, axis, [(half - 1, half), (half, half - 1)])
    x = (x.astype(f32) + got.astype(f32)).astype(bf16)
    for k in range(half - 2, -1, -1):
        got = lax.ppermute(x, axis, [(k + 1, k), (n - 2 - k, n - 1 - k)])
        x = jnp.where((me == k) | (me == n - 1 - k), got, x)
    return x


def normalize(values):
    center = values - jnp.mean(values, axis=-1, keepdims=True)
    rate = lax.rsqrt(jnp.mean(center * center, axis=-1, keepdims=True) + epsilon)
    return center * rate, rate


def norm_back(grad, gain, unit, rate):
    e = grad * gain
    return rate * (e - jnp.mean(e, axis=-1, keepdims=True) - unit * jnp.mean(e * unit, axis=-1, keepdims=True))


def local(
    inputs,
    lengths,
    ln1_gain,
    ln1_bias,
    w_qkv,
    qv_bias,
    w_out,
    out_bias,
    ln2_gain,
    ln2_bias,
    w_up,
    up_bias,
    w_down,
    down_bias,
    cotangent,
):
    nf, nc, nt = (lax.axis_size(a) for a in ("fsdp", "ctx", "tp"))
    f, c, t = (lax.axis_index(a) for a in ("fsdp", "ctx", "tp"))
    images, own_slots, width = inputs.shape
    per = images // nc
    slots = own_slots * nc
    rows = per * slots
    block = width // nf
    order = bitrev(nf)
    head_cols = w_qkv.shape[2]
    heads = head_cols // HD
    ff_cols = w_up.shape[1]
    scale = HD**-0.5

    def to_relative(x):
        return jnp.concatenate([lax.dynamic_slice_in_dim(x, (f ^ j) * block, block, x.ndim - 1) for j in order], axis=-1)

    def from_relative(x):
        parts = [order.index(j) for j in range(nf)]
        table = jnp.array(parts, jnp.int32)
        return jnp.concatenate(
            [lax.dynamic_slice_in_dim(x, table[f ^ b] * block, block, x.ndim - 1) for b in range(nf)], axis=-1
        )

    def to_images(x):
        x = to_relative(x).reshape(nc, per, own_slots, width)
        out = [lax.dynamic_index_in_dim(x, c, 0, False)]
        for s in range(1, nc):
            out.append(swap(lax.dynamic_index_in_dim(x, c ^ s, 0, False), "ctx", s))
        return jnp.stack(out, axis=1).reshape(rows, width)

    def from_images(x):
        x = x.reshape(per, nc, own_slots, width)
        out = [x[:, 0]] + [swap(x[:, s], "ctx", s) for s in range(1, nc)]
        stack = jnp.stack(out)
        return jnp.concatenate([lax.dynamic_index_in_dim(stack, c ^ i, 0, False) for i in range(nc)], axis=0)

    tokens = to_images(inputs)
    qkv_full = gather(w_qkv, "fsdp", 0)
    small = jnp.concatenate(
        [v[None] for v in (ln1_gain, ln1_bias, ln2_gain, ln2_bias, out_bias, down_bias)]
        + [qv_bias, up_bias.reshape(-1, block)]
    )
    n_up = up_bias.shape[0] // block
    small_full = gather(small[None], "fsdp", 0).astype(f32)
    gain_one, shift_one, gain_two, shift_two, out_shift, down_shift = (small_full[:, i].reshape(width) for i in range(6))
    table = jnp.array([order.index(j) for j in range(nf)], jnp.int32)
    mine = [table[f ^ (t * (nf // nt) + i)] for i in range(nf // nt)]
    half_blocks = [lax.dynamic_index_in_dim(small_full, p, 0, False) for p in mine]
    query_shift = jnp.concatenate([b[6] for b in half_blocks])
    value_shift = jnp.concatenate([b[7] for b in half_blocks])
    up_shift = jnp.concatenate([b[8:].reshape(-1) for b in half_blocks])
    out_full = gather(w_out, "fsdp", 1)
    up_full = gather(w_up, "fsdp", 0)
    down_full = gather(w_down, "fsdp", 1)
    cot = to_images(cotangent)

    own_lengths = lax.dynamic_slice_in_dim(lengths, c * per, per)
    slot_ids = jnp.concatenate([(c ^ s) * own_slots + jnp.arange(own_slots) for s in range(nc)])
    live_slots = slot_ids[None, :] < own_lengths[:, None]
    live = live_slots.astype(f32).reshape(rows, 1)

    masked = tokens.astype(f32) * live
    unit_one, rate_one = normalize(masked)
    normed = (unit_one * gain_one + shift_one).astype(bf16)
    project = jnp.einsum("nd,dke->nke", normed, qkv_full, preferred_element_type=f32)
    queries = (project[:, 0] + query_shift).astype(bf16).reshape(per, slots, heads, HD)
    keys = project[:, 1].astype(bf16).reshape(per, slots, heads, HD)
    values = (project[:, 2] + value_shift).astype(bf16).reshape(per, slots, heads, HD)
    raw = jnp.einsum("bqhe,bkhe->bhqk", queries, keys, preferred_element_type=f32) * scale
    scores = jnp.where(live_slots[:, None, None, :], raw, -1e30)
    expo = jnp.exp(scores - jnp.max(scores, axis=-1, keepdims=True))
    attn_prob = expo / jnp.sum(expo, axis=-1, keepdims=True)
    prob_low = attn_prob.astype(bf16)
    mixed = (
        jnp.einsum("bhqk,bkhe->bqhe", prob_low, values, preferred_element_type=f32).reshape(rows, head_cols).astype(bf16)
    )

    def tp_sum(x):
        return x.astype(f32) + swap(x, "tp", 1).astype(f32)

    branch = tp_sum(jnp.dot(mixed, out_full, preferred_element_type=f32).astype(bf16)) + out_shift
    middle = masked + branch
    unit_two, rate_two = normalize(middle)
    normed_two = (unit_two * gain_two + shift_two).astype(bf16)
    hidden = jnp.dot(normed_two, up_full, preferred_element_type=f32) + up_shift
    active, gelu_pull = jax.vjp(jax.nn.gelu, hidden)
    active_low = active.astype(bf16)
    grad_final = cot.astype(f32) * live
    grad_final_low = grad_final.astype(bf16)
    grad_active = jnp.einsum("nd,fd->nf", grad_final_low, down_full, preferred_element_type=f32)
    grad_hidden = gelu_pull(grad_active)[0].astype(bf16)
    grad_normed_two = tp_sum(jnp.einsum("nf,df->nd", grad_hidden, up_full, preferred_element_type=f32).astype(bf16))
    ffn_out = tp_sum(jnp.dot(active_low, down_full, preferred_element_type=f32).astype(bf16)) + down_shift
    result = from_relative(from_images(((middle + ffn_out) * live).astype(bf16)))

    def columns(x, h):
        return halves(x, 1)[h]

    def shard_sum(make, dim):
        return line_sum(scatter_sum(make, "fsdp", dim), "ctx")

    grad_w_down = shard_sum(
        lambda h: jnp.einsum("nf,nd->fd", active_low, columns(grad_final_low, h), preferred_element_type=f32), 1
    )
    grad_w_up = shard_sum(
        lambda h: jnp.einsum("nd,nf->df", columns(normed_two, h), grad_hidden, preferred_element_type=f32), 0
    )

    grad_middle = grad_final + norm_back(grad_normed_two, gain_two, unit_two, rate_two)
    grad_branch_low = grad_middle.astype(bf16)
    grad_w_out = shard_sum(
        lambda h: jnp.einsum("nk,nd->kd", mixed, columns(grad_branch_low, h), preferred_element_type=f32), 1
    )
    grad_mixed = (
        jnp.einsum("nd,kd->nk", grad_branch_low, out_full, preferred_element_type=f32)
        .astype(bf16)
        .reshape(per, slots, heads, HD)
    )
    grad_values = jnp.einsum("bhqk,bqhe->bkhe", prob_low, grad_mixed, preferred_element_type=f32)
    grad_prob = jnp.einsum("bqhe,bkhe->bhqk", grad_mixed, values, preferred_element_type=f32)
    row_center = jnp.sum(attn_prob * grad_prob, axis=-1, keepdims=True)
    grad_scores = (attn_prob * (grad_prob - row_center)).astype(bf16)
    grad_queries = jnp.einsum("bhqk,bkhe->bqhe", grad_scores, keys, preferred_element_type=f32) * scale
    grad_keys = jnp.einsum("bhqk,bqhe->bkhe", grad_scores, queries, preferred_element_type=f32) * scale
    grad_project = jnp.stack(
        [g.reshape(rows, head_cols).astype(bf16) for g in (grad_queries, grad_keys, grad_values)], axis=1
    )
    grad_normed_part = jnp.einsum("nke,dke->nd", grad_project, qkv_full, preferred_element_type=f32)
    grad_normed = tp_sum(grad_normed_part.astype(bf16))
    grad_w_qkv = shard_sum(
        lambda h: jnp.einsum("nd,nke->dke", columns(normed, h), grad_project, preferred_element_type=f32), 0
    )
    grad_masked = norm_back(grad_normed, gain_one, unit_one, rate_one)
    grad_inputs = from_relative(from_images(((grad_middle + grad_masked) * live).astype(bf16))).astype(f32)

    first = (t == 0).astype(f32)
    whole = [
        jnp.sum(grad_normed_part * unit_one, axis=0),
        jnp.sum(grad_normed_part, axis=0),
        jnp.sum(grad_normed_two * unit_two, axis=0) * first,
        jnp.sum(grad_normed_two, axis=0) * first,
        jnp.sum(grad_branch_low.astype(f32), axis=0) * first,
        jnp.sum(grad_final_low.astype(f32), axis=0) * first,
    ]
    pack = jnp.stack([v.reshape(nf, block) for v in whole], axis=1)
    qv_sum = jnp.sum(grad_project.astype(f32), axis=0)
    up_sum = jnp.sum(grad_hidden.astype(f32), axis=0)
    part = jnp.concatenate(
        [
            qv_sum[0].reshape(nf // nt, 1, block),
            qv_sum[2].reshape(nf // nt, 1, block),
            up_sum.reshape(nf // nt, n_up, block),
        ],
        axis=1,
    )
    spread = jnp.zeros((nf, 2 + n_up, block), f32)
    for i, p in enumerate(mine):
        spread = lax.dynamic_update_slice_in_dim(spread, part[i : i + 1], p, 0)
    pack = jnp.concatenate([pack, spread], axis=1)
    total = line_sum(scatter_sum(lambda h: halves(pack, 0)[h], "fsdp", 0), "ctx")
    total = tp_sum(total)[0]
    return (
        result,
        grad_inputs,
        total[0],
        total[1],
        grad_w_qkv.astype(f32),
        total[6:8],
        grad_w_out.astype(f32),
        total[4],
        total[2],
        total[3],
        grad_w_up.astype(f32),
        total[8:].reshape(-1),
        grad_w_down.astype(f32),
        total[5],
    )


def solution(mesh):
    in_specs = (
        P("fsdp", "ctx", None),
        P("fsdp"),
        P("fsdp"),
        P("fsdp"),
        P("fsdp", None, "tp"),
        P(None, "fsdp"),
        P("tp", "fsdp"),
        P("fsdp"),
        P("fsdp"),
        P("fsdp"),
        P("fsdp", "tp"),
        P("fsdp"),
        P("tp", "fsdp"),
        P("fsdp"),
        P("fsdp", "ctx", None),
    )
    out_specs = (
        P("fsdp", "ctx", None),
        P("fsdp", "ctx", None),
        P("fsdp"),
        P("fsdp"),
        P("fsdp", None, "tp"),
        P(None, "fsdp"),
        P("tp", "fsdp"),
        P("fsdp"),
        P("fsdp"),
        P("fsdp"),
        P("fsdp", "tp"),
        P("fsdp"),
        P("tp", "fsdp"),
        P("fsdp"),
    )
    return jax.shard_map(local, mesh=mesh, in_specs=in_specs, out_specs=out_specs, check_vma=False)
```

```python
import functools

import jax
import jax.numpy as jnp
from jax import lax
from jax.experimental import pallas as pl
from jax.experimental.pallas import tpu as pltpu
from jax.sharding import PartitionSpec as P

HD = 64
epsilon = 1e-06
f32 = jnp.float32
bf16 = jnp.bfloat16
PACK = 16
CHUNK = 512


def bits_of(n):
    out, bit = [], 1
    while bit < n:
        out.append(bit)
        bit *= 2
    return out


def bitrev(n):
    order = [0]
    for bit in reversed(bits_of(n)):
        order = order + [j | bit for j in order]
    return order


def place(x, n):
    bits = len(bits_of(n))
    out = 0
    for k in range(bits):
        out = out + ((x >> k) & 1) * (1 << (bits - 1 - k))
    return out


def swap(x, axis, bit):
    return lax.ppermute(x, axis, [(i, i ^ bit) for i in range(lax.axis_size(axis))])


def gather(pieces, axis):
    for bit in reversed(bits_of(lax.axis_size(axis) // len(pieces))):
        pieces = pieces + [swap(p, axis, bit) for p in pieces]
    return pieces


def first_swap(piece, axis):
    return swap(piece, axis, bits_of(lax.axis_size(axis))[-1])


class ShardSum:
    def __init__(self, run, cuts):
        self.run, self.cuts, self.n, self.got = run, cuts, lax.axis_size("fsdp"), []

    def begin(self, level):
        n = self.n >> level
        return self.run(n // 2, n, self.got, self.cuts if level == 0 else 1)

    def send(self, blocks, level):
        self.got.append([[swap(x, "fsdp", 1 << level) for x in pieces] for pieces in blocks])

    def step(self, level):
        self.send(self.begin(level), level)

    def own(self):
        return self.run(0, 1, self.got, self.cuts)[0]


def leaves(tree):
    return jax.tree.leaves(tree)


def tie(*trees):
    flat, where = jax.tree.flatten(trees)
    return jax.tree.unflatten(where, lax.optimization_barrier(flat))


def line_step(x, axis, number):
    assert lax.axis_size(axis) == 4
    pairs = ([(0, 1), (3, 2)], [(1, 2), (2, 1)], [(1, 0), (2, 3)])[number]
    return lax.ppermute(x, axis, pairs)


def line_add(idx, x, got):
    (out,) = call(add_kernel, [jax.ShapeDtypeStruct(x.shape, bf16)], [idx, x, got])
    return out


NN = (((1,), (0,)), ((), ()))
NT = (((1,), (1,)), ((), ()))
TN = (((0,), (0,)), ((), ()))


def mm(a, b, dims=NN):
    return lax.dot_general(a, b, dims, preferred_element_type=f32)


def call(kernel, outs, args, scratch=(), mib=12):
    vm = pl.BlockSpec(memory_space=pltpu.VMEM)
    return pl.pallas_call(
        kernel,
        out_shape=outs,
        in_specs=[pl.BlockSpec(memory_space=pltpu.SMEM)] + [vm] * (len(args) - 1),
        out_specs=[vm] * len(outs),
        scratch_shapes=list(scratch),
        compiler_params=pltpu.CompilerParams(vmem_limit_bytes=mib << 20),
        cost_estimate=pl.CostEstimate(flops=0, bytes_accessed=0, transcendentals=0),
    )(*args)


def rows_of(small, r):
    return jnp.concatenate([small[p].astype(f32)[r : r + 1] for p in range(small.shape[0])], axis=1)


def live_rows(idx, s, n):
    return (idx[1] ^ s) * n + lax.broadcasted_iota(jnp.int32, (n, 1), 0) < idx[3]


def live_keys(idx, nc, n):
    col = lax.broadcasted_iota(jnp.int32, (1, nc * n), 1)
    slot = col
    for s in range(nc):
        slot = jnp.where((col >= s * n) & (col < (s + 1) * n), slot + ((idx[1] ^ s) - s) * n, slot)
    return slot < idx[3]


def to_relative(idx, x, box):
    nf, _, block = box.shape
    for b in range(nf):
        box[place(idx[0] ^ b, nf)] = x[:, b * block : (b + 1) * block]
    return jnp.concatenate([box[p] for p in range(nf)], axis=1)


def from_relative(idx, x, box):
    nf, _, block = box.shape
    for p in range(nf):
        box[p] = x[:, p * block : (p + 1) * block]
    return jnp.concatenate([box[place(idx[0] ^ b, nf)] for b in range(nf)], axis=1)


def mean(x):
    return jnp.mean(x, axis=-1, keepdims=True)


def normalize(x):
    center = x - mean(x)
    rate = lax.rsqrt(mean(center * center) + epsilon)
    return center * rate, rate


def norm_back(grad, gain, unit, rate):
    e = grad * gain
    return rate * (e - mean(e) - unit * mean(e * unit))


def softmax_of(q, k, keep, scale):
    scores = jnp.where(keep, mm(q, k, NT) * scale, -1e30)
    expo = jnp.exp(scores - jnp.max(scores, axis=-1, keepdims=True))
    return expo * (1.0 / jnp.sum(expo, axis=-1, keepdims=True))


def sides(n):
    lane = lax.broadcasted_iota(jnp.int32, (1, n), 1)
    return [(lane >= h * HD) & (lane < (h + 1) * HD) for h in range(n // HD)]


def only(keep, x):
    return jnp.where(keep, x.astype(f32), 0.0).astype(x.dtype)


def merge(keeps, parts):
    out = parts[0]
    for keep, part in zip(keeps[1:], parts[1:]):
        out = jnp.where(keep, part, out)
    return out


def fold(x, block, width):
    k = width // block
    rows = x.shape[0] // k
    return jnp.concatenate([x[i * rows : (i + 1) * rows] for i in range(k)], axis=1)


def unfold(x, block):
    return jnp.concatenate([x[:, i * block : (i + 1) * block] for i in range(x.shape[1] // block)], axis=0)


def pack_kernel(wo, *refs):
    *vectors, qv, up, out = refs
    block = qv.shape[1]
    out[:block] = fold(wo[...], block, out.shape[1])
    lines = [x[...].astype(f32).reshape(1, block) for x in vectors] + [qv[...].astype(f32), up[...].astype(f32)]
    lines.append(jnp.zeros((PACK - 8 - up.shape[0], block), f32))
    out[block:, :block] = jnp.concatenate(lines, axis=0).astype(bf16)
    out[block:, block:] = jnp.zeros((PACK, out.shape[1] - block), bf16)


def attend_kernel(nc, nf, nt, n_up, *refs):
    idx, refs = refs[0], refs[1:]
    toks, wq, aux = refs[:nc], refs[nc : nc + nf], refs[nc + nf : nc + 2 * nf]
    masked, unit1, rate1, normed, q, k, v, mixed, *branch, up_shift, small, box = refs[nc + 2 * nf :]
    n = toks[0].shape[0]
    block = small.shape[2]
    for p in range(nf):
        small[p] = aux[p][block:, :block]
    hc = q.shape[1]
    gain, shift = rows_of(small, 0), rows_of(small, 1)
    for s in range(nc):
        here = slice(s * n, (s + 1) * n)
        x = jnp.where(live_rows(idx, s, n), toks[s][...].astype(f32), 0.0)
        x = to_relative(idx, x, box)
        masked[here, :] = x.astype(bf16)
        unit, rate = normalize(x)
        unit1[here, :] = unit
        rate1[here, :] = jnp.broadcast_to(rate, (n, 128))
        normed[here, :] = (unit * gain + shift).astype(bf16)
    shifts = []
    for i in range(nf // nt):
        mine = small[place(idx[0] ^ (idx[2] * (nf // nt) + i), nf)].astype(f32)
        shifts.append((mine[6:7], mine[7:8]))
        for r in range(n_up):
            up_shift[:, (i * n_up + r) * block : (i * n_up + r + 1) * block] = mine[8 + r : 9 + r]
    q_shift = jnp.concatenate([a for a, _ in shifts], axis=1)
    v_shift = jnp.concatenate([b for _, b in shifts], axis=1)
    for j, (out, bias) in enumerate(((q, q_shift), (k, None), (v, v_shift))):
        acc = mm(normed[:, :block], wq[0][j * block : (j + 1) * block])
        for p in range(1, nf):
            acc = acc + mm(normed[:, p * block : (p + 1) * block], wq[p][j * block : (j + 1) * block])
        out[...] = (acc if bias is None else acc + bias).astype(bf16)
    keep = live_keys(idx, nc, n)
    halves = sides(128)

    def pair(i, _):
        at = pl.ds(pl.multiple_of(i * 128, 128), 128)
        qp, kp, vp = q[:, at], k[:, at], v[:, at]
        parts = [mm(softmax_of(only(h, qp), kp, keep, HD**-0.5).astype(bf16), vp) for h in halves]
        mixed[:, at] = merge(halves, parts).astype(bf16)
        return 0

    lax.fori_loop(0, hc // 128, pair, 0)
    for p in range(nf):
        out_w = unfold(aux[p][:block], block)
        for h, out in enumerate(branch):
            part = mixed[h * out.shape[0] : (h + 1) * out.shape[0]]
            out[:, p * block : (p + 1) * block] = mm(part, out_w).astype(bf16)


def up_kernel(nc, nf, *refs):
    idx, masked, own_a, own_b, got_a, got_b, small, up_shift = refs[:8]
    cots, wu = refs[8 : 8 + nc], refs[8 + nc : 8 + nc + nf]
    middle, unit2, rate2, normed2, gl, active, slope, box = refs[8 + nc + nf :]
    n = cots[0].shape[0]
    block = small.shape[2]
    gain, shift, bias = rows_of(small, 2), rows_of(small, 3), rows_of(small, 4)
    for s in range(nc):
        here = slice(s * n, (s + 1) * n)
        own, got = (own_a, got_a) if s < nc // 2 else (own_b, got_b)
        part = slice(s % (nc // 2) * n, (s % (nc // 2) + 1) * n)
        x = masked[here, :].astype(f32) + (own[part, :].astype(f32) + got[part, :].astype(f32) + bias)
        middle[here, :] = x
        unit, rate = normalize(x)
        unit2[here, :] = unit
        rate2[here, :] = jnp.broadcast_to(rate, (n, 128))
        normed2[here, :] = (unit * gain + shift).astype(bf16)
        c = jnp.where(live_rows(idx, s, n), cots[s][...].astype(f32), 0.0)
        gl[here, :] = to_relative(idx, c, box).astype(bf16)
    chunk = min(CHUNK, active.shape[1])

    def step(i, _):
        at = pl.ds(pl.multiple_of(i * chunk, chunk), chunk)
        acc = mm(normed2[:, :block], wu[0][:, at])
        for p in range(1, nf):
            acc = acc + mm(normed2[:, p * block : (p + 1) * block], wu[p][:, at])
        x = acc + up_shift[:, at]
        root = 0.7978845608028654
        tanh = jnp.tanh(root * (x + 0.044715 * (x * x * x)))
        half = 0.5 * (1.0 + tanh)
        active[:, at] = (x * half).astype(bf16)
        slope[:, at] = half + 0.5 * x * (1.0 - tanh * tanh) * (root * (1.0 + 3 * 0.044715 * (x * x)))
        return 0

    lax.fori_loop(0, active.shape[1] // chunk, step, 0)


def hidden_back_kernel(nf, *refs):
    _, gl, slope = refs[:3]
    wd, wu = refs[3 : 3 + nf], refs[3 + nf : 3 + 2 * nf]
    gh, gnt, gh_sum, acc = refs[3 + 2 * nf :]
    block = wd[0].shape[1]
    chunk = min(CHUNK, gh.shape[1])
    acc[...] = jnp.zeros_like(acc)

    def step(i, _):
        at = pl.ds(pl.multiple_of(i * chunk, chunk), chunk)
        ga = mm(gl[:, :block], wd[0][at, :], NT)
        for p in range(1, nf):
            ga = ga + mm(gl[:, p * block : (p + 1) * block], wd[p][at, :], NT)
        g = (ga * slope[:, at]).astype(bf16)
        gh[:, at] = g
        gh_sum[:, at] = jnp.sum(g.astype(f32), axis=0, keepdims=True)
        for p in range(nf):
            acc[:, p * block : (p + 1) * block] += mm(g, wu[p][:, at], NT)
        return 0

    lax.fori_loop(0, gh.shape[1] // chunk, step, 0)
    gnt[...] = acc[...].astype(bf16)


def down_kernel(nf, idx, active, *refs):
    out = refs[nf]
    block = refs[0].shape[1]
    for p in range(nf):
        out[:, p * block : (p + 1) * block] = mm(active[...], refs[p][...]).astype(bf16)


def attend_back_kernel(nc, nf, *refs):
    idx, gl, own, got, unit2, rate2, small, q, k, v = refs[:10]
    aux = refs[10 : 10 + nf]
    gmid, gb, gq, gk, gv, sums, qv_sum, gm = refs[10 + nf :]
    n = gl.shape[0] // nc
    block = small.shape[2]
    hc = q.shape[1]
    gain = rows_of(small, 2)
    totals = [0.0] * 4
    for s in range(nc):
        here = slice(s * n, (s + 1) * n)
        g = own[here, :].astype(f32) + got[here, :].astype(f32)
        u = unit2[here, :]
        c = gl[here, :].astype(f32)
        x = c + norm_back(g, gain, u, rate2[here, :1])
        gmid[here, :] = x
        low = x.astype(bf16)
        gb[here, :] = low
        for r, value in enumerate((g * u, g, low.astype(f32), c)):
            totals[r] = totals[r] + jnp.sum(value, axis=0, keepdims=True)
    sums[...] = jnp.concatenate(totals + [jnp.zeros((4, gl.shape[1]), f32)], axis=0)
    acc = mm(gb[:, :block], unfold(aux[0][:block], block), NT)
    for p in range(1, nf):
        acc = acc + mm(gb[:, p * block : (p + 1) * block], unfold(aux[p][:block], block), NT)
    gm[...] = acc.astype(bf16)
    keep = live_keys(idx, nc, n)
    halves = sides(128)
    scale = HD**-0.5

    def pair(i, _):
        at = pl.ds(pl.multiple_of(i * 128, 128), 128)
        qp, kp, vp, gp = q[:, at], k[:, at], v[:, at], gm[:, at]
        dq, dk, dv = [], [], []
        for h in halves:
            prob = softmax_of(only(h, qp), kp, keep, scale)
            grad = mm(only(h, gp), vp, NT)
            dv.append(mm(prob.astype(bf16), gp, TN))
            ds = (prob * (grad - jnp.sum(prob * grad, axis=-1, keepdims=True))).astype(bf16)
            dq.append(mm(ds, kp))
            dk.append(mm(ds, qp, TN))
        a = (merge(halves, dq) * scale).astype(bf16)
        b = merge(halves, dv).astype(bf16)
        gq[:, at] = a
        gk[:, at] = (merge(halves, dk) * scale).astype(bf16)
        gv[:, at] = b
        total = [jnp.sum(x.astype(f32), axis=0, keepdims=True) for x in (a, b)]
        qv_sum[:, at] = jnp.concatenate(total + [jnp.zeros((6, 128), f32)], axis=0)
        return 0

    lax.fori_loop(0, hc // 128, pair, 0)


def normed_back_kernel(nf, nt, n_up, idx, gq, gk, gv, unit1, sums, qv_sum, gh_sum, *refs):
    wq, (gn, pack) = refs[:nf], refs[nf:]
    block = pack.shape[2]
    order = bitrev(nf)
    first = jnp.where(idx[2] == 0, 1.0, 0.0)
    held = nf // nt
    for p in range(nf):
        here = slice(p * block, (p + 1) * block)
        acc = mm(gq[...], wq[p][:block], NT) + mm(gk[...], wq[p][block : 2 * block], NT)
        acc = acc + mm(gv[...], wq[p][2 * block : 3 * block], NT)
        gn[:, here] = acc.astype(bf16)
        rows = [jnp.sum(acc * unit1[:, here], axis=0, keepdims=True), jnp.sum(acc, axis=0, keepdims=True)]
        rows += [sums[r : r + 1, here] * first for r in range(4)]
        which = (idx[0] ^ order[p]) - idx[2] * held

        def mine(of):
            out = jnp.zeros((1, block), f32)
            for i in range(held):
                out = jnp.where(which == i, of(i), out)
            return out

        rows += [mine(lambda i, r=r: qv_sum[r : r + 1, i * block : (i + 1) * block]) for r in range(2)]
        rows += [
            mine(lambda i, r=r: gh_sum[:, (i * n_up + r) * block : (i * n_up + r + 1) * block]) for r in range(n_up)
        ]
        rows.append(jnp.zeros((PACK - len(rows), block), f32))
        pack[p] = jnp.concatenate(rows, axis=0).astype(bf16)


def input_back_kernel(nc, idx, own, got, unit1, rate1, gmid, small, *refs):
    outs, box = refs[:nc], refs[nc]
    n = gmid.shape[0] // nc
    gain = rows_of(small, 0)
    for s in range(nc):
        here = slice(s * n, (s + 1) * n)
        g = own[here, :].astype(f32) + got[here, :].astype(f32)
        x = gmid[here, :] + norm_back(g, gain, unit1[here, :], rate1[here, :1])
        x = jnp.where(live_rows(idx, s, n), x, 0.0)
        outs[s][...] = from_relative(idx, x, box).astype(bf16)


def output_kernel(nc, idx, own, got, middle, small, *refs):
    outs, box = refs[:nc], refs[nc]
    n = middle.shape[0] // nc
    bias = rows_of(small, 5)
    for s in range(nc):
        here = slice(s * n, (s + 1) * n)
        x = middle[here, :] + (own[here, :].astype(f32) + got[here, :].astype(f32) + bias)
        x = jnp.where(live_rows(idx, s, n), x, 0.0)
        outs[s][...] = from_relative(idx, x, box).astype(bf16)


def assemble_kernel(nc, idx, *refs):
    out = refs[nc]
    for s in range(nc):
        out[idx[1] ^ s] = refs[s][...].astype(out.dtype)


def shard_kernel(first, last, parts, block, counts, cuts, *refs):
    refs = list(refs[1:])
    mats = [refs.pop(0) for kind in parts for _ in range(1 if kind == "small" else 2)]
    gots = [[[refs.pop(0) for _ in range(count)] for _ in range(first, last)] for count in counts]
    outs = [[refs.pop(0) for _ in range(cuts)] for _ in range(first, last)]
    wide = outs[0][0].shape[1]
    step = block // max(cuts, *counts, 1)
    for p in range(last - first):
        at, taken = 0, 0
        for kind in parts:
            here = slice((first + p) * block, (first + p + 1) * block)
            rows = PACK if kind == "small" else block
            for low in range(0, rows, step if kind == "ffn" else rows):
                size = step if kind == "ffn" else rows
                if kind == "small":
                    x = mats[taken][first + p].astype(f32)
                    x = jnp.concatenate([x, jnp.zeros((rows, wide - block), f32)], axis=1)
                elif kind == "out":
                    x = fold(mm(mats[taken][...], mats[taken + 1][:, here], TN), block, wide)
                else:
                    left = slice(here.start + low, here.start + low + size)
                    x = mm(mats[taken][:, left], mats[taken + 1][...], TN)
                for got in gots:
                    each = got[p][0].shape[0]
                    x = x + got[p][at // each][at % each : at % each + size].astype(f32)
                each = outs[p][0].shape[0]
                outs[p][at // each][at % each : at % each + size] = x.astype(bf16)
                at += size
            taken += 1 if kind == "small" else 2


def add_kernel(_, x, got, out):
    out[...] = (x[...].astype(f32) + got[...].astype(f32)).astype(bf16)


def picked(idx, own, got):
    return jnp.where(idx[4] == 1, got.astype(f32), own.astype(f32))


def finish_up_kernel(idx, *refs):
    out = refs[-1]
    rows = refs[0].shape[0]
    for i in range(len(refs) // 2):
        out[i * rows : (i + 1) * rows] = picked(idx, refs[2 * i][...], refs[2 * i + 1][...])


def finish_down_kernel(idx, *refs):
    out = refs[-1]
    rows = refs[0].shape[0]
    step = min(out.shape[0], 512)
    for i in range(len(refs) // 2):
        for j in range(0, out.shape[0], step):
            x = picked(idx, refs[2 * i][:, j : j + step], refs[2 * i + 1][:, j : j + step])
            out[j : j + step, i * rows : (i + 1) * rows] = x.T


def small_kernel(block, idx, own, got, out):
    out[...] = picked(idx, own[2 * block :, :block], got[2 * block :, :block]).astype(bf16)


def finish_kernel(block, idx, a, a_got, b, b_got, qkv, out_w):
    kv = picked(idx, a[: 2 * block], a_got[: 2 * block])
    qo = picked(idx, b[...], b_got[...])
    qkv[:block] = qo[:block]
    qkv[block:] = kv
    out_w[...] = unfold(qo[block:], block)


def shape(*dims, dtype=f32):
    return jax.ShapeDtypeStruct(dims, dtype)


def local(
    inputs,
    lengths,
    ln1_gain,
    ln1_bias,
    w_qkv,
    qv_bias,
    w_out,
    out_bias,
    ln2_gain,
    ln2_bias,
    w_up,
    up_bias,
    w_down,
    down_bias,
    cotangent,
):
    nf, nc, nt = (lax.axis_size(a) for a in ("fsdp", "ctx", "tp"))
    f, c, t = (lax.axis_index(a) for a in ("fsdp", "ctx", "tp"))
    images, n, width = inputs.shape
    assert images == nc
    rows = n * nc
    block = width // nf
    hc = w_qkv.shape[2]
    ff = w_up.shape[1]
    n_up = up_bias.shape[0] // block
    outer = (c == 0) | (c == nc - 1)
    idx = jnp.stack([f, c, t, lax.dynamic_index_in_dim(lengths, c, 0, False), outer.astype(jnp.int32)]).astype(jnp.int32)
    wide = functools.partial(shape, rows, width)

    def to_image(x):
        return [lax.dynamic_index_in_dim(x, c, 0, False)] + [
            swap(lax.dynamic_index_in_dim(x, c ^ s, 0, False), "ctx", s) for s in range(1, nc)
        ]

    vm = pl.BlockSpec(memory_space=pltpu.VMEM)
    w_proj = w_qkv.transpose(1, 0, 2).reshape(3 * block, hc)
    proj_got = first_swap(w_proj, "fsdp")
    toks = to_image(inputs)
    packed = pl.pallas_call(
        pack_kernel,
        out_shape=shape(block + PACK, hc, dtype=bf16),
        in_specs=[vm] * 9,
        out_specs=vm,
    )(w_out, ln1_gain, ln1_bias, ln2_gain, ln2_bias, out_bias, down_bias, qv_bias, up_bias.reshape(n_up, block))
    packed_got = first_swap(packed, "fsdp")
    proj_got, packed_got, w_up_later, cotangent, toks = tie(proj_got, packed_got, w_up, cotangent, toks)
    wq = gather([w_proj, proj_got], "fsdp")
    aux = gather([packed, packed_got], "fsdp")
    up_got = first_swap(w_up_later, "fsdp")
    cots = to_image(cotangent)

    masked, unit1, rate1, normed, q, k, v, mixed, branch_a, branch_b, up_shift, small = call(
        functools.partial(attend_kernel, nc, nf, nt, n_up),
        [
            wide(dtype=bf16),
            wide(),
            shape(rows, 128),
            wide(dtype=bf16),
            *[shape(rows, hc, dtype=bf16)] * 4,
            *[shape(rows // 2, width, dtype=bf16)] * 2,
            shape(1, ff),
            shape(nf, PACK, block, dtype=bf16),
        ],
        [idx, *toks, *wq, *aux],
        [pltpu.VMEM((nf, n, block), f32)],
    )
    branch_a, branch_b, cots = tie(branch_a, branch_b, cots)
    got_a, got_b = swap(branch_a, "tp", 1), swap(branch_b, "tp", 1)
    got_a, up_got, w_down_later = tie(got_a, up_got, w_down)
    wu = gather([w_up, up_got], "fsdp")
    down_got = first_swap(w_down_later, "fsdp")

    middle, unit2, rate2, normed2, gl, active, slope = call(
        functools.partial(up_kernel, nc, nf),
        [
            wide(),
            wide(),
            shape(rows, 128),
            wide(dtype=bf16),
            wide(dtype=bf16),
            shape(rows, ff, dtype=bf16),
            shape(rows, ff),
        ],
        [idx, masked, branch_a, branch_b, got_a, got_b, small, up_shift, *cots, *wu],
        [pltpu.VMEM((nf, n, block), f32)],
    )

    def shard_sum(parts, mats, cuts):
        rows_in = sum(PACK if kind == "small" else block for kind in parts)
        width_in = ff if parts == ("ffn",) else hc

        def run(first, last, got, cuts):
            have = [level[first:last] for level in got]
            counts = [len(level[0]) for level in have]
            out = call(
                functools.partial(shard_kernel, first, last, parts, block, counts, cuts),
                [shape(rows_in // cuts, width_in, dtype=bf16)] * ((last - first) * cuts),
                [idx, *mats, *leaves(have)],
            )
            return [out[i * cuts : (i + 1) * cuts] for i in range(last - first)]

        return ShardSum(run, cuts)

    levels = len(bits_of(nf))
    down_sum = shard_sum(("ffn",), (gl, active), 2)
    down_sum.step(0)
    down_got, down_sum.got = tie(down_got, down_sum.got)
    wd = gather([w_down, down_got], "fsdp")
    down_part = down_sum.begin(1)
    slope, down_part = tie(slope, down_part)
    down_sum.send(down_part, 1)
    gh, gnt, gh_sum = call(
        functools.partial(hidden_back_kernel, nf),
        [shape(rows, ff, dtype=bf16), wide(dtype=bf16), shape(1, ff)],
        [idx, gl, slope, *wd, *wu],
        [pltpu.VMEM((rows, width), f32)],
    )
    gnt_got = swap(gnt, "tp", 1)
    up_sum = shard_sum(("ffn",), (normed2, gh), 2)
    up_sum.step(0)
    (ffn,) = call(functools.partial(down_kernel, nf), [wide(dtype=bf16)], [idx, active, *wd])
    gnt_got, up_sum.got, down_sum.got, ffn = tie(gnt_got, up_sum.got, down_sum.got, ffn)
    up_sum.step(1)
    for level in range(2, levels):
        down_sum.step(level)
        up_sum.step(level)
    down = down_sum.own()
    down_in = [line_step(x, "ctx", 0) for x in down]
    ffn_got = swap(ffn, "tp", 1)

    gmid, gb, gq, gk, gv, sums, qv_sum = call(
        functools.partial(attend_back_kernel, nc, nf),
        [wide(), wide(dtype=bf16), *[shape(rows, hc, dtype=bf16)] * 3, shape(8, width), shape(8, hc)],
        [idx, gl, gnt, gnt_got, unit2, rate2, small, q, k, v, *aux],
        [pltpu.VMEM((rows, hc), bf16)],
    )
    gn, pack = call(
        functools.partial(normed_back_kernel, nf, nt, n_up),
        [wide(dtype=bf16), shape(nf, PACK, block, dtype=bf16)],
        [idx, gq, gk, gv, unit1, sums, qv_sum, gh_sum, *wq],
    )
    gn_got = swap(gn, "tp", 1)
    tails = [
        shard_sum(("k", "v", "small"), (normed, gk, normed, gv, pack), 1),
        shard_sum(("q", "out"), (normed, gq, mixed, gb), 1),
    ]
    for one in tails:
        one.step(0)
    finals = call(
        functools.partial(output_kernel, nc),
        [shape(n, width, dtype=bf16)] * nc,
        [idx, ffn, ffn_got, middle, small],
        [pltpu.VMEM((nf, n, block), f32)],
    )

    def exchanged(blocks):
        return [blocks[0]] + [swap(blocks[s], "ctx", s) for s in range(1, nc)]

    def assembled(blocks, dtype):
        (out,) = call(functools.partial(assemble_kernel, nc), [shape(nc, n, width, dtype=dtype)], [idx, *blocks])
        return out

    def added(x, got):
        return [line_add(idx, a, b) for a, b in zip(x, got)]

    finals = exchanged(finals)
    up_sum.got, down_in, finals, tails[0].got, tails[1].got = tie(up_sum.got, down_in, finals, tails[0].got, tails[1].got)
    result = assembled(finals, bf16)
    parts = [one.begin(1) for one in tails]
    up = up_sum.own()
    down = added(down, down_in)
    gn_got, parts, up, down = tie(gn_got, parts, up, down)
    for one, part in zip(tails, parts):
        one.send(part, 1)
        for level in range(2, levels):
            one.step(level)
    up_in = [line_step(x, "ctx", 0) for x in up]
    down_in = [line_step(x, "ctx", 1) for x in down]
    grads = call(
        functools.partial(input_back_kernel, nc),
        [shape(n, width, dtype=bf16)] * nc,
        [idx, gn, gn_got, unit1, rate1, gmid, small],
        [pltpu.VMEM((nf, n, block), f32)],
    )
    grads = exchanged(grads)
    grads, up_in, down_in, tails[0].got, tails[1].got = tie(grads, up_in, down_in, tails[0].got, tails[1].got)
    grad_inputs = assembled(grads, f32)
    down, up = added(down, down_in), added(up, up_in)
    down_in = [line_step(x, "ctx", 2) for x in down]
    up_in = [line_step(x, "ctx", 1) for x in up]
    held = [one.own()[0] for one in tails]
    held_in = [line_step(x, "ctx", 0) for x in held]
    up_in, down_in, held_in = tie(up_in, down_in, held_in)
    held, up = added(held, held_in), added(up, up_in)
    held_in = [line_step(x, "ctx", 1) for x in held]
    up_in = [line_step(x, "ctx", 2) for x in up]
    (grad_down,) = call(finish_down_kernel, [shape(ff, block)], [idx, *[x for pair in zip(down, down_in) for x in pair]])
    held_in, up_in = tie(held_in, up_in)
    held = added(held, held_in)
    held_in = [line_step(x, "ctx", 2) for x in held]
    (grad_up,) = call(finish_up_kernel, [shape(block, ff)], [idx, *[x for pair in zip(up, up_in) for x in pair]])
    (total,) = call(functools.partial(small_kernel, block), [shape(PACK, block, dtype=bf16)], [idx, held[0], held_in[0]])
    grad_qkv, grad_out = call(
        functools.partial(finish_kernel, block),
        [shape(3 * block, hc), shape(hc, block)],
        [idx, held[0], held_in[0], held[1], held_in[1]],
    )
    total = total.astype(f32) + swap(total, "tp", 1).astype(f32)
    return (
        result,
        grad_inputs,
        total[0],
        total[1],
        grad_qkv.reshape(3, block, hc).transpose(1, 0, 2),
        total[6:8],
        grad_out,
        total[4],
        total[2],
        total[3],
        grad_up,
        total[8 : 8 + n_up].reshape(-1),
        grad_down,
        total[5],
    )


def solution(mesh):
    in_specs = (
        P("fsdp", "ctx", None),
        P("fsdp"),
        P("fsdp"),
        P("fsdp"),
        P("fsdp", None, "tp"),
        P(None, "fsdp"),
        P("tp", "fsdp"),
        P("fsdp"),
        P("fsdp"),
        P("fsdp"),
        P("fsdp", "tp"),
        P("fsdp"),
        P("tp", "fsdp"),
        P("fsdp"),
        P("fsdp", "ctx", None),
    )
    out_specs = (
        P("fsdp", "ctx", None),
        P("fsdp", "ctx", None),
        P("fsdp"),
        P("fsdp"),
        P("fsdp", None, "tp"),
        P(None, "fsdp"),
        P("tp", "fsdp"),
        P("fsdp"),
        P("fsdp"),
        P("fsdp"),
        P("fsdp", "tp"),
        P("fsdp"),
        P("tp", "fsdp"),
        P("fsdp"),
    )
    return jax.shard_map(local, mesh=mesh, in_specs=in_specs, out_specs=out_specs, check_vma=False)
```

```python
import functools

import jax
import jax.numpy as jnp
from jax import lax
from jax.experimental import pallas as pl
from jax.experimental.pallas import tpu as pltpu
from jax.sharding import PartitionSpec as P

HD = 64
epsilon = 1e-06
f32 = jnp.float32
bf16 = jnp.bfloat16
PACK = 16
CHUNK = 512


def bits_of(n):
    out, bit = [], 1
    while bit < n:
        out.append(bit)
        bit *= 2
    return out


def bitrev(n):
    order = [0]
    for bit in reversed(bits_of(n)):
        order = order + [j | bit for j in order]
    return order


def place(x, n):
    bits = len(bits_of(n))
    out = 0
    for k in range(bits):
        out = out + ((x >> k) & 1) * (1 << (bits - 1 - k))
    return out


def swap(x, axis, bit):
    return lax.ppermute(x, axis, [(i, i ^ bit) for i in range(lax.axis_size(axis))])


def gather(pieces, axis):
    for bit in reversed(bits_of(lax.axis_size(axis) // len(pieces))):
        pieces = pieces + [swap(p, axis, bit) for p in pieces]
    return pieces


def first_swap(piece, axis):
    return swap(piece, axis, bits_of(lax.axis_size(axis))[-1])


class ShardSum:
    def __init__(self, run, whole, cuts, last_cuts):
        self.run, self.whole, self.cuts, self.last_cuts = run, whole, cuts, last_cuts
        self.n, self.got = lax.axis_size("fsdp"), []

    def begin(self, level):
        n = self.n >> level
        return self.run(n // 2, n, self.got, self.cuts if level == 0 else self.whole)

    def send(self, blocks, level):
        self.got.append([[swap(x, "fsdp", 1 << level) for x in pieces] for pieces in blocks])

    def step(self, level):
        self.send(self.begin(level), level)

    def own(self):
        return self.run(0, 1, self.got, self.last_cuts)[0]


def leaves(tree):
    return jax.tree.leaves(tree)


def tie(*trees):
    flat, where = jax.tree.flatten(trees)
    return jax.tree.unflatten(where, lax.optimization_barrier(flat))


def line_step(x, axis, number):
    assert lax.axis_size(axis) == 4
    pairs = ([(0, 1), (3, 2)], [(1, 2), (2, 1)], [(1, 0), (2, 3)])[number]
    return lax.ppermute(x, axis, pairs)


def line_add(idx, x, got, clock):
    (out,) = call(add_kernel, [jax.ShapeDtypeStruct(x.shape, bf16)], [idx, x, got], clock=clock)
    return out


NN = (((1,), (0,)), ((), ()))
NT = (((1,), (1,)), ((), ()))
TN = (((0,), (0,)), ((), ()))


def mm(a, b, dims=NN):
    return lax.dot_general(a, b, dims, preferred_element_type=f32)


def call(kernel, outs, args, scratch=(), mib=12, far=(), clock=None):
    vm = pl.BlockSpec(memory_space=pltpu.VMEM)
    near = len(args)
    last = [] if clock is None else clock[:]
    args = [*args, *far, *last]
    count = len(args) - len(last)

    def body(*refs):
        kernel(*refs[:count], *refs[count + len(last) :])

    results = pl.pallas_call(
        body,
        out_shape=outs,
        in_specs=[pl.BlockSpec(memory_space=pltpu.SMEM)]
        + [vm] * (near - 1)
        + [pl.BlockSpec(memory_space=pl.ANY)] * (len(far) + len(last)),
        out_specs=[vm] * len(outs),
        scratch_shapes=list(scratch),
        compiler_params=pltpu.CompilerParams(vmem_limit_bytes=mib << 20),
        cost_estimate=pl.CostEstimate(flops=0, bytes_accessed=0, transcendentals=0),
    )(*args)
    if clock is not None:
        clock[:] = [results[-1]]
    return results


def rows_of(small, r):
    return jnp.concatenate([small[p].astype(f32)[r : r + 1] for p in range(small.shape[0])], axis=1)


def live_rows(idx, s, n):
    return (idx[1] ^ s) * n + lax.broadcasted_iota(jnp.int32, (n, 1), 0) < idx[3]


def live_keys(idx, nc, n):
    col = lax.broadcasted_iota(jnp.int32, (1, nc * n), 1)
    slot = col
    for s in range(nc):
        slot = jnp.where((col >= s * n) & (col < (s + 1) * n), slot + ((idx[1] ^ s) - s) * n, slot)
    return slot < idx[3]


def to_relative(idx, x, box):
    nf, _, block = box.shape
    for b in range(nf):
        box[place(idx[0] ^ b, nf)] = x[:, b * block : (b + 1) * block]
    return jnp.concatenate([box[p] for p in range(nf)], axis=1)


def from_relative(idx, x, box):
    nf, _, block = box.shape
    for p in range(nf):
        box[p] = x[:, p * block : (p + 1) * block]
    return jnp.concatenate([box[place(idx[0] ^ b, nf)] for b in range(nf)], axis=1)


def mean(x):
    return jnp.mean(x, axis=-1, keepdims=True)


def normalize(x):
    center = x - mean(x)
    rate = lax.rsqrt(mean(center * center) + epsilon)
    return center * rate, rate


def norm_back(grad, gain, unit, rate):
    e = grad * gain
    return rate * (e - mean(e) - unit * mean(e * unit))


def softmax_of(q, k, keep, scale):
    scores = jnp.where(keep, mm(q, k, NT) * scale, -1e30)
    expo = jnp.exp(scores - jnp.max(scores, axis=-1, keepdims=True))
    return expo * (1.0 / jnp.sum(expo, axis=-1, keepdims=True))


def sides(n):
    lane = lax.broadcasted_iota(jnp.int32, (1, n), 1)
    return [(lane >= h * HD) & (lane < (h + 1) * HD) for h in range(n // HD)]


def only(keep, x):
    return jnp.where(keep, x.astype(f32), 0.0).astype(x.dtype)


def merge(keeps, parts):
    out = parts[0]
    for keep, part in zip(keeps[1:], parts[1:]):
        out = jnp.where(keep, part, out)
    return out


def fold(x, block, width):
    k = width // block
    rows = x.shape[0] // k
    return jnp.concatenate([x[i * rows : (i + 1) * rows] for i in range(k)], axis=1)


def unfold(x, block):
    return jnp.concatenate([x[:, i * block : (i + 1) * block] for i in range(x.shape[1] // block)], axis=0)


def pack_kernel(_, wo, *refs):
    *vectors, qv, up, out = refs
    block = qv.shape[1]
    out[:block] = fold(wo[...], block, out.shape[1])
    lines = [x[...].astype(f32).reshape(1, block) for x in vectors] + [qv[...].astype(f32), up[...].astype(f32)]
    lines.append(jnp.zeros((PACK - 8 - up.shape[0], block), f32))
    out[block:, :block] = jnp.concatenate(lines, axis=0).astype(bf16)
    out[block:, block:] = jnp.zeros((PACK, out.shape[1] - block), bf16)


def attend_kernel(nc, nf, nt, n_up, *refs):
    idx, refs = refs[0], refs[1:]
    sources = refs[: nc + 2 * nf]
    masked, unit1, rate1, normed, q, k, v, mixed, *branch, up_shift, small, box, tok_all, w_all, aux_all, sems = refs[
        nc + 2 * nf :
    ]
    toks = [tok_all.at[s] for s in range(nc)]
    wq, aux = [w_all.at[p] for p in range(nf)], [aux_all.at[p] for p in range(nf)]
    places = [*toks, *wq, *aux]
    order = [*range(nc), *range(nc + nf, nc + 2 * nf), *range(nc, nc + nf)]
    copies = {i: pltpu.make_async_copy(sources[i], places[i], sems.at[i]) for i in order}
    for i in order:
        copies[i].start()
    for i in order[: nc + nf]:
        copies[i].wait()
    n = toks[0].shape[0]
    block = small.shape[2]
    for p in range(nf):
        small[p] = aux[p][block:, :block]
    hc = q.shape[1]
    gain, shift = rows_of(small, 0), rows_of(small, 1)
    for s in range(nc):
        here = slice(s * n, (s + 1) * n)
        x = jnp.where(live_rows(idx, s, n), toks[s][...].astype(f32), 0.0)
        x = to_relative(idx, x, box)
        masked[here, :] = x.astype(bf16)
        unit, rate = normalize(x)
        unit1[here, :] = unit
        rate1[here, :] = jnp.broadcast_to(rate, (n, 128))
        normed[here, :] = (unit * gain + shift).astype(bf16)
    shifts = []
    for i in range(nf // nt):
        mine = small[place(idx[0] ^ (idx[2] * (nf // nt) + i), nf)].astype(f32)
        shifts.append((mine[6:7], mine[7:8]))
        for r in range(n_up):
            up_shift[:, (i * n_up + r) * block : (i * n_up + r + 1) * block] = mine[8 + r : 9 + r]
    q_shift = jnp.concatenate([a for a, _ in shifts], axis=1)
    v_shift = jnp.concatenate([b for _, b in shifts], axis=1)
    for i in order[nc + nf :]:
        copies[i].wait()
    for j, (out, bias) in enumerate(((q, q_shift), (k, None), (v, v_shift))):
        acc = mm(normed[:, :block], wq[0][j * block : (j + 1) * block])
        for p in range(1, nf):
            acc = acc + mm(normed[:, p * block : (p + 1) * block], wq[p][j * block : (j + 1) * block])
        out[...] = (acc if bias is None else acc + bias).astype(bf16)
    keep = live_keys(idx, nc, n)
    halves = sides(128)

    def pair(i, _):
        at = pl.ds(pl.multiple_of(i * 128, 128), 128)
        qp, kp, vp = q[:, at], k[:, at], v[:, at]
        parts = [mm(softmax_of(only(h, qp), kp, keep, HD**-0.5).astype(bf16), vp) for h in halves]
        mixed[:, at] = merge(halves, parts).astype(bf16)
        return 0

    lax.fori_loop(0, hc // 128, pair, 0)
    for p in range(nf):
        out_w = unfold(aux[p][:block], block)
        for h, out in enumerate(branch):
            part = mixed[h * out.shape[0] : (h + 1) * out.shape[0]]
            out[:, p * block : (p + 1) * block] = mm(part, out_w).astype(bf16)


def up_kernel(nc, nf, *refs):
    idx, masked, own_a, own_b, got_a, got_b, small, up_shift = refs[:8]
    wu = refs[8 : 8 + nf]
    middle, unit2, rate2, normed2, active, slope = refs[8 + nf :]
    n = masked.shape[0] // nc
    block = small.shape[2]
    gain, shift, bias = rows_of(small, 2), rows_of(small, 3), rows_of(small, 4)
    for s in range(nc):
        here = slice(s * n, (s + 1) * n)
        own, got = (own_a, got_a) if s < nc // 2 else (own_b, got_b)
        part = slice(s % (nc // 2) * n, (s % (nc // 2) + 1) * n)
        x = masked[here, :].astype(f32) + (own[part, :].astype(f32) + got[part, :].astype(f32) + bias)
        middle[here, :] = x
        unit, rate = normalize(x)
        unit2[here, :] = unit
        rate2[here, :] = jnp.broadcast_to(rate, (n, 128))
        normed2[here, :] = (unit * gain + shift).astype(bf16)
    chunk = min(CHUNK, active.shape[1])

    def step(i, _):
        at = pl.ds(pl.multiple_of(i * chunk, chunk), chunk)
        acc = mm(normed2[:, :block], wu[0][:, at])
        for p in range(1, nf):
            acc = acc + mm(normed2[:, p * block : (p + 1) * block], wu[p][:, at])
        x = acc + up_shift[:, at]
        root = 0.7978845608028654
        tanh = jnp.tanh(root * (x + 0.044715 * (x * x * x)))
        half = 0.5 * (1.0 + tanh)
        active[:, at] = (x * half).astype(bf16)
        slope[:, at] = half + 0.5 * x * (1.0 - tanh * tanh) * (root * (1.0 + 3 * 0.044715 * (x * x)))
        return 0

    lax.fori_loop(0, active.shape[1] // chunk, step, 0)


def cotangent_kernel(nc, idx, *refs):
    gl, box = refs[nc:]
    n = refs[0].shape[0]
    for s in range(nc):
        c = jnp.where(live_rows(idx, s, n), refs[s][...].astype(f32), 0.0)
        gl[s * n : (s + 1) * n, :] = to_relative(idx, c, box).astype(bf16)


def hidden_back_kernel(nf, *refs):
    _, gl, slope = refs[:3]
    wd, wu = refs[3 : 3 + nf], refs[3 + nf : 3 + 2 * nf]
    gh, gnt, gh_sum, acc = refs[3 + 2 * nf :]
    block = wd[0].shape[1]
    chunk = min(CHUNK, gh.shape[1])
    acc[...] = jnp.zeros_like(acc)

    def step(i, _):
        at = pl.ds(pl.multiple_of(i * chunk, chunk), chunk)
        ga = mm(gl[:, :block], wd[0][at, :], NT)
        for p in range(1, nf):
            ga = ga + mm(gl[:, p * block : (p + 1) * block], wd[p][at, :], NT)
        g = (ga * slope[:, at]).astype(bf16)
        gh[:, at] = g
        gh_sum[:, at] = jnp.sum(g.astype(f32), axis=0, keepdims=True)
        for p in range(nf):
            acc[:, p * block : (p + 1) * block] += mm(g, wu[p][:, at], NT)
        return 0

    lax.fori_loop(0, gh.shape[1] // chunk, step, 0)
    gnt[...] = acc[...].astype(bf16)


def down_kernel(nf, idx, active, *refs):
    out = refs[nf]
    block = refs[0].shape[1]
    for p in range(nf):
        out[:, p * block : (p + 1) * block] = mm(active[...], refs[p][...]).astype(bf16)


def attend_back_kernel(nc, nf, *refs):
    idx, gl, own, got, unit2, rate2, small, q, k, v = refs[:10]
    aux = refs[10 : 10 + nf]
    gmid, gb, gq, gk, gv, sums, qv_sum, gm = refs[10 + nf :]
    n = gl.shape[0] // nc
    block = small.shape[2]
    hc = q.shape[1]
    gain = rows_of(small, 2)
    totals = [0.0] * 4
    for s in range(nc):
        here = slice(s * n, (s + 1) * n)
        g = own[here, :].astype(f32) + got[here, :].astype(f32)
        u = unit2[here, :]
        c = gl[here, :].astype(f32)
        x = c + norm_back(g, gain, u, rate2[here, :1])
        gmid[here, :] = x
        low = x.astype(bf16)
        gb[here, :] = low
        for r, value in enumerate((g * u, g, low.astype(f32), c)):
            totals[r] = totals[r] + jnp.sum(value, axis=0, keepdims=True)
    sums[...] = jnp.concatenate(totals + [jnp.zeros((4, gl.shape[1]), f32)], axis=0)
    acc = mm(gb[:, :block], unfold(aux[0][:block], block), NT)
    for p in range(1, nf):
        acc = acc + mm(gb[:, p * block : (p + 1) * block], unfold(aux[p][:block], block), NT)
    gm[...] = acc.astype(bf16)
    keep = live_keys(idx, nc, n)
    halves = sides(128)
    scale = HD**-0.5

    def pair(i, _):
        at = pl.ds(pl.multiple_of(i * 128, 128), 128)
        qp, kp, vp, gp = q[:, at], k[:, at], v[:, at], gm[:, at]
        dq, dk, dv = [], [], []
        for h in halves:
            prob = softmax_of(only(h, qp), kp, keep, scale)
            grad = mm(only(h, gp), vp, NT)
            dv.append(mm(prob.astype(bf16), gp, TN))
            ds = (prob * (grad - jnp.sum(prob * grad, axis=-1, keepdims=True))).astype(bf16)
            dq.append(mm(ds, kp))
            dk.append(mm(ds, qp, TN))
        a = (merge(halves, dq) * scale).astype(bf16)
        b = merge(halves, dv).astype(bf16)
        gq[:, at] = a
        gk[:, at] = (merge(halves, dk) * scale).astype(bf16)
        gv[:, at] = b
        total = [jnp.sum(x.astype(f32), axis=0, keepdims=True) for x in (a, b)]
        qv_sum[:, at] = jnp.concatenate(total + [jnp.zeros((6, 128), f32)], axis=0)
        return 0

    lax.fori_loop(0, hc // 128, pair, 0)


def normed_back_kernel(nf, nt, n_up, idx, gq, gk, gv, unit1, sums, qv_sum, gh_sum, ffn, *refs):
    wq, (gn, cross, pack) = refs[:nf], refs[nf:]
    block = pack.shape[2]
    order = bitrev(nf)
    first = jnp.where(idx[2] == 0, 1.0, 0.0)
    held = nf // nt
    for p in range(nf):
        here = slice(p * block, (p + 1) * block)
        acc = mm(gq[...], wq[p][:block], NT) + mm(gk[...], wq[p][block : 2 * block], NT)
        acc = acc + mm(gv[...], wq[p][2 * block : 3 * block], NT)
        gn[:, here] = acc.astype(bf16)
        cross[:, here] = jnp.where(idx[2] == 0, acc, ffn[:, here].astype(f32)).astype(bf16)
        rows = [jnp.sum(acc * unit1[:, here], axis=0, keepdims=True), jnp.sum(acc, axis=0, keepdims=True)]
        rows += [sums[r : r + 1, here] * first for r in range(4)]
        which = (idx[0] ^ order[p]) - idx[2] * held

        def mine(of):
            out = jnp.zeros((1, block), f32)
            for i in range(held):
                out = jnp.where(which == i, of(i), out)
            return out

        rows += [mine(lambda i, r=r: qv_sum[r : r + 1, i * block : (i + 1) * block]) for r in range(2)]
        rows += [
            mine(lambda i, r=r: gh_sum[:, (i * n_up + r) * block : (i * n_up + r + 1) * block]) for r in range(n_up)
        ]
        rows.append(jnp.zeros((PACK - len(rows), block), f32))
        pack[p] = jnp.concatenate(rows, axis=0).astype(bf16)


def outputs_kernel(nc, idx, ffn, cross_got, middle, gn, unit1, rate1, gmid, small, stay, pass_on, go, box):
    n = gmid.shape[0] // nc
    outs = [stay, go.at[0], pass_on, go.at[1]]

    @pl.when(idx[2] == 0)
    def _():
        bias = rows_of(small, 5)
        for s in range(nc):
            here = slice(s * n, (s + 1) * n)
            x = middle[here, :] + (ffn[here, :].astype(f32) + cross_got[here, :].astype(f32) + bias)
            outs[s][...] = from_relative(idx, jnp.where(live_rows(idx, s, n), x, 0.0), box).astype(bf16)

    @pl.when(idx[2] != 0)
    def _():
        gain = rows_of(small, 0)
        for s in range(nc):
            here = slice(s * n, (s + 1) * n)
            g = gn[here, :].astype(f32) + cross_got[here, :].astype(f32)
            x = gmid[here, :] + norm_back(g, gain, unit1[here, :], rate1[here, :1])
            outs[s][...] = from_relative(idx, jnp.where(live_rows(idx, s, n), x, 0.0), box).astype(bf16)


def relay_kernel(_, own, got, out):
    out[0] = own[...]
    out[1] = got[1]


def assemble_kernel(idx, own, near, far, out):
    out[idx[1]] = own[...]
    out[idx[1] ^ 1] = near[0]
    out[idx[1] ^ 2] = far[0]
    out[idx[1] ^ 3] = far[1]


def split_kernel(idx, own, got, result, grad):
    @pl.when(idx[2] == 0)
    def _():
        result[...] = own[...]
        grad[...] = got[...].astype(f32)

    @pl.when(idx[2] != 0)
    def _():
        result[...] = got[...]
        grad[...] = own[...].astype(f32)


def piece_at(pieces, at):
    for piece in pieces:
        if at < piece.shape[0]:
            return piece, at
        at -= piece.shape[0]


def shard_kernel(first, last, parts, block, step, counts, cuts, *refs):
    refs = list(refs[1:])
    mats = [refs.pop(0) for kind in parts for _ in range(1 if kind == "small" else 2)]
    gots = [[[refs.pop(0) for _ in range(count)] for _ in range(first, last)] for count in counts]
    outs = [[refs.pop(0) for _ in range(cuts)] for _ in range(first, last)]
    wide = outs[0][0].shape[1]
    for p in range(last - first):
        at, taken = 0, 0
        for kind in parts:
            here = slice((first + p) * block, (first + p + 1) * block)
            rows = PACK if kind == "small" else block
            size = step if kind == "ffn" else rows
            for low in range(0, rows, size):
                if kind == "small":
                    x = mats[taken][first + p].astype(f32)
                    x = jnp.concatenate([x, jnp.zeros((rows, wide - block), f32)], axis=1)
                elif kind == "out":
                    x = fold(mm(mats[taken][...], mats[taken + 1][:, here], TN), block, wide)
                else:
                    left = slice(here.start + low, here.start + low + size)
                    x = mm(mats[taken][:, left], mats[taken + 1][...], TN)
                for got in gots:
                    piece, i = piece_at(got[p], at)
                    x = x + piece[i : i + size].astype(f32)
                piece, i = piece_at(outs[p], at)
                piece[i : i + size] = x.astype(bf16)
                at += size
            taken += 1 if kind == "small" else 2


def add_kernel(_, x, got, out):
    out[...] = (x[...].astype(f32) + got[...].astype(f32)).astype(bf16)


def picked(idx, own, got):
    return jnp.where(idx[4] == 1, got.astype(f32), own.astype(f32))


def finish_up_kernel(idx, *refs):
    out = refs[-1]
    rows = refs[0].shape[0]
    for i in range(len(refs) // 2):
        out[i * rows : (i + 1) * rows] = picked(idx, refs[2 * i][...], refs[2 * i + 1][...])


def finish_down_kernel(idx, *refs):
    out = refs[-1]
    rows = refs[0].shape[0]
    step = min(out.shape[0], 512)
    for i in range(len(refs) // 2):
        for j in range(0, out.shape[0], step):
            x = picked(idx, refs[2 * i][:, j : j + step], refs[2 * i + 1][:, j : j + step])
            out[j : j + step, i * rows : (i + 1) * rows] = x.T


def small_kernel(block, idx, own, got, out):
    out[...] = picked(idx, own[2 * block :, :block], got[2 * block :, :block]).astype(bf16)


def finish_kernel(block, idx, a, a_got, b, b_got, qkv, out_w):
    kv = picked(idx, a[: 2 * block], a_got[: 2 * block])
    qo = picked(idx, b[...], b_got[...])
    qkv[:block] = qo[:block]
    qkv[block:] = kv
    out_w[...] = unfold(qo[block:], block)


def shape(*dims, dtype=f32):
    return jax.ShapeDtypeStruct(dims, dtype)


def local(
    inputs,
    lengths,
    ln1_gain,
    ln1_bias,
    w_qkv,
    qv_bias,
    w_out,
    out_bias,
    ln2_gain,
    ln2_bias,
    w_up,
    up_bias,
    w_down,
    down_bias,
    cotangent,
):
    nf, nc, nt = (lax.axis_size(a) for a in ("fsdp", "ctx", "tp"))
    f, c, t = (lax.axis_index(a) for a in ("fsdp", "ctx", "tp"))
    images, n, width = inputs.shape
    assert images == nc
    rows = n * nc
    block = width // nf
    hc = w_qkv.shape[2]
    ff = w_up.shape[1]
    n_up = up_bias.shape[0] // block
    outer = (c == 0) | (c == nc - 1)
    idx = jnp.stack([f, c, t, lax.dynamic_index_in_dim(lengths, c, 0, False), outer.astype(jnp.int32)]).astype(jnp.int32)
    wide = functools.partial(shape, rows, width)

    def to_image(x):
        return [lax.dynamic_index_in_dim(x, c, 0, False)] + [
            swap(lax.dynamic_index_in_dim(x, c ^ s, 0, False), "ctx", s) for s in range(1, nc)
        ]

    clock = []

    w_proj = w_qkv.transpose(1, 0, 2).reshape(3 * block, hc)
    proj_got = first_swap(w_proj, "fsdp")
    toks = to_image(inputs)
    (packed,) = call(
        pack_kernel,
        [shape(block + PACK, hc, dtype=bf16)],
        [idx, w_out, ln1_gain, ln1_bias, ln2_gain, ln2_bias, out_bias, down_bias, qv_bias, up_bias.reshape(n_up, block)],
    )
    packed_got = first_swap(packed, "fsdp")
    proj_got, packed_got, w_up_later, toks = tie(proj_got, packed_got, w_up, toks)
    wq = gather([w_proj, proj_got], "fsdp")
    aux = gather([packed, packed_got], "fsdp")
    up_got = first_swap(w_up_later, "fsdp")
    masked, unit1, rate1, normed, q, k, v, mixed, branch_a, branch_b, up_shift, small = call(
        functools.partial(attend_kernel, nc, nf, nt, n_up),
        [
            wide(dtype=bf16),
            wide(),
            shape(rows, 128),
            wide(dtype=bf16),
            *[shape(rows, hc, dtype=bf16)] * 4,
            *[shape(rows // 2, width, dtype=bf16)] * 2,
            shape(1, ff),
            shape(nf, PACK, block, dtype=bf16),
        ],
        [idx],
        [
            pltpu.VMEM((nf, n, block), f32),
            pltpu.VMEM((nc, n, width), bf16),
            pltpu.VMEM((nf, 3 * block, hc), bf16),
            pltpu.VMEM((nf, block + PACK, hc), bf16),
            pltpu.SemaphoreType.DMA((nc + 2 * nf,)),
        ],
        mib=24,
        far=[*toks, *wq, *aux],
        clock=clock,
    )
    got_a, got_b = swap(branch_a, "tp", 1), swap(branch_b, "tp", 1)
    got_a, up_got, w_down_later, cotangent = tie(got_a, up_got, w_down, cotangent)
    cots = to_image(cotangent)
    wu = gather([w_up, up_got], "fsdp")
    down_got = first_swap(w_down_later, "fsdp")

    middle, unit2, rate2, normed2, active, slope = call(
        functools.partial(up_kernel, nc, nf),
        [
            wide(),
            wide(),
            shape(rows, 128),
            wide(dtype=bf16),
            shape(rows, ff, dtype=bf16),
            shape(rows, ff),
        ],
        [idx, masked, branch_a, branch_b, got_a, got_b, small, up_shift, *wu],
        clock=clock,
    )
    (gl,) = call(
        functools.partial(cotangent_kernel, nc),
        [wide(dtype=bf16)],
        [idx, *cots],
        [pltpu.VMEM((nf, n, block), f32)],
        clock=clock,
    )

    def shard_sum(parts, mats, cuts, last_cuts):
        total = sum(PACK if kind == "small" else block for kind in parts)
        width_in = ff if parts == ("ffn",) else hc

        def run(first, last, got, cuts):
            have = [level[first:last] for level in got]
            counts = [len(level[0]) for level in have]
            out = call(
                functools.partial(shard_kernel, first, last, parts, block, block // 2, counts, len(cuts)),
                [shape(rows_in, width_in, dtype=bf16) for rows_in in cuts] * (last - first),
                [idx, *mats, *leaves(have)],
                clock=clock,
            )
            return [out[i * len(cuts) : (i + 1) * len(cuts)] for i in range(last - first)]

        return ShardSum(run, [total], cuts, last_cuts)

    levels = len(bits_of(nf))
    down_sum = shard_sum(("ffn",), (gl, active), [block // 2] * 2, [block])
    down_sum.step(0)
    down_got, down_sum.got = tie(down_got, down_sum.got)
    wd = gather([w_down, down_got], "fsdp")
    down_part = down_sum.begin(1)
    slope, down_part = tie(slope, down_part)
    down_sum.send(down_part, 1)
    gh, gnt, gh_sum = call(
        functools.partial(hidden_back_kernel, nf),
        [shape(rows, ff, dtype=bf16), wide(dtype=bf16), shape(1, ff)],
        [idx, gl, slope, *wd, *wu],
        [pltpu.VMEM((rows, width), f32)],
        clock=clock,
    )
    gnt_got = swap(gnt, "tp", 1)
    up_sum = shard_sum(("ffn",), (normed2, gh), [block // 2] * 2, [block])
    up_sum.step(0)
    (ffn,) = call(functools.partial(down_kernel, nf), [wide(dtype=bf16)], [idx, active, *wd], clock=clock)
    gnt_got, up_sum.got, down_sum.got = tie(gnt_got, up_sum.got, down_sum.got)
    for level in range(1, levels):
        up_sum.step(level)
    for level in range(2, levels):
        down_sum.step(level)
    (down,) = down_sum.own()
    down_in = line_step(down, "ctx", 0)
    gmid, gb, gq, gk, gv, sums, qv_sum = call(
        functools.partial(attend_back_kernel, nc, nf),
        [wide(), wide(dtype=bf16), *[shape(rows, hc, dtype=bf16)] * 3, shape(8, width), shape(8, hc)],
        [idx, gl, gnt, gnt_got, unit2, rate2, small, q, k, v, *aux],
        [pltpu.VMEM((rows, hc), bf16)],
        clock=clock,
    )
    gn, cross, pack = call(
        functools.partial(normed_back_kernel, nf, nt, n_up),
        [wide(dtype=bf16), wide(dtype=bf16), shape(nf, PACK, block, dtype=bf16)],
        [idx, gq, gk, gv, unit1, sums, qv_sum, gh_sum, ffn, *wq],
        clock=clock,
    )
    cross_got = swap(cross, "tp", 1)
    kv_rows, qo_rows = 2 * block + PACK, 2 * block
    packed_sum = shard_sum(
        ("k", "v", "small", "q", "out"),
        (normed, gk, normed, gv, pack, normed, gq, mixed, gb),
        [kv_rows + qo_rows],
        [kv_rows, qo_rows],
    )
    packed_sum.step(0)

    def passed(x, got, number):
        x = line_add(idx, x, got, clock)
        return x, line_step(x, "ctx", number)

    (up,) = up_sum.own()
    up_in = line_step(up, "ctx", 0)
    down, down_in = passed(down, down_in, 1)
    token, _ = tie(rate2, down)
    clock[:] = [swap(token, "fsdp", 1)]
    for level in range(1, levels):
        packed_sum.step(level)
    assert nt == 2 and nc == 4
    stay, pass_on, go = call(
        functools.partial(outputs_kernel, nc),
        [shape(n, width, dtype=bf16), shape(n, width, dtype=bf16), shape(2, n, width, dtype=bf16)],
        [idx, ffn, cross_got, middle, gn, unit1, rate1, gmid, small],
        [pltpu.VMEM((nf, n, block), f32)],
        clock=clock,
    )
    near = swap(go, "ctx", 1)
    down, down_in = passed(down, down_in, 2)
    up, up_in = passed(up, up_in, 1)
    kv, qo = packed_sum.own()
    kv_in, qo_in = line_step(kv, "ctx", 0), line_step(qo, "ctx", 0)
    (relayed,) = call(relay_kernel, [shape(2, n, width, dtype=bf16)], [idx, pass_on, near], clock=clock)
    far = swap(relayed, "ctx", 2)
    kv, kv_in = passed(kv, kv_in, 1)
    (grad_down,) = call(finish_down_kernel, [shape(ff, block)], [idx, down, down_in], clock=clock)
    up, up_in = passed(up, up_in, 2)
    qo, qo_in = passed(qo, qo_in, 1)
    kv, kv_in = passed(kv, kv_in, 2)
    (ours,) = call(assemble_kernel, [shape(nc, n, width, dtype=bf16)], [idx, stay, near, far], clock=clock)
    theirs = swap(ours, "tp", 1)
    (grad_up,) = call(finish_up_kernel, [shape(block, ff)], [idx, up, up_in], clock=clock)
    qo, qo_in = passed(qo, qo_in, 2)
    (total,) = call(
        functools.partial(small_kernel, block), [shape(PACK, block, dtype=bf16)], [idx, kv, kv_in], clock=clock
    )
    total = total.astype(f32) + swap(total, "tp", 1).astype(f32)
    result, grad_inputs = call(
        split_kernel, [shape(nc, n, width, dtype=bf16), shape(nc, n, width)], [idx, ours, theirs], clock=clock
    )
    grad_qkv, grad_out = call(
        functools.partial(finish_kernel, block),
        [shape(3 * block, hc), shape(hc, block)],
        [idx, kv, kv_in, qo, qo_in],
        clock=clock,
    )
    return (
        result,
        grad_inputs,
        total[0],
        total[1],
        grad_qkv.reshape(3, block, hc).transpose(1, 0, 2),
        total[6:8],
        grad_out,
        total[4],
        total[2],
        total[3],
        grad_up,
        total[8 : 8 + n_up].reshape(-1),
        grad_down,
        total[5],
    )


def solution(mesh):
    in_specs = (
        P("fsdp", "ctx", None),
        P("fsdp"),
        P("fsdp"),
        P("fsdp"),
        P("fsdp", None, "tp"),
        P(None, "fsdp"),
        P("tp", "fsdp"),
        P("fsdp"),
        P("fsdp"),
        P("fsdp"),
        P("fsdp", "tp"),
        P("fsdp"),
        P("tp", "fsdp"),
        P("fsdp"),
        P("fsdp", "ctx", None),
    )
    out_specs = (
        P("fsdp", "ctx", None),
        P("fsdp", "ctx", None),
        P("fsdp"),
        P("fsdp"),
        P("fsdp", None, "tp"),
        P(None, "fsdp"),
        P("tp", "fsdp"),
        P("fsdp"),
        P("fsdp"),
        P("fsdp"),
        P("fsdp", "tp"),
        P("fsdp"),
        P("tp", "fsdp"),
        P("fsdp"),
    )
    return jax.shard_map(local, mesh=mesh, in_specs=in_specs, out_specs=out_specs, check_vma=False)
```

```python
import functools
import types

import jax
import jax.numpy as jnp
from jax import lax
from jax.experimental import pallas as pl
from jax.experimental.pallas import tpu as pltpu
from jax.sharding import PartitionSpec as P

HD = 64
epsilon = 1e-06
f32 = jnp.float32
bf16 = jnp.bfloat16
PACK = 16
CHUNK = 512
LATE = "late"
ORDER = (
    "u0", "da2", "ffn", "ub1", "ua1", "db2", "back", "da", "ub2", "normed", "t0", "db", "ua2", "kv1", "ub", "outputs",
    "ua", "da", "kv2", "db", "qo1", "relay", "ua", "kv", "grad_down", "ub", "qo2", "assemble", "qo", "kv", "split",
    "qo", "small", "grad_up", "finish",
)


def bits_of(n):
    out, bit = [], 1
    while bit < n:
        out.append(bit)
        bit *= 2
    return out


def bitrev(n):
    order = [0]
    for bit in reversed(bits_of(n)):
        order = order + [j | bit for j in order]
    return order


def place(x, n):
    bits = len(bits_of(n))
    out = 0
    for k in range(bits):
        out = out + ((x >> k) & 1) * (1 << (bits - 1 - k))
    return out


def swap(x, axis, bit):
    return lax.ppermute(x, axis, [(i, i ^ bit) for i in range(lax.axis_size(axis))])


def gather(pieces, axis):
    for bit in reversed(bits_of(lax.axis_size(axis) // len(pieces))):
        pieces = pieces + [swap(p, axis, bit) for p in pieces]
    return pieces


def first_swap(piece, axis):
    return swap(piece, axis, bits_of(lax.axis_size(axis))[-1])


class ShardSum:
    def __init__(self, run):
        self.run, self.n, self.first, self.got = run, lax.axis_size("fsdp"), None, [[], []]

    def start(self):
        (x,) = self.run(self.n // 2, self.n, None, [], 0, None)
        self.first = swap(x, "fsdp", 1)

    def start_by_pieces(self):
        for piece in range(2):
            self.send(self.begin(piece), piece)

    def level(self, piece):
        return len(self.got[piece]) + (self.first is not None)

    def begin(self, piece):
        level = self.level(piece)
        n = self.n >> level
        return self.run(n // 2, n, self.first, self.got[piece], level, piece)

    def send(self, blocks, piece):
        level = self.level(piece)
        self.got[piece].append([swap(x, "fsdp", 1 << level) for x in blocks])

    def own(self, piece):
        return self.run(0, 1, self.first, self.got[piece], self.level(piece), piece)[0]


def tie(*trees):
    flat, where = jax.tree.flatten(trees)
    return jax.tree.unflatten(where, lax.optimization_barrier(flat))


class Line:
    def __init__(self, x, idx, clock):
        assert lax.axis_size("ctx") == 4
        self.held, self.idx, self.clock, self.step = x, idx, clock, 0
        self.got = self.send()

    def send(self):
        pairs = ([(0, 1), (3, 2)], [(1, 2), (2, 1)], [(1, 0), (2, 3)])[self.step]
        return lax.ppermute(self.held, "ctx", pairs)

    def advance(self, name):
        self.step += 1
        out = [jax.ShapeDtypeStruct(self.held.shape, bf16)]
        args, name = [self.idx, self.held, self.got], f"{name}_{self.step}"
        (self.held,) = call(add_kernel, out, args, clock=self.clock, name=name)
        self.got = self.send()

    def ends(self):
        return [self.held, self.got]


NN = (((1,), (0,)), ((), ()))
NT = (((1,), (1,)), ((), ()))
TN = (((0,), (0,)), ((), ()))


def mm(a, b, dims=NN):
    return lax.dot_general(a, b, dims, preferred_element_type=f32)


def call(kernel, outs, args, scratch=(), mib=12, far=(), clock=None, name=None):
    vm = pl.BlockSpec(memory_space=pltpu.VMEM)
    near = len(args)
    last = [] if clock is None else [x for x in clock if x is not LATE]
    late = clock is not None and any(x is LATE for x in clock)
    args = [*args, *far, *last]
    count = len(args) - len(last)

    def body(*refs):
        kernel(*refs[:count], *refs[count + len(last) :])

    results = pl.pallas_call(
        body,
        out_shape=outs,
        in_specs=[pl.BlockSpec(memory_space=pltpu.SMEM)]
        + [vm] * (near - 1)
        + [pl.BlockSpec(memory_space=pl.ANY)] * (len(far) + len(last)),
        out_specs=[vm] * len(outs),
        scratch_shapes=list(scratch),
        compiler_params=pltpu.CompilerParams(vmem_limit_bytes=mib << 20),
        cost_estimate=pl.CostEstimate(flops=int(3e10) if late else 0, bytes_accessed=0, transcendentals=0),
        name=name,
    )(*args)
    if clock is not None:
        clock[:] = [results[-1], LATE] if late else [results[-1]]
    return results


def rows_of(small, r):
    return jnp.concatenate([small[p].astype(f32)[r : r + 1] for p in range(small.shape[0])], axis=1)


def live_rows(idx, s, n):
    return (idx[1] ^ s) * n + lax.broadcasted_iota(jnp.int32, (n, 1), 0) < idx[3]


def live_keys(idx, nc, n):
    col = lax.broadcasted_iota(jnp.int32, (1, nc * n), 1)
    slot = col
    for s in range(nc):
        slot = jnp.where((col >= s * n) & (col < (s + 1) * n), slot + ((idx[1] ^ s) - s) * n, slot)
    return slot < idx[3]


def to_relative(idx, x, box):
    nf, _, block = box.shape
    for b in range(nf):
        box[place(idx[0] ^ b, nf)] = x[:, b * block : (b + 1) * block]
    return jnp.concatenate([box[p] for p in range(nf)], axis=1)


def from_relative(idx, x, box):
    nf, _, block = box.shape
    for p in range(nf):
        box[p] = x[:, p * block : (p + 1) * block]
    return jnp.concatenate([box[place(idx[0] ^ b, nf)] for b in range(nf)], axis=1)


def mean(x):
    return jnp.mean(x, axis=-1, keepdims=True)


def normalize(x):
    center = x - mean(x)
    rate = lax.rsqrt(mean(center * center) + epsilon)
    return center * rate, rate


def norm_back(grad, gain, unit, rate):
    e = grad * gain
    return rate * (e - mean(e) - unit * mean(e * unit))


def softmax_of(q, k, keep, scale):
    scores = jnp.where(keep, mm(q, k, NT) * scale, -1e30)
    expo = jnp.exp(scores - jnp.max(scores, axis=-1, keepdims=True))
    return expo * (1.0 / jnp.sum(expo, axis=-1, keepdims=True))


def sides(n):
    lane = lax.broadcasted_iota(jnp.int32, (1, n), 1)
    return [(lane >= h * HD) & (lane < (h + 1) * HD) for h in range(n // HD)]


def only(keep, x):
    return jnp.where(keep, x.astype(f32), 0.0).astype(x.dtype)


def merge(keeps, parts):
    out = parts[0]
    for keep, part in zip(keeps[1:], parts[1:]):
        out = jnp.where(keep, part, out)
    return out


def fold(x, block, width):
    k = width // block
    rows = x.shape[0] // k
    return jnp.concatenate([x[i * rows : (i + 1) * rows] for i in range(k)], axis=1)


def unfold(x, block):
    return jnp.concatenate([x[:, i * block : (i + 1) * block] for i in range(x.shape[1] // block)], axis=0)


def pack_kernel(_, wo, *refs):
    *vectors, qv, up, out = refs
    block = qv.shape[1]
    out[:block] = fold(wo[...], block, out.shape[1])
    lines = [x[...].astype(f32).reshape(1, block) for x in vectors] + [qv[...].astype(f32), up[...].astype(f32)]
    lines.append(jnp.zeros((PACK - 8 - up.shape[0], block), f32))
    out[block:, :block] = jnp.concatenate(lines, axis=0).astype(bf16)
    out[block:, block:] = jnp.zeros((PACK, out.shape[1] - block), bf16)


def attend_kernel(nc, nf, nt, n_up, *refs):
    idx, refs = refs[0], refs[1:]
    sources = refs[: nc + 2 * nf]
    masked, unit1, rate1, normed, q, k, v, mixed, *branch, up_shift, small, box, tok_all, w_all, aux_all, sems = refs[
        nc + 2 * nf :
    ]
    toks = [tok_all.at[s] for s in range(nc)]
    wq, aux = [w_all.at[p] for p in range(nf)], [aux_all.at[p] for p in range(nf)]
    places = [*toks, *wq, *aux]
    order = [*range(nc), *range(nc + nf, nc + 2 * nf), *range(nc, nc + nf)]
    copies = {i: pltpu.make_async_copy(sources[i], places[i], sems.at[i]) for i in order}
    for i in order:
        copies[i].start()
    for i in order[: nc + nf]:
        copies[i].wait()
    n = toks[0].shape[0]
    block = small.shape[2]
    for p in range(nf):
        small[p] = aux[p][block:, :block]
    hc = q.shape[1]
    gain, shift = rows_of(small, 0), rows_of(small, 1)
    for s in range(nc):
        here = slice(s * n, (s + 1) * n)
        x = jnp.where(live_rows(idx, s, n), toks[s][...].astype(f32), 0.0)
        x = to_relative(idx, x, box)
        masked[here, :] = x.astype(bf16)
        unit, rate = normalize(x)
        unit1[here, :] = unit
        rate1[here, :] = jnp.broadcast_to(rate, (n, 128))
        normed[here, :] = (unit * gain + shift).astype(bf16)
    shifts = []
    for i in range(nf // nt):
        mine = small[place(idx[0] ^ (idx[2] * (nf // nt) + i), nf)].astype(f32)
        shifts.append((mine[6:7], mine[7:8]))
        for r in range(n_up):
            up_shift[:, (i * n_up + r) * block : (i * n_up + r + 1) * block] = mine[8 + r : 9 + r]
    q_shift = jnp.concatenate([a for a, _ in shifts], axis=1)
    v_shift = jnp.concatenate([b for _, b in shifts], axis=1)
    for i in order[nc + nf :]:
        copies[i].wait()
    for j, (out, bias) in enumerate(((q, q_shift), (k, None), (v, v_shift))):
        acc = mm(normed[:, :block], wq[0][j * block : (j + 1) * block])
        for p in range(1, nf):
            acc = acc + mm(normed[:, p * block : (p + 1) * block], wq[p][j * block : (j + 1) * block])
        out[...] = (acc if bias is None else acc + bias).astype(bf16)
    keep = live_keys(idx, nc, n)
    halves = sides(128)

    def pair(i, _):
        at = pl.ds(pl.multiple_of(i * 128, 128), 128)
        qp, kp, vp = q[:, at], k[:, at], v[:, at]
        parts = [mm(softmax_of(only(h, qp), kp, keep, HD**-0.5).astype(bf16), vp) for h in halves]
        mixed[:, at] = merge(halves, parts).astype(bf16)
        return 0

    lax.fori_loop(0, hc // 128, pair, 0)
    for p in range(nf):
        out_w = unfold(aux[p][:block], block)
        for h, out in enumerate(branch):
            part = mixed[h * out.shape[0] : (h + 1) * out.shape[0]]
            out[:, p * block : (p + 1) * block] = mm(part, out_w).astype(bf16)


def up_kernel(nc, nf, *refs):
    idx, masked, own_a, own_b, got_a, got_b, small, up_shift = refs[:8]
    wu = refs[8 : 8 + nf]
    middle, unit2, rate2, normed2, active, slope = refs[8 + nf :]
    n = masked.shape[0] // nc
    block = small.shape[2]
    gain, shift, bias = rows_of(small, 2), rows_of(small, 3), rows_of(small, 4)
    for s in range(nc):
        here = slice(s * n, (s + 1) * n)
        own, got = (own_a, got_a) if s < nc // 2 else (own_b, got_b)
        part = slice(s % (nc // 2) * n, (s % (nc // 2) + 1) * n)
        x = masked[here, :].astype(f32) + (own[part, :].astype(f32) + got[part, :].astype(f32) + bias)
        middle[here, :] = x
        unit, rate = normalize(x)
        unit2[here, :] = unit
        rate2[here, :] = jnp.broadcast_to(rate, (n, 128))
        normed2[here, :] = (unit * gain + shift).astype(bf16)
    chunk = min(CHUNK, active.shape[1])

    def step(i, _):
        at = pl.ds(pl.multiple_of(i * chunk, chunk), chunk)
        acc = mm(normed2[:, :block], wu[0][:, at])
        for p in range(1, nf):
            acc = acc + mm(normed2[:, p * block : (p + 1) * block], wu[p][:, at])
        x = acc + up_shift[:, at]
        root = 0.7978845608028654
        tanh = jnp.tanh(root * (x + 0.044715 * (x * x * x)))
        half = 0.5 * (1.0 + tanh)
        active[:, at] = (x * half).astype(bf16)
        slope[:, at] = half + 0.5 * x * (1.0 - tanh * tanh) * (root * (1.0 + 3 * 0.044715 * (x * x)))
        return 0

    lax.fori_loop(0, active.shape[1] // chunk, step, 0)


def cotangent_kernel(nc, idx, *refs):
    gl, box = refs[nc:]
    n = refs[0].shape[0]
    for s in range(nc):
        c = jnp.where(live_rows(idx, s, n), refs[s][...].astype(f32), 0.0)
        gl[s * n : (s + 1) * n, :] = to_relative(idx, c, box).astype(bf16)


def hidden_back_kernel(nf, *refs):
    _, gl, slope = refs[:3]
    wd, wu = refs[3 : 3 + nf], refs[3 + nf : 3 + 2 * nf]
    gh, gnt, gh_sum, acc = refs[3 + 2 * nf :]
    block = wd[0].shape[1]
    chunk = min(CHUNK, gh.shape[1])
    acc[...] = jnp.zeros_like(acc)

    def step(i, _):
        at = pl.ds(pl.multiple_of(i * chunk, chunk), chunk)
        ga = mm(gl[:, :block], wd[0][at, :], NT)
        for p in range(1, nf):
            ga = ga + mm(gl[:, p * block : (p + 1) * block], wd[p][at, :], NT)
        g = (ga * slope[:, at]).astype(bf16)
        gh[:, at] = g
        gh_sum[:, at] = jnp.sum(g.astype(f32), axis=0, keepdims=True)
        for p in range(nf):
            acc[:, p * block : (p + 1) * block] += mm(g, wu[p][:, at], NT)
        return 0

    lax.fori_loop(0, gh.shape[1] // chunk, step, 0)
    gnt[...] = acc[...].astype(bf16)


def down_kernel(nf, idx, active, *refs):
    out = refs[nf]
    block = refs[0].shape[1]
    for p in range(nf):
        out[:, p * block : (p + 1) * block] = mm(active[...], refs[p][...]).astype(bf16)


def attend_back_kernel(nc, nf, *refs):
    idx, gl, own, got, unit2, rate2, small, q, k, v = refs[:10]
    aux = refs[10 : 10 + nf]
    gmid, gb, gq, gk, gv, sums, qv_sum, gm = refs[10 + nf :]
    n = gl.shape[0] // nc
    block = small.shape[2]
    hc = q.shape[1]
    gain = rows_of(small, 2)
    totals = [0.0] * 4
    for s in range(nc):
        here = slice(s * n, (s + 1) * n)
        g = own[here, :].astype(f32) + got[here, :].astype(f32)
        u = unit2[here, :]
        c = gl[here, :].astype(f32)
        x = c + norm_back(g, gain, u, rate2[here, :1])
        gmid[here, :] = x
        low = x.astype(bf16)
        gb[here, :] = low
        for r, value in enumerate((g * u, g, low.astype(f32), c)):
            totals[r] = totals[r] + jnp.sum(value, axis=0, keepdims=True)
    sums[...] = jnp.concatenate(totals + [jnp.zeros((4, gl.shape[1]), f32)], axis=0)
    acc = mm(gb[:, :block], unfold(aux[0][:block], block), NT)
    for p in range(1, nf):
        acc = acc + mm(gb[:, p * block : (p + 1) * block], unfold(aux[p][:block], block), NT)
    gm[...] = acc.astype(bf16)
    keep = live_keys(idx, nc, n)
    halves = sides(128)
    scale = HD**-0.5

    def pair(i, _):
        at = pl.ds(pl.multiple_of(i * 128, 128), 128)
        qp, kp, vp, gp = q[:, at], k[:, at], v[:, at], gm[:, at]
        dq, dk, dv = [], [], []
        for h in halves:
            prob = softmax_of(only(h, qp), kp, keep, scale)
            grad = mm(only(h, gp), vp, NT)
            dv.append(mm(prob.astype(bf16), gp, TN))
            ds = (prob * (grad - jnp.sum(prob * grad, axis=-1, keepdims=True))).astype(bf16)
            dq.append(mm(ds, kp))
            dk.append(mm(ds, qp, TN))
        a = (merge(halves, dq) * scale).astype(bf16)
        b = merge(halves, dv).astype(bf16)
        gq[:, at] = a
        gk[:, at] = (merge(halves, dk) * scale).astype(bf16)
        gv[:, at] = b
        total = [jnp.sum(x.astype(f32), axis=0, keepdims=True) for x in (a, b)]
        qv_sum[:, at] = jnp.concatenate(total + [jnp.zeros((6, 128), f32)], axis=0)
        return 0

    lax.fori_loop(0, hc // 128, pair, 0)


def normed_back_kernel(nf, nt, n_up, idx, gq, gk, gv, unit1, sums, qv_sum, gh_sum, ffn, *refs):
    wq, (gn, cross, pack) = refs[:nf], refs[nf:]
    block = pack.shape[2]
    order = bitrev(nf)
    first = jnp.where(idx[2] == 0, 1.0, 0.0)
    held = nf // nt
    for p in range(nf):
        here = slice(p * block, (p + 1) * block)
        acc = mm(gq[...], wq[p][:block], NT) + mm(gk[...], wq[p][block : 2 * block], NT)
        acc = acc + mm(gv[...], wq[p][2 * block : 3 * block], NT)
        gn[:, here] = acc.astype(bf16)
        cross[:, here] = jnp.where(idx[2] == 0, acc, ffn[:, here].astype(f32)).astype(bf16)
        rows = [jnp.sum(acc * unit1[:, here], axis=0, keepdims=True), jnp.sum(acc, axis=0, keepdims=True)]
        rows += [sums[r : r + 1, here] * first for r in range(4)]
        which = (idx[0] ^ order[p]) - idx[2] * held

        def mine(of):
            out = jnp.zeros((1, block), f32)
            for i in range(held):
                out = jnp.where(which == i, of(i), out)
            return out

        rows += [mine(lambda i, r=r: qv_sum[r : r + 1, i * block : (i + 1) * block]) for r in range(2)]
        rows += [
            mine(lambda i, r=r: gh_sum[:, (i * n_up + r) * block : (i * n_up + r + 1) * block]) for r in range(n_up)
        ]
        rows.append(jnp.zeros((PACK - len(rows), block), f32))
        pack[p] = jnp.concatenate(rows, axis=0).astype(bf16)


def outputs_kernel(nc, idx, ffn, cross_got, middle, gn, unit1, rate1, gmid, small, stay, pass_on, go, box):
    n = gmid.shape[0] // nc
    outs = [stay, go.at[0], pass_on, go.at[1]]

    @pl.when(idx[2] == 0)
    def _():
        bias = rows_of(small, 5)
        for s in range(nc):
            here = slice(s * n, (s + 1) * n)
            x = middle[here, :] + (ffn[here, :].astype(f32) + cross_got[here, :].astype(f32) + bias)
            outs[s][...] = from_relative(idx, jnp.where(live_rows(idx, s, n), x, 0.0), box).astype(bf16)

    @pl.when(idx[2] != 0)
    def _():
        gain = rows_of(small, 0)
        for s in range(nc):
            here = slice(s * n, (s + 1) * n)
            g = gn[here, :].astype(f32) + cross_got[here, :].astype(f32)
            x = gmid[here, :] + norm_back(g, gain, unit1[here, :], rate1[here, :1])
            outs[s][...] = from_relative(idx, jnp.where(live_rows(idx, s, n), x, 0.0), box).astype(bf16)


def relay_kernel(_, own, got, out):
    out[0] = own[...]
    out[1] = got[1]


def assemble_kernel(idx, own, near, far, out):
    out[idx[1]] = own[...]
    out[idx[1] ^ 1] = near[0]
    out[idx[1] ^ 2] = far[0]
    out[idx[1] ^ 3] = far[1]


def split_kernel(idx, own, got, result, grad):
    @pl.when(idx[2] == 0)
    def _():
        result[...] = own[...]
        grad[...] = got[...].astype(f32)

    @pl.when(idx[2] != 0)
    def _():
        result[...] = got[...]
        grad[...] = own[...].astype(f32)


def shard_kernel(first, last, parts, base, block, levels, *refs):
    refs = list(refs[1:])
    mats = [refs.pop(0) for kind in parts for _ in range(1 if kind == "small" else 2)]
    early = [refs.pop(0)] if base is not None and base >= 0 else []
    gots = [[refs.pop(0) for _ in range(first, last)] for _ in range(levels)]
    outs = [refs[0].at[p] for p in range(last - first)] if base is None else refs
    for p, out in enumerate(outs):
        at, taken = 0, 0
        low = (first + p) * block
        for kind in parts:
            if kind == "small":
                x = mats[taken][first + p].astype(f32)
                x = jnp.concatenate([x, jnp.zeros((PACK, out.shape[1] - block), f32)], axis=1)
            elif kind == "out":
                x = fold(mm(mats[taken][...], mats[taken + 1][:, low : low + block], TN), block, out.shape[1])
            else:
                start = low + (block // 2 if kind == "second_half" else 0)
                size = block if kind == "all" else block // 2
                x = mm(mats[taken][:, start : start + size], mats[taken + 1][...], TN)
            size = x.shape[0]
            for got in early:
                x = x + got[first + p, base + at : base + at + size].astype(f32)
            for got in gots:
                x = x + got[p][at : at + size].astype(f32)
            out[at : at + size] = x.astype(bf16)
            at += size
            taken += 1 if kind == "small" else 2


def add_kernel(_, x, got, out):
    out[...] = (x[...].astype(f32) + got[...].astype(f32)).astype(bf16)


def picked(idx, own, got):
    return jnp.where(idx[4] == 1, got.astype(f32), own.astype(f32))


def finish_up_kernel(idx, *refs):
    out = refs[-1]
    rows = refs[0].shape[0]
    for i in range(len(refs) // 2):
        out[i * rows : (i + 1) * rows] = picked(idx, refs[2 * i][...], refs[2 * i + 1][...])


def finish_down_kernel(idx, *refs):
    out = refs[-1]
    rows = refs[0].shape[0]
    step = min(out.shape[0], 512)
    for i in range(len(refs) // 2):
        for j in range(0, out.shape[0], step):
            x = picked(idx, refs[2 * i][:, j : j + step], refs[2 * i + 1][:, j : j + step])
            out[j : j + step, i * rows : (i + 1) * rows] = x.T


def small_kernel(block, idx, own, got, out):
    out[...] = picked(idx, own[2 * block :, :block], got[2 * block :, :block]).astype(bf16)


def finish_kernel(block, idx, a, a_got, b, b_got, qkv, out_w):
    kv = picked(idx, a[: 2 * block], a_got[: 2 * block])
    qo = picked(idx, b[...], b_got[...])
    qkv[:block] = qo[:block]
    qkv[block:] = kv
    out_w[...] = unfold(qo[block:], block)


def shape(*dims, dtype=f32):
    return jax.ShapeDtypeStruct(dims, dtype)


def local(
    inputs,
    lengths,
    ln1_gain,
    ln1_bias,
    w_qkv,
    qv_bias,
    w_out,
    out_bias,
    ln2_gain,
    ln2_bias,
    w_up,
    up_bias,
    w_down,
    down_bias,
    cotangent,
):
    nf, nc, nt = (lax.axis_size(a) for a in ("fsdp", "ctx", "tp"))
    f, c, t = (lax.axis_index(a) for a in ("fsdp", "ctx", "tp"))
    images, n, width = inputs.shape
    assert images == nc
    rows = n * nc
    block = width // nf
    hc = w_qkv.shape[2]
    ff = w_up.shape[1]
    n_up = up_bias.shape[0] // block
    outer = (c == 0) | (c == nc - 1)
    idx = jnp.stack([f, c, t, lax.dynamic_index_in_dim(lengths, c, 0, False), outer.astype(jnp.int32)]).astype(jnp.int32)
    wide = functools.partial(shape, rows, width)

    def to_image(x):
        return [lax.dynamic_index_in_dim(x, c, 0, False)] + [
            swap(lax.dynamic_index_in_dim(x, c ^ s, 0, False), "ctx", s) for s in range(1, nc)
        ]

    clock = []

    w_proj = w_qkv.transpose(1, 0, 2).reshape(3 * block, hc)
    proj_got = first_swap(w_proj, "fsdp")
    toks = to_image(inputs)
    (packed,) = call(
        pack_kernel,
        [shape(block + PACK, hc, dtype=bf16)],
        [idx, w_out, ln1_gain, ln1_bias, ln2_gain, ln2_bias, out_bias, down_bias, qv_bias, up_bias.reshape(n_up, block)],
        name="pack",
    )
    packed_got = first_swap(packed, "fsdp")
    proj_got, packed_got, w_up_later, toks = tie(proj_got, packed_got, w_up, toks)
    wq = gather([w_proj, proj_got], "fsdp")
    aux = gather([packed, packed_got], "fsdp")
    up_got = first_swap(w_up_later, "fsdp")
    masked, unit1, rate1, normed, q, k, v, mixed, branch_a, branch_b, up_shift, small = call(
        functools.partial(attend_kernel, nc, nf, nt, n_up),
        [
            wide(dtype=bf16),
            wide(),
            shape(rows, 128),
            wide(dtype=bf16),
            *[shape(rows, hc, dtype=bf16)] * 4,
            *[shape(rows // 2, width, dtype=bf16)] * 2,
            shape(1, ff),
            shape(nf, PACK, block, dtype=bf16),
        ],
        [idx],
        [
            pltpu.VMEM((nf, n, block), f32),
            pltpu.VMEM((nc, n, width), bf16),
            pltpu.VMEM((nf, 3 * block, hc), bf16),
            pltpu.VMEM((nf, block + PACK, hc), bf16),
            pltpu.SemaphoreType.DMA((nc + 2 * nf,)),
        ],
        mib=24,
        far=[*toks, *wq, *aux],
        clock=clock,
        name="attend",
    )
    got_a, got_b = swap(branch_a, "tp", 1), swap(branch_b, "tp", 1)
    got_a, up_got, w_down_later, cotangent = tie(got_a, up_got, w_down, cotangent)
    cots = to_image(cotangent)
    wu = gather([w_up, up_got], "fsdp")
    down_got = first_swap(w_down_later, "fsdp")

    middle, unit2, rate2, normed2, active, slope = call(
        functools.partial(up_kernel, nc, nf),
        [
            wide(),
            wide(),
            shape(rows, 128),
            wide(dtype=bf16),
            shape(rows, ff, dtype=bf16),
            shape(rows, ff),
        ],
        [idx, masked, branch_a, branch_b, got_a, got_b, small, up_shift, *wu],
        clock=clock,
        name="hidden",
    )
    (gl,) = call(
        functools.partial(cotangent_kernel, nc),
        [wide(dtype=bf16)],
        [idx, *cots],
        [pltpu.VMEM((nf, n, block), f32)],
        clock=clock,
        name="cotangent",
    )

    def shard_sum(names, pieces):
        kinds = {"small": PACK, "first_half": block // 2, "second_half": block // 2}
        heights = [sum(kinds.get(kind, block) for kind in parts) for parts, _ in pieces]
        width_in = ff if len(pieces[0][0]) == 1 else hc

        def run(first, last, early, got, level, piece):
            if piece is None:
                parts, mats, base = sum((p for p, _ in pieces), ()), sum((m for _, m in pieces), ()), None
                outs = [shape(last - first, sum(heights), width_in, dtype=bf16)]
            else:
                (parts, mats), base = pieces[piece], sum(heights[:piece]) if early is not None else -1
                outs = [shape(heights[piece], width_in, dtype=bf16)] * (last - first)
            return call(
                functools.partial(shard_kernel, first, last, parts, base, block, len(got)),
                outs,
                [idx, *mats, *([] if early is None else [early]), *[x for one in got for x in one[first:last]]],
                clock=clock,
                name=names[0] + "0" if piece is None else f"{names[piece + 1]}{level}",
            )

        return ShardSum(run)

    levels = len(bits_of(nf))
    first, second = ("first_half",), ("second_half",)
    down = shard_sum(("d", "da", "db"), [(first, (gl, active)), (second, (gl, active))])
    down.start_by_pieces()
    down_got, down.got = tie(down_got, down.got)
    wd = gather([w_down, down_got], "fsdp")
    part_a, part_b = down.begin(0), down.begin(1)
    slope, part_a, part_b = tie(slope, part_a, part_b)
    down.send(part_a, 0)
    down.send(part_b, 1)
    gh, gnt, gh_sum = call(
        functools.partial(hidden_back_kernel, nf),
        [shape(rows, ff, dtype=bf16), wide(dtype=bf16), shape(1, ff)],
        [idx, gl, slope, *wd, *wu],
        [pltpu.VMEM((rows, width), f32)],
        clock=clock,
        name="hidden_back",
    )
    gnt_got = swap(gnt, "tp", 1)
    assert nt == 2 and nc == 4

    o = types.SimpleNamespace(lines={})
    clock.append(LATE)

    def back():
        o.gmid, o.gb, o.gq, o.gk, o.gv, o.sums, o.qv_sum = call(
            functools.partial(attend_back_kernel, nc, nf),
            [wide(), wide(dtype=bf16), *[shape(rows, hc, dtype=bf16)] * 3, shape(8, width), shape(8, hc)],
            [idx, gl, gnt, gnt_got, unit2, rate2, small, q, k, v, *aux],
            [pltpu.VMEM((rows, hc), bf16)],
            clock=clock,
            name="back",
        )

    def normed_back():
        o.gn, o.cross, o.pack = call(
            functools.partial(normed_back_kernel, nf, nt, n_up),
            [wide(dtype=bf16), wide(dtype=bf16), shape(nf, PACK, block, dtype=bf16)],
            [idx, o.gq, o.gk, o.gv, unit1, o.sums, o.qv_sum, gh_sum, o.ffn, *wq],
            clock=clock,
            name="normed",
        )
        o.cross_got = swap(o.cross, "tp", 1)

    def outputs():
        o.stay, o.pass_on, o.go = call(
            functools.partial(outputs_kernel, nc),
            [shape(n, width, dtype=bf16), shape(n, width, dtype=bf16), shape(2, n, width, dtype=bf16)],
            [idx, o.ffn, o.cross_got, middle, o.gn, unit1, rate1, o.gmid, small],
            [pltpu.VMEM((nf, n, block), f32)],
            clock=clock,
            name="outputs",
        )
        o.near = swap(o.go, "ctx", 1)

    def relay():
        (x,) = call(relay_kernel, [shape(2, n, width, dtype=bf16)], [idx, o.pass_on, o.near], clock=clock, name="relay")
        o.far = swap(x, "ctx", 2)

    def assemble():
        out, args = [shape(nc, n, width, dtype=bf16)], [idx, o.stay, o.near, o.far]
        (o.ours,) = call(assemble_kernel, out, args, clock=clock, name="assemble")
        o.theirs = swap(o.ours, "tp", 1)

    def split():
        out = [shape(nc, n, width, dtype=bf16), shape(nc, n, width)]
        o.result, o.grad_inputs = call(split_kernel, out, [idx, o.ours, o.theirs], clock=clock, name="split")

    def finish_down():
        args = [idx, *o.lines["da"].ends(), *o.lines["db"].ends()]
        (o.grad_down,) = call(finish_down_kernel, [shape(ff, block)], args, clock=clock, name="grad_down")

    def finish_up():
        args = [idx, *o.lines["ua"].ends(), *o.lines["ub"].ends()]
        (o.grad_up,) = call(finish_up_kernel, [shape(block, ff)], args, clock=clock, name="grad_up")

    def small_sums():
        out, args = [shape(PACK, block, dtype=bf16)], [idx, *o.lines["kv"].ends()]
        (x,) = call(functools.partial(small_kernel, block), out, args, clock=clock, name="small")
        o.total = x.astype(f32) + swap(x, "tp", 1).astype(f32)

    def finish():
        o.grad_qkv, o.grad_out = call(
            functools.partial(finish_kernel, block),
            [shape(3 * block, hc), shape(hc, block)],
            [idx, *o.lines["kv"].ends(), *o.lines["qo"].ends()],
            clock=clock,
            name="finish",
        )

    def ffn_out():
        (o.ffn,) = call(functools.partial(down_kernel, nf), [wide(dtype=bf16)], [idx, active, *wd], clock=clock, name="ffn")

    def start_up():
        o.up = shard_sum(("u", "ua", "ub"), [(first, (normed2, gh)), (second, (normed2, gh))])
        o.up.start()

    def start_rest():
        kv = (("all", "all", "small"), (normed, o.gk, normed, o.gv, o.pack))
        qo = (("all", "out"), (normed, o.gq, mixed, o.gb))
        o.rest = shard_sum(("t", "kv", "qo"), [kv, qo])
        o.rest.start()

    o.down = down
    places = {"da": ("down", 0), "db": ("down", 1), "ua": ("up", 0), "ub": ("up", 1), "kv": ("rest", 0), "qo": ("rest", 1)}
    steps = {
        "back": back,
        "normed": normed_back,
        "outputs": outputs,
        "relay": relay,
        "assemble": assemble,
        "split": split,
        "grad_down": finish_down,
        "grad_up": finish_up,
        "small": small_sums,
        "finish": finish,
        "ffn": ffn_out,
        "u0": start_up,
        "t0": start_rest,
    }
    for name in ORDER:
        if name in steps:
            steps[name]()
        elif name[-1] == "1":
            which, piece = places[name[:-1]]
            one = getattr(o, which)
            one.send(one.begin(piece), piece)
        elif name[-1] == "2":
            which, piece = places[name[:-1]]
            one = getattr(o, which)
            for _ in range(2, levels):
                one.send(one.begin(piece), piece)
            o.lines[name[:-1]] = Line(one.own(piece), idx, clock)
        else:
            o.lines[name].advance(name)
    total = o.total[:]
    return (
        o.result,
        o.grad_inputs,
        total[0],
        total[1],
        o.grad_qkv.reshape(3, block, hc).transpose(1, 0, 2),
        total[6:8],
        o.grad_out,
        total[4],
        total[2],
        total[3],
        o.grad_up,
        total[8 : 8 + n_up].reshape(-1),
        o.grad_down,
        total[5],
    )


def solution(mesh):
    in_specs = (
        P("fsdp", "ctx", None),
        P("fsdp"),
        P("fsdp"),
        P("fsdp"),
        P("fsdp", None, "tp"),
        P(None, "fsdp"),
        P("tp", "fsdp"),
        P("fsdp"),
        P("fsdp"),
        P("fsdp"),
        P("fsdp", "tp"),
        P("fsdp"),
        P("tp", "fsdp"),
        P("fsdp"),
        P("fsdp", "ctx", None),
    )
    out_specs = (
        P("fsdp", "ctx", None),
        P("fsdp", "ctx", None),
        P("fsdp"),
        P("fsdp"),
        P("fsdp", None, "tp"),
        P(None, "fsdp"),
        P("tp", "fsdp"),
        P("fsdp"),
        P("fsdp"),
        P("fsdp"),
        P("fsdp", "tp"),
        P("fsdp"),
        P("tp", "fsdp"),
        P("fsdp"),
    )
    return jax.shard_map(local, mesh=mesh, in_specs=in_specs, out_specs=out_specs, check_vma=False)
```

```python
import functools
import types

import jax
import jax.numpy as jnp
from jax import lax
from jax.experimental import pallas as pl
from jax.experimental.pallas import tpu as pltpu
from jax.sharding import PartitionSpec as P

HD = 64
epsilon = 1e-06
f32 = jnp.float32
bf16 = jnp.bfloat16
PACK = 16
CHUNK = 512
LATE = "late"
ORDER = (
    "u0", "da2", "ffn", "ub1", "ua1", "db2", "back", "da", "ub2", "normed", "t0", "db", "ua2", "kv1", "ub", "outputs",
    "ua", "da", "kv2", "db", "qo1", "relay", "ua", "kv", "grad_down", "ub", "qo2", "assemble", "qo", "kv", "split",
    "qo", "small", "grad_up", "finish",
)


def bits_of(n):
    out, bit = [], 1
    while bit < n:
        out.append(bit)
        bit *= 2
    return out


def bitrev(n):
    order = [0]
    for bit in reversed(bits_of(n)):
        order = order + [j | bit for j in order]
    return order


def place(x, n):
    bits = len(bits_of(n))
    out = 0
    for k in range(bits):
        out = out + ((x >> k) & 1) * (1 << (bits - 1 - k))
    return out


def swap(x, axis, bit):
    return lax.ppermute(x, axis, [(i, i ^ bit) for i in range(lax.axis_size(axis))])


def gather(pieces, axis):
    for bit in reversed(bits_of(lax.axis_size(axis) // len(pieces))):
        pieces = pieces + [swap(p, axis, bit) for p in pieces]
    return pieces


def first_swap(piece, axis):
    return swap(piece, axis, bits_of(lax.axis_size(axis))[-1])


class ShardSum:
    def __init__(self, run):
        self.run, self.n, self.first, self.got = run, lax.axis_size("fsdp"), None, [[], []]

    def start(self):
        (x,) = self.run(self.n // 2, self.n, None, [], 0, None)
        self.first = swap(x, "fsdp", 1)

    def start_by_pieces(self):
        for piece in range(2):
            self.send(self.begin(piece), piece)

    def level(self, piece):
        return len(self.got[piece]) + (self.first is not None)

    def begin(self, piece):
        level = self.level(piece)
        n = self.n >> level
        return self.run(n // 2, n, self.first, self.got[piece], level, piece)

    def send(self, blocks, piece):
        level = self.level(piece)
        self.got[piece].append([swap(x, "fsdp", 1 << level) for x in blocks])

    def own(self, piece):
        return self.run(0, 1, self.first, self.got[piece], self.level(piece), piece)[0]


def tie(*trees):
    flat, where = jax.tree.flatten(trees)
    return jax.tree.unflatten(where, lax.optimization_barrier(flat))


class Line:
    def __init__(self, x, idx, clock):
        assert lax.axis_size("ctx") == 4
        self.held, self.idx, self.clock, self.step = x, idx, clock, 0
        self.got = self.send()

    def send(self):
        pairs = ([(0, 1), (3, 2)], [(1, 2), (2, 1)], [(1, 0), (2, 3)])[self.step]
        return lax.ppermute(self.held, "ctx", pairs)

    def advance(self, name):
        self.step += 1
        out = [jax.ShapeDtypeStruct(self.held.shape, bf16)]
        args, name = [self.idx, self.held, self.got], f"{name}_{self.step}"
        (self.held,) = call(add_kernel, out, args, clock=self.clock, name=name)
        self.got = self.send()

    def ends(self):
        return [self.held, self.got]


NN = (((1,), (0,)), ((), ()))
NT = (((1,), (1,)), ((), ()))
TN = (((0,), (0,)), ((), ()))


def mm(a, b, dims=NN):
    return lax.dot_general(a, b, dims, preferred_element_type=f32)


def call(kernel, outs, args, scratch=(), mib=12, far=(), clock=None, name=None):
    vm = pl.BlockSpec(memory_space=pltpu.VMEM)
    near = len(args)
    last = [] if clock is None else [x for x in clock if x is not LATE]
    late = clock is not None and any(x is LATE for x in clock)
    args = [*args, *far, *last]
    count = len(args) - len(last)

    def body(*refs):
        kernel(*refs[:count], *refs[count + len(last) :])

    results = pl.pallas_call(
        body,
        out_shape=outs,
        in_specs=[pl.BlockSpec(memory_space=pltpu.SMEM)]
        + [vm] * (near - 1)
        + [pl.BlockSpec(memory_space=pl.ANY)] * (len(far) + len(last)),
        out_specs=[vm] * len(outs),
        scratch_shapes=list(scratch),
        compiler_params=pltpu.CompilerParams(vmem_limit_bytes=mib << 20),
        cost_estimate=pl.CostEstimate(flops=int(3e10) if late else 0, bytes_accessed=0, transcendentals=0),
        name=name,
    )(*args)
    if clock is not None:
        clock[:] = [results[-1], LATE] if late else [results[-1]]
    return results


def rows_of(small, r):
    return jnp.concatenate([small[p].astype(f32)[r : r + 1] for p in range(small.shape[0])], axis=1)


def live_rows(idx, s, n):
    return (idx[1] ^ s) * n + lax.broadcasted_iota(jnp.int32, (n, 1), 0) < idx[3]


def live_keys(idx, nc, n):
    col = lax.broadcasted_iota(jnp.int32, (1, nc * n), 1)
    slot = col
    for s in range(nc):
        slot = jnp.where((col >= s * n) & (col < (s + 1) * n), slot + ((idx[1] ^ s) - s) * n, slot)
    return slot < idx[3]


def to_relative(idx, x, box):
    nf, _, block = box.shape
    for b in range(nf):
        box[place(idx[0] ^ b, nf)] = x[:, b * block : (b + 1) * block]
    return jnp.concatenate([box[p] for p in range(nf)], axis=1)


def from_relative(idx, x, box):
    nf, _, block = box.shape
    for p in range(nf):
        box[p] = x[:, p * block : (p + 1) * block]
    return jnp.concatenate([box[place(idx[0] ^ b, nf)] for b in range(nf)], axis=1)


def mean(x):
    return jnp.mean(x, axis=-1, keepdims=True)


def normalize(x):
    center = x - mean(x)
    rate = lax.rsqrt(mean(center * center) + epsilon)
    return center * rate, rate


def norm_back(grad, gain, unit, rate):
    e = grad * gain
    return rate * (e - mean(e) - unit * mean(e * unit))


def softmax_of(q, k, keep, scale):
    scores = jnp.where(keep, mm(q, k, NT) * scale, -1e30)
    expo = jnp.exp(scores - jnp.max(scores, axis=-1, keepdims=True))
    return expo * (1.0 / jnp.sum(expo, axis=-1, keepdims=True))


def sides(n):
    lane = lax.broadcasted_iota(jnp.int32, (1, n), 1)
    return [(lane >= h * HD) & (lane < (h + 1) * HD) for h in range(n // HD)]


def only(keep, x):
    return jnp.where(keep, x.astype(f32), 0.0).astype(x.dtype)


def merge(keeps, parts):
    out = parts[0]
    for keep, part in zip(keeps[1:], parts[1:]):
        out = jnp.where(keep, part, out)
    return out


def fold(x, block, width):
    k = width // block
    rows = x.shape[0] // k
    return jnp.concatenate([x[i * rows : (i + 1) * rows] for i in range(k)], axis=1)


def unfold(x, block):
    return jnp.concatenate([x[:, i * block : (i + 1) * block] for i in range(x.shape[1] // block)], axis=0)


def pack_kernel(_, wo, *refs):
    *vectors, qv, up, out = refs
    block = qv.shape[1]
    out[:block] = fold(wo[...], block, out.shape[1])
    lines = [x[...].astype(f32).reshape(1, block) for x in vectors] + [qv[...].astype(f32), up[...].astype(f32)]
    lines.append(jnp.zeros((PACK - 8 - up.shape[0], block), f32))
    out[block:, :block] = jnp.concatenate(lines, axis=0).astype(bf16)
    out[block:, block:] = jnp.zeros((PACK, out.shape[1] - block), bf16)


def attend_kernel(nc, nf, nt, n_up, *refs):
    idx, refs = refs[0], refs[1:]
    sources = refs[: nc + 2 * nf]
    masked, unit1, rate1, normed, q, k, v, mixed, *branch, up_shift, small, box, tok_all, w_all, aux_all, sems = refs[
        nc + 2 * nf :
    ]
    toks = [tok_all.at[s] for s in range(nc)]
    wq, aux = [w_all.at[p] for p in range(nf)], [aux_all.at[p] for p in range(nf)]
    places = [*toks, *wq, *aux]
    order = [*range(nc), *range(nc + nf, nc + 2 * nf), *range(nc, nc + nf)]
    copies = {i: pltpu.make_async_copy(sources[i], places[i], sems.at[i]) for i in order}
    for i in order:
        copies[i].start()
    for i in order[: nc + nf]:
        copies[i].wait()
    n = toks[0].shape[0]
    block = small.shape[2]
    for p in range(nf):
        small[p] = aux[p][block:, :block]
    hc = q.shape[1]
    gain, shift = rows_of(small, 0), rows_of(small, 1)
    for s in range(nc):
        here = slice(s * n, (s + 1) * n)
        x = jnp.where(live_rows(idx, s, n), toks[s][...].astype(f32), 0.0)
        x = to_relative(idx, x, box)
        masked[here, :] = x.astype(bf16)
        unit, rate = normalize(x)
        unit1[here, :] = unit
        rate1[here, :] = jnp.broadcast_to(rate, (n, 128))
        normed[here, :] = (unit * gain + shift).astype(bf16)
    shifts = []
    for i in range(nf // nt):
        mine = small[place(idx[0] ^ (idx[2] * (nf // nt) + i), nf)].astype(f32)
        shifts.append((mine[6:7], mine[7:8]))
        for r in range(n_up):
            up_shift[:, (i * n_up + r) * block : (i * n_up + r + 1) * block] = mine[8 + r : 9 + r]
    q_shift = jnp.concatenate([a for a, _ in shifts], axis=1)
    v_shift = jnp.concatenate([b for _, b in shifts], axis=1)
    for i in order[nc + nf :]:
        copies[i].wait()
    for j, (out, bias) in enumerate(((q, q_shift), (k, None), (v, v_shift))):
        acc = mm(normed[:, :block], wq[0][j * block : (j + 1) * block])
        for p in range(1, nf):
            acc = acc + mm(normed[:, p * block : (p + 1) * block], wq[p][j * block : (j + 1) * block])
        out[...] = (acc if bias is None else acc + bias).astype(bf16)
    keep = live_keys(idx, nc, n)
    halves = sides(128)

    def pair(i, _):
        at = pl.ds(pl.multiple_of(i * 128, 128), 128)
        qp, kp, vp = q[:, at], k[:, at], v[:, at]
        parts = [mm(softmax_of(only(h, qp), kp, keep, HD**-0.5).astype(bf16), vp) for h in halves]
        mixed[:, at] = merge(halves, parts).astype(bf16)
        return 0

    lax.fori_loop(0, hc // 128, pair, 0)
    for p in range(nf):
        out_w = unfold(aux[p][:block], block)
        for h, out in enumerate(branch):
            part = mixed[h * out.shape[0] : (h + 1) * out.shape[0]]
            out[:, p * block : (p + 1) * block] = mm(part, out_w).astype(bf16)


def up_kernel(nc, nf, *refs):
    idx, masked, own_a, own_b, got_a, got_b, small, up_shift = refs[:8]
    wu = refs[8 : 8 + nf]
    middle, unit2, rate2, normed2, active, slope = refs[8 + nf :]
    n = masked.shape[0] // nc
    block = small.shape[2]
    gain, shift, bias = rows_of(small, 2), rows_of(small, 3), rows_of(small, 4)
    for s in range(nc):
        here = slice(s * n, (s + 1) * n)
        own, got = (own_a, got_a) if s < nc // 2 else (own_b, got_b)
        part = slice(s % (nc // 2) * n, (s % (nc // 2) + 1) * n)
        x = masked[here, :].astype(f32) + (own[part, :].astype(f32) + got[part, :].astype(f32) + bias)
        middle[here, :] = x
        unit, rate = normalize(x)
        unit2[here, :] = unit
        rate2[here, :] = jnp.broadcast_to(rate, (n, 128))
        normed2[here, :] = (unit * gain + shift).astype(bf16)
    chunk = min(CHUNK, active.shape[1])

    def step(i, _):
        at = pl.ds(pl.multiple_of(i * chunk, chunk), chunk)
        acc = mm(normed2[:, :block], wu[0][:, at])
        for p in range(1, nf):
            acc = acc + mm(normed2[:, p * block : (p + 1) * block], wu[p][:, at])
        x = acc + up_shift[:, at]
        root = 0.7978845608028654
        tanh = jnp.tanh(root * (x + 0.044715 * (x * x * x)))
        half = 0.5 * (1.0 + tanh)
        active[:, at] = (x * half).astype(bf16)
        slope[:, at] = half + 0.5 * x * (1.0 - tanh * tanh) * (root * (1.0 + 3 * 0.044715 * (x * x)))
        return 0

    lax.fori_loop(0, active.shape[1] // chunk, step, 0)


def cotangent_kernel(idx, own, near, far, gl, box):
    n = own.shape[0]
    for s, x in enumerate((own, near.at[0], far.at[0], far.at[1])):
        c = jnp.where(live_rows(idx, s, n), x[...].astype(f32), 0.0)
        gl[s * n : (s + 1) * n, :] = to_relative(idx, c, box).astype(bf16)


def hidden_back_kernel(nf, *refs):
    _, gl, slope = refs[:3]
    wd, wu = refs[3 : 3 + nf], refs[3 + nf : 3 + 2 * nf]
    gh, gnt, gh_sum, acc = refs[3 + 2 * nf :]
    block = wd[0].shape[1]
    chunk = min(CHUNK, gh.shape[1])
    acc[...] = jnp.zeros_like(acc)

    def step(i, _):
        at = pl.ds(pl.multiple_of(i * chunk, chunk), chunk)
        ga = mm(gl[:, :block], wd[0][at, :], NT)
        for p in range(1, nf):
            ga = ga + mm(gl[:, p * block : (p + 1) * block], wd[p][at, :], NT)
        g = (ga * slope[:, at]).astype(bf16)
        gh[:, at] = g
        gh_sum[:, at] = jnp.sum(g.astype(f32), axis=0, keepdims=True)
        for p in range(nf):
            acc[:, p * block : (p + 1) * block] += mm(g, wu[p][:, at], NT)
        return 0

    lax.fori_loop(0, gh.shape[1] // chunk, step, 0)
    gnt[...] = acc[...].astype(bf16)


def down_kernel(nf, idx, active, *refs):
    out = refs[nf]
    block = refs[0].shape[1]
    for p in range(nf):
        out[:, p * block : (p + 1) * block] = mm(active[...], refs[p][...]).astype(bf16)


def attend_back_kernel(nc, nf, *refs):
    idx, gl, own, got, unit2, rate2, small, q, k, v = refs[:10]
    aux = refs[10 : 10 + nf]
    gmid, gb, gq, gk, gv, sums, qv_sum, gm = refs[10 + nf :]
    n = gl.shape[0] // nc
    block = small.shape[2]
    hc = q.shape[1]
    gain = rows_of(small, 2)
    totals = [0.0] * 4
    for s in range(nc):
        here = slice(s * n, (s + 1) * n)
        g = own[here, :].astype(f32) + got[here, :].astype(f32)
        u = unit2[here, :]
        c = gl[here, :].astype(f32)
        x = c + norm_back(g, gain, u, rate2[here, :1])
        gmid[here, :] = x
        low = x.astype(bf16)
        gb[here, :] = low
        for r, value in enumerate((g * u, g, low.astype(f32), c)):
            totals[r] = totals[r] + jnp.sum(value, axis=0, keepdims=True)
    sums[...] = jnp.concatenate(totals + [jnp.zeros((4, gl.shape[1]), f32)], axis=0)
    acc = mm(gb[:, :block], unfold(aux[0][:block], block), NT)
    for p in range(1, nf):
        acc = acc + mm(gb[:, p * block : (p + 1) * block], unfold(aux[p][:block], block), NT)
    gm[...] = acc.astype(bf16)
    keep = live_keys(idx, nc, n)
    halves = sides(128)
    scale = HD**-0.5

    def pair(i, _):
        at = pl.ds(pl.multiple_of(i * 128, 128), 128)
        qp, kp, vp, gp = q[:, at], k[:, at], v[:, at], gm[:, at]
        dq, dk, dv = [], [], []
        for h in halves:
            prob = softmax_of(only(h, qp), kp, keep, scale)
            grad = mm(only(h, gp), vp, NT)
            dv.append(mm(prob.astype(bf16), gp, TN))
            ds = (prob * (grad - jnp.sum(prob * grad, axis=-1, keepdims=True))).astype(bf16)
            dq.append(mm(ds, kp))
            dk.append(mm(ds, qp, TN))
        a = (merge(halves, dq) * scale).astype(bf16)
        b = merge(halves, dv).astype(bf16)
        gq[:, at] = a
        gk[:, at] = (merge(halves, dk) * scale).astype(bf16)
        gv[:, at] = b
        total = [jnp.sum(x.astype(f32), axis=0, keepdims=True) for x in (a, b)]
        qv_sum[:, at] = jnp.concatenate(total + [jnp.zeros((6, 128), f32)], axis=0)
        return 0

    lax.fori_loop(0, hc // 128, pair, 0)


def normed_back_kernel(nf, nt, n_up, idx, gq, gk, gv, unit1, sums, qv_sum, gh_sum, ffn, *refs):
    wq, (gn, cross, pack) = refs[:nf], refs[nf:]
    block = pack.shape[2]
    order = bitrev(nf)
    first = jnp.where(idx[2] == 0, 1.0, 0.0)
    held = nf // nt
    for p in range(nf):
        here = slice(p * block, (p + 1) * block)
        acc = mm(gq[...], wq[p][:block], NT) + mm(gk[...], wq[p][block : 2 * block], NT)
        acc = acc + mm(gv[...], wq[p][2 * block : 3 * block], NT)
        gn[:, here] = acc.astype(bf16)
        cross[:, here] = jnp.where(idx[2] == 0, acc, ffn[:, here].astype(f32)).astype(bf16)
        rows = [jnp.sum(acc * unit1[:, here], axis=0, keepdims=True), jnp.sum(acc, axis=0, keepdims=True)]
        rows += [sums[r : r + 1, here] * first for r in range(4)]
        which = (idx[0] ^ order[p]) - idx[2] * held

        def mine(of):
            out = jnp.zeros((1, block), f32)
            for i in range(held):
                out = jnp.where(which == i, of(i), out)
            return out

        rows += [mine(lambda i, r=r: qv_sum[r : r + 1, i * block : (i + 1) * block]) for r in range(2)]
        rows += [
            mine(lambda i, r=r: gh_sum[:, (i * n_up + r) * block : (i * n_up + r + 1) * block]) for r in range(n_up)
        ]
        rows.append(jnp.zeros((PACK - len(rows), block), f32))
        pack[p] = jnp.concatenate(rows, axis=0).astype(bf16)


def outputs_kernel(nc, idx, ffn, cross_got, middle, gn, unit1, rate1, gmid, small, stay, pass_on, go, box):
    n = gmid.shape[0] // nc
    outs = [stay, go.at[0], pass_on, go.at[1]]

    @pl.when(idx[2] == 0)
    def _():
        bias = rows_of(small, 5)
        for s in range(nc):
            here = slice(s * n, (s + 1) * n)
            x = middle[here, :] + (ffn[here, :].astype(f32) + cross_got[here, :].astype(f32) + bias)
            outs[s][...] = from_relative(idx, jnp.where(live_rows(idx, s, n), x, 0.0), box).astype(bf16)

    @pl.when(idx[2] != 0)
    def _():
        gain = rows_of(small, 0)
        for s in range(nc):
            here = slice(s * n, (s + 1) * n)
            g = gn[here, :].astype(f32) + cross_got[here, :].astype(f32)
            x = gmid[here, :] + norm_back(g, gain, unit1[here, :], rate1[here, :1])
            outs[s][...] = from_relative(idx, jnp.where(live_rows(idx, s, n), x, 0.0), box).astype(bf16)


def relay_kernel(_, own, got, out):
    out[0] = own[...]
    out[1] = got[1]


def assemble_kernel(idx, own, near, far, out):
    out[idx[1]] = own[...]
    out[idx[1] ^ 1] = near[0]
    out[idx[1] ^ 2] = far[0]
    out[idx[1] ^ 3] = far[1]


def split_kernel(idx, own, got, result, grad):
    @pl.when(idx[2] == 0)
    def _():
        result[...] = own[...]
        grad[...] = got[...].astype(f32)

    @pl.when(idx[2] != 0)
    def _():
        result[...] = got[...]
        grad[...] = own[...].astype(f32)


def shard_kernel(first, last, parts, base, block, levels, *refs):
    refs = list(refs[1:])
    mats = [refs.pop(0) for kind in parts for _ in range(1 if kind == "small" else 2)]
    early = [refs.pop(0)] if base is not None and base >= 0 else []
    gots = [[refs.pop(0) for _ in range(first, last)] for _ in range(levels)]
    outs = [refs[0].at[p] for p in range(last - first)] if base is None else refs
    for p, out in enumerate(outs):
        at, taken = 0, 0
        low = (first + p) * block
        for kind in parts:
            if kind == "small":
                x = mats[taken][first + p].astype(f32)
                x = jnp.concatenate([x, jnp.zeros((PACK, out.shape[1] - block), f32)], axis=1)
            elif kind == "out":
                x = fold(mm(mats[taken][...], mats[taken + 1][:, low : low + block], TN), block, out.shape[1])
            else:
                start = low + (block // 2 if kind == "second_half" else 0)
                size = block if kind == "all" else block // 2
                x = mm(mats[taken][:, start : start + size], mats[taken + 1][...], TN)
            size = x.shape[0]
            for got in early:
                x = x + got[first + p, base + at : base + at + size].astype(f32)
            for got in gots:
                x = x + got[p][at : at + size].astype(f32)
            out[at : at + size] = x.astype(bf16)
            at += size
            taken += 1 if kind == "small" else 2


def add_kernel(_, x, got, out):
    out[...] = (x[...].astype(f32) + got[...].astype(f32)).astype(bf16)


def picked(idx, own, got):
    return jnp.where(idx[4] == 1, got.astype(f32), own.astype(f32))


def finish_up_kernel(idx, *refs):
    out = refs[-1]
    rows = refs[0].shape[0]
    for i in range(len(refs) // 2):
        out[i * rows : (i + 1) * rows] = picked(idx, refs[2 * i][...], refs[2 * i + 1][...])


def finish_down_kernel(idx, *refs):
    out = refs[-1]
    rows = refs[0].shape[0]
    step = min(out.shape[0], 512)
    for i in range(len(refs) // 2):
        for j in range(0, out.shape[0], step):
            x = picked(idx, refs[2 * i][:, j : j + step], refs[2 * i + 1][:, j : j + step])
            out[j : j + step, i * rows : (i + 1) * rows] = x.T


def small_kernel(block, idx, own, got, out):
    out[...] = picked(idx, own[2 * block :, :block], got[2 * block :, :block]).astype(bf16)


def finish_kernel(block, idx, a, a_got, b, b_got, qkv, out_w):
    kv = picked(idx, a[: 2 * block], a_got[: 2 * block])
    qo = picked(idx, b[...], b_got[...])
    qkv[:block] = qo[:block]
    qkv[block:] = kv
    out_w[...] = unfold(qo[block:], block)


def shape(*dims, dtype=f32):
    return jax.ShapeDtypeStruct(dims, dtype)


def local(
    inputs,
    lengths,
    ln1_gain,
    ln1_bias,
    w_qkv,
    qv_bias,
    w_out,
    out_bias,
    ln2_gain,
    ln2_bias,
    w_up,
    up_bias,
    w_down,
    down_bias,
    cotangent,
):
    nf, nc, nt = (lax.axis_size(a) for a in ("fsdp", "ctx", "tp"))
    f, c, t = (lax.axis_index(a) for a in ("fsdp", "ctx", "tp"))
    images, n, width = inputs.shape
    assert images == nc == 4 and nt == 2
    rows = n * nc
    block = width // nf
    hc = w_qkv.shape[2]
    ff = w_up.shape[1]
    n_up = up_bias.shape[0] // block
    outer = (c == 0) | (c == nc - 1)
    idx = jnp.stack([f, c, t, lax.dynamic_index_in_dim(lengths, c, 0, False), outer.astype(jnp.int32)]).astype(jnp.int32)
    wide = functools.partial(shape, rows, width)

    def to_image(x):
        return [lax.dynamic_index_in_dim(x, c, 0, False)] + [
            swap(lax.dynamic_index_in_dim(x, c ^ s, 0, False), "ctx", s) for s in range(1, nc)
        ]

    clock = []

    w_proj = w_qkv.transpose(1, 0, 2).reshape(3 * block, hc)
    proj_got = first_swap(w_proj, "fsdp")
    toks = to_image(inputs)
    (packed,) = call(
        pack_kernel,
        [shape(block + PACK, hc, dtype=bf16)],
        [idx, w_out, ln1_gain, ln1_bias, ln2_gain, ln2_bias, out_bias, down_bias, qv_bias, up_bias.reshape(n_up, block)],
        name="pack",
    )
    packed_got = first_swap(packed, "fsdp")
    proj_got, packed_got, w_up_later, toks, cotangent = tie(proj_got, packed_got, w_up, toks, cotangent)
    own, pass_on = (lax.dynamic_index_in_dim(cotangent, c ^ s, 0, False) for s in (0, 2))
    near = swap(jnp.stack([lax.dynamic_index_in_dim(cotangent, c ^ s, 0, False) for s in (1, 3)]), "ctx", 1)
    wq = gather([w_proj, proj_got], "fsdp")
    aux = gather([packed, packed_got], "fsdp")
    up_got = first_swap(w_up_later, "fsdp")
    masked, unit1, rate1, normed, q, k, v, mixed, branch_a, branch_b, up_shift, small = call(
        functools.partial(attend_kernel, nc, nf, nt, n_up),
        [
            wide(dtype=bf16),
            wide(),
            shape(rows, 128),
            wide(dtype=bf16),
            *[shape(rows, hc, dtype=bf16)] * 4,
            *[shape(rows // 2, width, dtype=bf16)] * 2,
            shape(1, ff),
            shape(nf, PACK, block, dtype=bf16),
        ],
        [idx],
        [
            pltpu.VMEM((nf, n, block), f32),
            pltpu.VMEM((nc, n, width), bf16),
            pltpu.VMEM((nf, 3 * block, hc), bf16),
            pltpu.VMEM((nf, block + PACK, hc), bf16),
            pltpu.SemaphoreType.DMA((nc + 2 * nf,)),
        ],
        mib=24,
        far=[*toks, *wq, *aux],
        clock=clock,
        name="attend",
    )
    branch_a, near = tie(branch_a, near)
    got_a, got_b = swap(branch_a, "tp", 1), swap(branch_b, "tp", 1)
    got_a, up_got, w_down_later = tie(got_a, up_got, w_down)
    (relayed,) = call(relay_kernel, [shape(2, n, width, dtype=bf16)], [idx, pass_on, near], name="relay_in")
    cots = [own, near, swap(relayed, "ctx", 2)]
    wu = gather([w_up, up_got], "fsdp")
    down_got = first_swap(w_down_later, "fsdp")

    middle, unit2, rate2, normed2, active, slope = call(
        functools.partial(up_kernel, nc, nf),
        [
            wide(),
            wide(),
            shape(rows, 128),
            wide(dtype=bf16),
            shape(rows, ff, dtype=bf16),
            shape(rows, ff),
        ],
        [idx, masked, branch_a, branch_b, got_a, got_b, small, up_shift, *wu],
        clock=clock,
        name="hidden",
    )
    (gl,) = call(
        cotangent_kernel,
        [wide(dtype=bf16)],
        [idx, *cots],
        [pltpu.VMEM((nf, n, block), f32)],
        clock=clock,
        name="cotangent",
    )

    def shard_sum(names, pieces):
        kinds = {"small": PACK, "first_half": block // 2, "second_half": block // 2}
        heights = [sum(kinds.get(kind, block) for kind in parts) for parts, _ in pieces]
        width_in = ff if len(pieces[0][0]) == 1 else hc

        def run(first, last, early, got, level, piece):
            if piece is None:
                parts, mats, base = sum((p for p, _ in pieces), ()), sum((m for _, m in pieces), ()), None
                outs = [shape(last - first, sum(heights), width_in, dtype=bf16)]
            else:
                (parts, mats), base = pieces[piece], sum(heights[:piece]) if early is not None else -1
                outs = [shape(heights[piece], width_in, dtype=bf16)] * (last - first)
            return call(
                functools.partial(shard_kernel, first, last, parts, base, block, len(got)),
                outs,
                [idx, *mats, *([] if early is None else [early]), *[x for one in got for x in one[first:last]]],
                clock=clock,
                name=names[0] + "0" if piece is None else f"{names[piece + 1]}{level}",
            )

        return ShardSum(run)

    levels = len(bits_of(nf))
    first, second = ("first_half",), ("second_half",)
    down = shard_sum(("d", "da", "db"), [(first, (gl, active)), (second, (gl, active))])
    down.start_by_pieces()
    down_got, down.got = tie(down_got, down.got)
    wd = gather([w_down, down_got], "fsdp")
    part_a, part_b = down.begin(0), down.begin(1)
    slope, part_a, part_b = tie(slope, part_a, part_b)
    down.send(part_a, 0)
    down.send(part_b, 1)
    gh, gnt, gh_sum = call(
        functools.partial(hidden_back_kernel, nf),
        [shape(rows, ff, dtype=bf16), wide(dtype=bf16), shape(1, ff)],
        [idx, gl, slope, *wd, *wu],
        [pltpu.VMEM((rows, width), f32)],
        clock=clock,
        name="hidden_back",
    )
    gnt_got = swap(gnt, "tp", 1)

    o = types.SimpleNamespace(lines={})
    clock.append(LATE)

    def back():
        o.gmid, o.gb, o.gq, o.gk, o.gv, o.sums, o.qv_sum = call(
            functools.partial(attend_back_kernel, nc, nf),
            [wide(), wide(dtype=bf16), *[shape(rows, hc, dtype=bf16)] * 3, shape(8, width), shape(8, hc)],
            [idx, gl, gnt, gnt_got, unit2, rate2, small, q, k, v, *aux],
            [pltpu.VMEM((rows, hc), bf16)],
            clock=clock,
            name="back",
        )

    def normed_back():
        o.gn, o.cross, o.pack = call(
            functools.partial(normed_back_kernel, nf, nt, n_up),
            [wide(dtype=bf16), wide(dtype=bf16), shape(nf, PACK, block, dtype=bf16)],
            [idx, o.gq, o.gk, o.gv, unit1, o.sums, o.qv_sum, gh_sum, o.ffn, *wq],
            clock=clock,
            name="normed",
        )
        o.cross_got = swap(o.cross, "tp", 1)

    def outputs():
        o.stay, o.pass_on, o.go = call(
            functools.partial(outputs_kernel, nc),
            [shape(n, width, dtype=bf16), shape(n, width, dtype=bf16), shape(2, n, width, dtype=bf16)],
            [idx, o.ffn, o.cross_got, middle, o.gn, unit1, rate1, o.gmid, small],
            [pltpu.VMEM((nf, n, block), f32)],
            clock=clock,
            name="outputs",
        )
        o.near = swap(o.go, "ctx", 1)

    def relay():
        (x,) = call(relay_kernel, [shape(2, n, width, dtype=bf16)], [idx, o.pass_on, o.near], clock=clock, name="relay")
        o.far = swap(x, "ctx", 2)

    def assemble():
        out, args = [shape(nc, n, width, dtype=bf16)], [idx, o.stay, o.near, o.far]
        (o.ours,) = call(assemble_kernel, out, args, clock=clock, name="assemble")
        o.theirs = swap(o.ours, "tp", 1)

    def split():
        out = [shape(nc, n, width, dtype=bf16), shape(nc, n, width)]
        o.result, o.grad_inputs = call(split_kernel, out, [idx, o.ours, o.theirs], clock=clock, name="split")

    def finish_down():
        args = [idx, *o.lines["da"].ends(), *o.lines["db"].ends()]
        (o.grad_down,) = call(finish_down_kernel, [shape(ff, block)], args, clock=clock, name="grad_down")

    def finish_up():
        args = [idx, *o.lines["ua"].ends(), *o.lines["ub"].ends()]
        (o.grad_up,) = call(finish_up_kernel, [shape(block, ff)], args, clock=clock, name="grad_up")

    def small_sums():
        out, args = [shape(PACK, block, dtype=bf16)], [idx, *o.lines["kv"].ends()]
        (x,) = call(functools.partial(small_kernel, block), out, args, clock=clock, name="small")
        o.total = x.astype(f32) + swap(x, "tp", 1).astype(f32)

    def finish():
        o.grad_qkv, o.grad_out = call(
            functools.partial(finish_kernel, block),
            [shape(3 * block, hc), shape(hc, block)],
            [idx, *o.lines["kv"].ends(), *o.lines["qo"].ends()],
            clock=clock,
            name="finish",
        )

    def ffn_out():
        (o.ffn,) = call(functools.partial(down_kernel, nf), [wide(dtype=bf16)], [idx, active, *wd], clock=clock, name="ffn")

    def start_up():
        o.up = shard_sum(("u", "ua", "ub"), [(first, (normed2, gh)), (second, (normed2, gh))])
        o.up.start()

    def start_rest():
        kv = (("all", "all", "small"), (normed, o.gk, normed, o.gv, o.pack))
        qo = (("all", "out"), (normed, o.gq, mixed, o.gb))
        o.rest = shard_sum(("t", "kv", "qo"), [kv, qo])
        o.rest.start()

    o.down = down
    places = {"da": ("down", 0), "db": ("down", 1), "ua": ("up", 0), "ub": ("up", 1), "kv": ("rest", 0), "qo": ("rest", 1)}
    steps = {
        "back": back,
        "normed": normed_back,
        "outputs": outputs,
        "relay": relay,
        "assemble": assemble,
        "split": split,
        "grad_down": finish_down,
        "grad_up": finish_up,
        "small": small_sums,
        "finish": finish,
        "ffn": ffn_out,
        "u0": start_up,
        "t0": start_rest,
    }
    for name in ORDER:
        if name in steps:
            steps[name]()
        elif name[-1] == "1":
            which, piece = places[name[:-1]]
            one = getattr(o, which)
            one.send(one.begin(piece), piece)
        elif name[-1] == "2":
            which, piece = places[name[:-1]]
            one = getattr(o, which)
            for _ in range(2, levels):
                one.send(one.begin(piece), piece)
            o.lines[name[:-1]] = Line(one.own(piece), idx, clock)
        else:
            o.lines[name].advance(name)
    total = o.total[:]
    return (
        o.result,
        o.grad_inputs,
        total[0],
        total[1],
        o.grad_qkv.reshape(3, block, hc).transpose(1, 0, 2),
        total[6:8],
        o.grad_out,
        total[4],
        total[2],
        total[3],
        o.grad_up,
        total[8 : 8 + n_up].reshape(-1),
        o.grad_down,
        total[5],
    )


def solution(mesh):
    in_specs = (
        P("fsdp", "ctx", None),
        P("fsdp"),
        P("fsdp"),
        P("fsdp"),
        P("fsdp", None, "tp"),
        P(None, "fsdp"),
        P("tp", "fsdp"),
        P("fsdp"),
        P("fsdp"),
        P("fsdp"),
        P("fsdp", "tp"),
        P("fsdp"),
        P("tp", "fsdp"),
        P("fsdp"),
        P("fsdp", "ctx", None),
    )
    out_specs = (
        P("fsdp", "ctx", None),
        P("fsdp", "ctx", None),
        P("fsdp"),
        P("fsdp"),
        P("fsdp", None, "tp"),
        P(None, "fsdp"),
        P("tp", "fsdp"),
        P("fsdp"),
        P("fsdp"),
        P("fsdp"),
        P("fsdp", "tp"),
        P("fsdp"),
        P("tp", "fsdp"),
        P("fsdp"),
    )
    return jax.shard_map(local, mesh=mesh, in_specs=in_specs, out_specs=out_specs, check_vma=False)
```

```python
import functools
import types

import jax
import jax.numpy as jnp
from jax import lax
from jax.experimental import pallas as pl
from jax.experimental.pallas import tpu as pltpu
from jax.sharding import PartitionSpec as P

HD = 64
epsilon = 1e-06
f32 = jnp.float32
bf16 = jnp.bfloat16
PACK = 16
CHUNK = 512
LATE = "late"
ORDER = (
    "u0", "ffn", "da2", "ub1", "db2", "da", "back", "normed", "ub2", "da", "db", "ua1", "t0", "outputs", "ub", "db",
    "ua2", "kv1", "relay", "grad_down", "ua", "kv2", "qo1", "ub", "assemble", "qo2", "kv", "ua", "split", "qo", "kv",
    "qo", "small", "grad_up", "finish",
)


def bits_of(n):
    out, bit = [], 1
    while bit < n:
        out.append(bit)
        bit *= 2
    return out


def bitrev(n):
    order = [0]
    for bit in reversed(bits_of(n)):
        order = order + [j | bit for j in order]
    return order


def place(x, n):
    bits = len(bits_of(n))
    out = 0
    for k in range(bits):
        out = out + ((x >> k) & 1) * (1 << (bits - 1 - k))
    return out


def swap(x, axis, bit):
    return lax.ppermute(x, axis, [(i, i ^ bit) for i in range(lax.axis_size(axis))])


def gather(pieces, axis):
    for bit in reversed(bits_of(lax.axis_size(axis) // len(pieces))):
        pieces = pieces + [swap(p, axis, bit) for p in pieces]
    return pieces


def first_swap(piece, axis):
    return swap(piece, axis, bits_of(lax.axis_size(axis))[-1])


class ShardSum:
    def __init__(self, run):
        self.run, self.n, self.first, self.got = run, lax.axis_size("fsdp"), None, [[], []]

    def start(self):
        (x,) = self.run(self.n // 2, self.n, None, [], 0, None)
        self.first = swap(x, "fsdp", 1)

    def start_by_pieces(self):
        for piece in range(2):
            self.send(self.begin(piece), piece)

    def level(self, piece):
        return len(self.got[piece]) + (self.first is not None)

    def begin(self, piece):
        level = self.level(piece)
        n = self.n >> level
        return self.run(n // 2, n, self.first, self.got[piece], level, piece)

    def send(self, blocks, piece):
        level = self.level(piece)
        self.got[piece].append([swap(x, "fsdp", 1 << level) for x in blocks])

    def own(self, piece):
        return self.run(0, 1, self.first, self.got[piece], self.level(piece), piece)[0]


def tie(*trees):
    flat, where = jax.tree.flatten(trees)
    return jax.tree.unflatten(where, lax.optimization_barrier(flat))


class Line:
    def __init__(self, x, idx, clock):
        assert lax.axis_size("ctx") == 4
        self.held, self.idx, self.clock, self.step = x, idx, clock, 0
        self.got = self.send()

    def send(self):
        pairs = ([(0, 1), (3, 2)], [(1, 2), (2, 1)], [(1, 0), (2, 3)])[self.step]
        return lax.ppermute(self.held, "ctx", pairs)

    def advance(self, name):
        self.step += 1
        out = [jax.ShapeDtypeStruct(self.held.shape, bf16)]
        args, name = [self.idx, self.held, self.got], f"{name}_{self.step}"
        (self.held,) = call(add_kernel, out, args, clock=self.clock, name=name)
        self.got = self.send()

    def ends(self):
        return [self.held, self.got]


NN = (((1,), (0,)), ((), ()))
NT = (((1,), (1,)), ((), ()))
TN = (((0,), (0,)), ((), ()))


def mm(a, b, dims=NN):
    return lax.dot_general(a, b, dims, preferred_element_type=f32)


def call(kernel, outs, args, scratch=(), mib=12, far=(), clock=None, name=None):
    vm = pl.BlockSpec(memory_space=pltpu.VMEM)
    near = len(args)
    last = [] if clock is None else [x for x in clock if x is not LATE]
    late = clock is not None and any(x is LATE for x in clock)
    args = [*args, *far, *last]
    count = len(args) - len(last)

    def body(*refs):
        kernel(*refs[:count], *refs[count + len(last) :])

    results = pl.pallas_call(
        body,
        out_shape=outs,
        in_specs=[pl.BlockSpec(memory_space=pltpu.SMEM)]
        + [vm] * (near - 1)
        + [pl.BlockSpec(memory_space=pl.ANY)] * (len(far) + len(last)),
        out_specs=[vm] * len(outs),
        scratch_shapes=list(scratch),
        compiler_params=pltpu.CompilerParams(vmem_limit_bytes=mib << 20),
        cost_estimate=pl.CostEstimate(flops=int(3e10) if late else 0, bytes_accessed=0, transcendentals=0),
        name=name,
    )(*args)
    if clock is not None:
        clock[:] = [results[-1], LATE] if late else [results[-1]]
    return results


def rows_of(small, r):
    return jnp.concatenate([small[p].astype(f32)[r : r + 1] for p in range(small.shape[0])], axis=1)


def live_rows(idx, s, n):
    return (idx[1] ^ s) * n + lax.broadcasted_iota(jnp.int32, (n, 1), 0) < idx[3]


def live_keys(idx, nc, n):
    col = lax.broadcasted_iota(jnp.int32, (1, nc * n), 1)
    slot = col
    for s in range(nc):
        slot = jnp.where((col >= s * n) & (col < (s + 1) * n), slot + ((idx[1] ^ s) - s) * n, slot)
    return slot < idx[3]


def to_relative(idx, x, box):
    nf, _, block = box.shape
    for b in range(nf):
        box[place(idx[0] ^ b, nf)] = x[:, b * block : (b + 1) * block]
    return jnp.concatenate([box[p] for p in range(nf)], axis=1)


def from_relative(idx, x, box):
    nf, _, block = box.shape
    for p in range(nf):
        box[p] = x[:, p * block : (p + 1) * block]
    return jnp.concatenate([box[place(idx[0] ^ b, nf)] for b in range(nf)], axis=1)


def mean(x):
    return jnp.mean(x, axis=-1, keepdims=True)


def normalize(x):
    center = x - mean(x)
    rate = lax.rsqrt(mean(center * center) + epsilon)
    return center * rate, rate


def norm_back(grad, gain, unit, rate):
    e = grad * gain
    return rate * (e - mean(e) - unit * mean(e * unit))


def softmax_of(q, k, keep, scale):
    scores = jnp.where(keep, mm(q, k, NT) * scale, -1e30)
    expo = jnp.exp(scores - jnp.max(scores, axis=-1, keepdims=True))
    return expo * (1.0 / jnp.sum(expo, axis=-1, keepdims=True))


def sides(n):
    lane = lax.broadcasted_iota(jnp.int32, (1, n), 1)
    return [(lane >= h * HD) & (lane < (h + 1) * HD) for h in range(n // HD)]


def only(keep, x):
    return jnp.where(keep, x.astype(f32), 0.0).astype(x.dtype)


def merge(keeps, parts):
    out = parts[0]
    for keep, part in zip(keeps[1:], parts[1:]):
        out = jnp.where(keep, part, out)
    return out


def fold(x, block, width):
    k = width // block
    rows = x.shape[0] // k
    return jnp.concatenate([x[i * rows : (i + 1) * rows] for i in range(k)], axis=1)


def unfold(x, block):
    return jnp.concatenate([x[:, i * block : (i + 1) * block] for i in range(x.shape[1] // block)], axis=0)


def pack_kernel(_, wo, *refs):
    *vectors, qv, up, out = refs
    block = qv.shape[1]
    out[:block] = fold(wo[...], block, out.shape[1])
    lines = [x[...].astype(f32).reshape(1, block) for x in vectors] + [qv[...].astype(f32), up[...].astype(f32)]
    lines.append(jnp.zeros((PACK - 8 - up.shape[0], block), f32))
    out[block:, :block] = jnp.concatenate(lines, axis=0).astype(bf16)
    out[block:, block:] = jnp.zeros((PACK, out.shape[1] - block), bf16)


def attend_kernel(nc, nf, nt, n_up, *refs):
    idx, refs = refs[0], refs[1:]
    sources = refs[: nc + 2 * nf]
    masked, unit1, rate1, normed, q, k, v, mixed, *branch, up_shift, small, box, tok_all, w_all, aux_all, sems = refs[
        nc + 2 * nf :
    ]
    toks = [tok_all.at[s] for s in range(nc)]
    wq, aux = [w_all.at[p] for p in range(nf)], [aux_all.at[p] for p in range(nf)]
    places = [*toks, *wq, *aux]
    order = [*range(nc), *range(nc + nf, nc + 2 * nf), *range(nc, nc + nf)]
    copies = {i: pltpu.make_async_copy(sources[i], places[i], sems.at[i]) for i in order}
    for i in order:
        copies[i].start()
    for i in order[: nc + nf]:
        copies[i].wait()
    n = toks[0].shape[0]
    block = small.shape[2]
    for p in range(nf):
        small[p] = aux[p][block:, :block]
    hc = q.shape[1]
    gain, shift = rows_of(small, 0), rows_of(small, 1)
    for s in range(nc):
        here = slice(s * n, (s + 1) * n)
        x = jnp.where(live_rows(idx, s, n), toks[s][...].astype(f32), 0.0)
        x = to_relative(idx, x, box)
        masked[here, :] = x.astype(bf16)
        unit, rate = normalize(x)
        unit1[here, :] = unit
        rate1[here, :] = jnp.broadcast_to(rate, (n, 128))
        normed[here, :] = (unit * gain + shift).astype(bf16)
    shifts = []
    for i in range(nf // nt):
        mine = small[place(idx[0] ^ (idx[2] * (nf // nt) + i), nf)].astype(f32)
        shifts.append((mine[6:7], mine[7:8]))
        for r in range(n_up):
            up_shift[:, (i * n_up + r) * block : (i * n_up + r + 1) * block] = mine[8 + r : 9 + r]
    q_shift = jnp.concatenate([a for a, _ in shifts], axis=1)
    v_shift = jnp.concatenate([b for _, b in shifts], axis=1)
    for i in order[nc + nf :]:
        copies[i].wait()
    for j, (out, bias) in enumerate(((q, q_shift), (k, None), (v, v_shift))):
        acc = mm(normed[:, :block], wq[0][j * block : (j + 1) * block])
        for p in range(1, nf):
            acc = acc + mm(normed[:, p * block : (p + 1) * block], wq[p][j * block : (j + 1) * block])
        out[...] = (acc if bias is None else acc + bias).astype(bf16)
    keep = live_keys(idx, nc, n)
    halves = sides(128)

    def pair(i, _):
        at = pl.ds(pl.multiple_of(i * 128, 128), 128)
        qp, kp, vp = q[:, at], k[:, at], v[:, at]
        parts = [mm(softmax_of(only(h, qp), kp, keep, HD**-0.5).astype(bf16), vp) for h in halves]
        mixed[:, at] = merge(halves, parts).astype(bf16)
        return 0

    lax.fori_loop(0, hc // 128, pair, 0)
    for p in range(nf):
        out_w = unfold(aux[p][:block], block)
        for h, out in enumerate(branch):
            part = mixed[h * out.shape[0] : (h + 1) * out.shape[0]]
            out[:, p * block : (p + 1) * block] = mm(part, out_w).astype(bf16)


def up_kernel(nc, nf, *refs):
    idx, masked, own_a, own_b, got_a, got_b, small, up_shift = refs[:8]
    wu = refs[8 : 8 + nf]
    middle, unit2, rate2, normed2, active, slope = refs[8 + nf :]
    n = masked.shape[0] // nc
    block = small.shape[2]
    gain, shift, bias = rows_of(small, 2), rows_of(small, 3), rows_of(small, 4)
    for s in range(nc):
        here = slice(s * n, (s + 1) * n)
        own, got = (own_a, got_a) if s < nc // 2 else (own_b, got_b)
        part = slice(s % (nc // 2) * n, (s % (nc // 2) + 1) * n)
        x = masked[here, :].astype(f32) + (own[part, :].astype(f32) + got[part, :].astype(f32) + bias)
        middle[here, :] = x
        unit, rate = normalize(x)
        unit2[here, :] = unit
        rate2[here, :] = jnp.broadcast_to(rate, (n, 128))
        normed2[here, :] = (unit * gain + shift).astype(bf16)
    chunk = min(CHUNK, active.shape[1])

    def step(i, _):
        at = pl.ds(pl.multiple_of(i * chunk, chunk), chunk)
        acc = mm(normed2[:, :block], wu[0][:, at])
        for p in range(1, nf):
            acc = acc + mm(normed2[:, p * block : (p + 1) * block], wu[p][:, at])
        x = acc + up_shift[:, at]
        root = 0.7978845608028654
        tanh = jnp.tanh(root * (x + 0.044715 * (x * x * x)))
        half = 0.5 * (1.0 + tanh)
        active[:, at] = (x * half).astype(bf16)
        slope[:, at] = half + 0.5 * x * (1.0 - tanh * tanh) * (root * (1.0 + 3 * 0.044715 * (x * x)))
        return 0

    lax.fori_loop(0, active.shape[1] // chunk, step, 0)


def cotangent_kernel(idx, own, near, far, gl, box):
    n = own.shape[0]
    for s, x in enumerate((own, near.at[0], far.at[0], far.at[1])):
        c = jnp.where(live_rows(idx, s, n), x[...].astype(f32), 0.0)
        gl[s * n : (s + 1) * n, :] = to_relative(idx, c, box).astype(bf16)


def hidden_back_kernel(nf, *refs):
    _, gl, slope = refs[:3]
    wd, wu = refs[3 : 3 + nf], refs[3 + nf : 3 + 2 * nf]
    gh, gnt, gh_sum, acc = refs[3 + 2 * nf :]
    block = wd[0].shape[1]
    chunk = min(CHUNK, gh.shape[1])
    acc[...] = jnp.zeros_like(acc)

    def step(i, _):
        at = pl.ds(pl.multiple_of(i * chunk, chunk), chunk)
        ga = mm(gl[:, :block], wd[0][at, :], NT)
        for p in range(1, nf):
            ga = ga + mm(gl[:, p * block : (p + 1) * block], wd[p][at, :], NT)
        g = (ga * slope[:, at]).astype(bf16)
        gh[:, at] = g
        gh_sum[:, at] = jnp.sum(g.astype(f32), axis=0, keepdims=True)
        for p in range(nf):
            acc[:, p * block : (p + 1) * block] += mm(g, wu[p][:, at], NT)
        return 0

    lax.fori_loop(0, gh.shape[1] // chunk, step, 0)
    gnt[...] = acc[...].astype(bf16)


def down_kernel(nf, idx, active, *refs):
    out = refs[nf]
    block = refs[0].shape[1]
    for p in range(nf):
        out[:, p * block : (p + 1) * block] = mm(active[...], refs[p][...]).astype(bf16)


def attend_back_kernel(nc, nf, *refs):
    idx, gl, own, got, unit2, rate2, small, q, k, v = refs[:10]
    aux = refs[10 : 10 + nf]
    gmid, gb, gq, gk, gv, sums, qv_sum, gm = refs[10 + nf :]
    n = gl.shape[0] // nc
    block = small.shape[2]
    hc = q.shape[1]
    gain = rows_of(small, 2)
    totals = [0.0] * 4
    for s in range(nc):
        here = slice(s * n, (s + 1) * n)
        g = own[here, :].astype(f32) + got[here, :].astype(f32)
        u = unit2[here, :]
        c = gl[here, :].astype(f32)
        x = c + norm_back(g, gain, u, rate2[here, :1])
        gmid[here, :] = x
        low = x.astype(bf16)
        gb[here, :] = low
        for r, value in enumerate((g * u, g, low.astype(f32), c)):
            totals[r] = totals[r] + jnp.sum(value, axis=0, keepdims=True)
    sums[...] = jnp.concatenate(totals + [jnp.zeros((4, gl.shape[1]), f32)], axis=0)
    acc = mm(gb[:, :block], unfold(aux[0][:block], block), NT)
    for p in range(1, nf):
        acc = acc + mm(gb[:, p * block : (p + 1) * block], unfold(aux[p][:block], block), NT)
    gm[...] = acc.astype(bf16)
    keep = live_keys(idx, nc, n)
    halves = sides(128)
    scale = HD**-0.5

    def pair(i, _):
        at = pl.ds(pl.multiple_of(i * 128, 128), 128)
        qp, kp, vp, gp = q[:, at], k[:, at], v[:, at], gm[:, at]
        dq, dk, dv = [], [], []
        for h in halves:
            prob = softmax_of(only(h, qp), kp, keep, scale)
            grad = mm(only(h, gp), vp, NT)
            dv.append(mm(prob.astype(bf16), gp, TN))
            ds = (prob * (grad - jnp.sum(prob * grad, axis=-1, keepdims=True))).astype(bf16)
            dq.append(mm(ds, kp))
            dk.append(mm(ds, qp, TN))
        a = (merge(halves, dq) * scale).astype(bf16)
        b = merge(halves, dv).astype(bf16)
        gq[:, at] = a
        gk[:, at] = (merge(halves, dk) * scale).astype(bf16)
        gv[:, at] = b
        total = [jnp.sum(x.astype(f32), axis=0, keepdims=True) for x in (a, b)]
        qv_sum[:, at] = jnp.concatenate(total + [jnp.zeros((6, 128), f32)], axis=0)
        return 0

    lax.fori_loop(0, hc // 128, pair, 0)


def normed_back_kernel(nf, nt, n_up, idx, gq, gk, gv, unit1, sums, qv_sum, gh_sum, ffn, *refs):
    wq, (gn, cross, pack) = refs[:nf], refs[nf:]
    block = pack.shape[2]
    order = bitrev(nf)
    first = jnp.where(idx[2] == 0, 1.0, 0.0)
    held = nf // nt
    for p in range(nf):
        here = slice(p * block, (p + 1) * block)
        acc = mm(gq[...], wq[p][:block], NT) + mm(gk[...], wq[p][block : 2 * block], NT)
        acc = acc + mm(gv[...], wq[p][2 * block : 3 * block], NT)
        gn[:, here] = acc.astype(bf16)
        cross[:, here] = jnp.where(idx[2] == 0, acc, ffn[:, here].astype(f32)).astype(bf16)
        rows = [jnp.sum(acc * unit1[:, here], axis=0, keepdims=True), jnp.sum(acc, axis=0, keepdims=True)]
        rows += [sums[r : r + 1, here] * first for r in range(4)]
        which = (idx[0] ^ order[p]) - idx[2] * held

        def mine(of):
            out = jnp.zeros((1, block), f32)
            for i in range(held):
                out = jnp.where(which == i, of(i), out)
            return out

        rows += [mine(lambda i, r=r: qv_sum[r : r + 1, i * block : (i + 1) * block]) for r in range(2)]
        rows += [
            mine(lambda i, r=r: gh_sum[:, (i * n_up + r) * block : (i * n_up + r + 1) * block]) for r in range(n_up)
        ]
        rows.append(jnp.zeros((PACK - len(rows), block), f32))
        pack[p] = jnp.concatenate(rows, axis=0).astype(bf16)


def outputs_kernel(nc, idx, ffn, cross_got, middle, gn, unit1, rate1, gmid, small, stay, pass_on, go, box):
    n = gmid.shape[0] // nc
    outs = [stay, go.at[0], pass_on, go.at[1]]

    @pl.when(idx[2] == 0)
    def _():
        bias = rows_of(small, 5)
        for s in range(nc):
            here = slice(s * n, (s + 1) * n)
            x = middle[here, :] + (ffn[here, :].astype(f32) + cross_got[here, :].astype(f32) + bias)
            outs[s][...] = from_relative(idx, jnp.where(live_rows(idx, s, n), x, 0.0), box).astype(bf16)

    @pl.when(idx[2] != 0)
    def _():
        gain = rows_of(small, 0)
        for s in range(nc):
            here = slice(s * n, (s + 1) * n)
            g = gn[here, :].astype(f32) + cross_got[here, :].astype(f32)
            x = gmid[here, :] + norm_back(g, gain, unit1[here, :], rate1[here, :1])
            outs[s][...] = from_relative(idx, jnp.where(live_rows(idx, s, n), x, 0.0), box).astype(bf16)


def relay_kernel(_, own, got, out):
    out[0] = own[...]
    out[1] = got[1]


def assemble_kernel(idx, own, near, far, out):
    out[idx[1]] = own[...]
    out[idx[1] ^ 1] = near[0]
    out[idx[1] ^ 2] = far[0]
    out[idx[1] ^ 3] = far[1]


def split_kernel(idx, own, got, result, grad):
    @pl.when(idx[2] == 0)
    def _():
        result[...] = own[...]
        grad[...] = got[...].astype(f32)

    @pl.when(idx[2] != 0)
    def _():
        result[...] = got[...]
        grad[...] = own[...].astype(f32)


def shard_kernel(first, last, parts, base, block, levels, *refs):
    refs = list(refs[1:])
    mats = [refs.pop(0) for kind in parts for _ in range(1 if kind == "small" else 2)]
    early = [refs.pop(0)] if base is not None and base >= 0 else []
    gots = [[refs.pop(0) for _ in range(first, last)] for _ in range(levels)]
    outs = [refs[0].at[p] for p in range(last - first)] if base is None else refs
    for p, out in enumerate(outs):
        at, taken = 0, 0
        low = (first + p) * block
        for kind in parts:
            if kind == "small":
                x = mats[taken][first + p].astype(f32)
                x = jnp.concatenate([x, jnp.zeros((PACK, out.shape[1] - block), f32)], axis=1)
            elif kind == "out":
                x = fold(mm(mats[taken][...], mats[taken + 1][:, low : low + block], TN), block, out.shape[1])
            else:
                start = low + (block // 2 if kind == "second_half" else 0)
                size = block if kind == "all" else block // 2
                x = mm(mats[taken][:, start : start + size], mats[taken + 1][...], TN)
            size = x.shape[0]
            for got in early:
                x = x + got[first + p, base + at : base + at + size].astype(f32)
            for got in gots:
                x = x + got[p][at : at + size].astype(f32)
            out[at : at + size] = x.astype(bf16)
            at += size
            taken += 1 if kind == "small" else 2


def add_kernel(_, x, got, out):
    out[...] = (x[...].astype(f32) + got[...].astype(f32)).astype(bf16)


def picked(idx, own, got):
    return jnp.where(idx[4] == 1, got.astype(f32), own.astype(f32))


def finish_up_kernel(idx, *refs):
    out = refs[-1]
    rows = refs[0].shape[0]
    for i in range(len(refs) // 2):
        out[i * rows : (i + 1) * rows] = picked(idx, refs[2 * i][...], refs[2 * i + 1][...])


def finish_down_kernel(idx, *refs):
    out = refs[-1]
    rows = refs[0].shape[0]
    step = min(out.shape[0], 512)
    for i in range(len(refs) // 2):
        for j in range(0, out.shape[0], step):
            x = picked(idx, refs[2 * i][:, j : j + step], refs[2 * i + 1][:, j : j + step])
            out[j : j + step, i * rows : (i + 1) * rows] = x.T


def small_kernel(block, idx, own, got, out):
    out[...] = picked(idx, own[2 * block :, :block], got[2 * block :, :block]).astype(bf16)


def finish_kernel(block, idx, a, a_got, b, b_got, qkv, out_w):
    kv = picked(idx, a[: 2 * block], a_got[: 2 * block])
    qo = picked(idx, b[...], b_got[...])
    qkv[:block] = qo[:block]
    qkv[block:] = kv
    out_w[...] = unfold(qo[block:], block)


def shape(*dims, dtype=f32):
    return jax.ShapeDtypeStruct(dims, dtype)


def local(
    inputs,
    lengths,
    ln1_gain,
    ln1_bias,
    w_qkv,
    qv_bias,
    w_out,
    out_bias,
    ln2_gain,
    ln2_bias,
    w_up,
    up_bias,
    w_down,
    down_bias,
    cotangent,
):
    nf, nc, nt = (lax.axis_size(a) for a in ("fsdp", "ctx", "tp"))
    f, c, t = (lax.axis_index(a) for a in ("fsdp", "ctx", "tp"))
    images, n, width = inputs.shape
    assert images == nc == 4 and nt == 2
    rows = n * nc
    block = width // nf
    hc = w_qkv.shape[2]
    ff = w_up.shape[1]
    n_up = up_bias.shape[0] // block
    outer = (c == 0) | (c == nc - 1)
    idx = jnp.stack([f, c, t, lax.dynamic_index_in_dim(lengths, c, 0, False), outer.astype(jnp.int32)]).astype(jnp.int32)
    wide = functools.partial(shape, rows, width)

    def to_image(x):
        return [lax.dynamic_index_in_dim(x, c, 0, False)] + [
            swap(lax.dynamic_index_in_dim(x, c ^ s, 0, False), "ctx", s) for s in range(1, nc)
        ]

    clock = []

    w_proj = w_qkv.transpose(1, 0, 2).reshape(3 * block, hc)
    proj_got = first_swap(w_proj, "fsdp")
    toks = to_image(inputs)
    (packed,) = call(
        pack_kernel,
        [shape(block + PACK, hc, dtype=bf16)],
        [idx, w_out, ln1_gain, ln1_bias, ln2_gain, ln2_bias, out_bias, down_bias, qv_bias, up_bias.reshape(n_up, block)],
        name="pack",
    )
    packed_got = first_swap(packed, "fsdp")
    proj_got, packed_got, w_up_later, toks, cotangent = tie(proj_got, packed_got, w_up, toks, cotangent)
    own, pass_on = (lax.dynamic_index_in_dim(cotangent, c ^ s, 0, False) for s in (0, 2))
    near = swap(jnp.stack([lax.dynamic_index_in_dim(cotangent, c ^ s, 0, False) for s in (1, 3)]), "ctx", 1)
    wq = gather([w_proj, proj_got], "fsdp")
    aux = gather([packed, packed_got], "fsdp")
    up_got = first_swap(w_up_later, "fsdp")
    masked, unit1, rate1, normed, q, k, v, mixed, branch_a, branch_b, up_shift, small = call(
        functools.partial(attend_kernel, nc, nf, nt, n_up),
        [
            wide(dtype=bf16),
            wide(),
            shape(rows, 128),
            wide(dtype=bf16),
            *[shape(rows, hc, dtype=bf16)] * 4,
            *[shape(rows // 2, width, dtype=bf16)] * 2,
            shape(1, ff),
            shape(nf, PACK, block, dtype=bf16),
        ],
        [idx],
        [
            pltpu.VMEM((nf, n, block), f32),
            pltpu.VMEM((nc, n, width), bf16),
            pltpu.VMEM((nf, 3 * block, hc), bf16),
            pltpu.VMEM((nf, block + PACK, hc), bf16),
            pltpu.SemaphoreType.DMA((nc + 2 * nf,)),
        ],
        mib=24,
        far=[*toks, *wq, *aux],
        clock=clock,
        name="attend",
    )
    branch_a, near = tie(branch_a, near)
    got_a, got_b = swap(branch_a, "tp", 1), swap(branch_b, "tp", 1)
    got_a, up_got, w_down_later = tie(got_a, up_got, w_down)
    (relayed,) = call(relay_kernel, [shape(2, n, width, dtype=bf16)], [idx, pass_on, near], name="relay_in")
    cots = [own, near, swap(relayed, "ctx", 2)]
    wu = gather([w_up, up_got], "fsdp")
    down_got = first_swap(w_down_later, "fsdp")

    middle, unit2, rate2, normed2, active, slope = call(
        functools.partial(up_kernel, nc, nf),
        [
            wide(),
            wide(),
            shape(rows, 128),
            wide(dtype=bf16),
            shape(rows, ff, dtype=bf16),
            shape(rows, ff),
        ],
        [idx, masked, branch_a, branch_b, got_a, got_b, small, up_shift, *wu],
        clock=clock,
        name="hidden",
    )
    (gl,) = call(
        cotangent_kernel,
        [wide(dtype=bf16)],
        [idx, *cots],
        [pltpu.VMEM((nf, n, block), f32)],
        clock=clock,
        name="cotangent",
    )

    def shard_sum(names, pieces):
        kinds = {"small": PACK, "first_half": block // 2, "second_half": block // 2}
        heights = [sum(kinds.get(kind, block) for kind in parts) for parts, _ in pieces]
        width_in = ff if len(pieces[0][0]) == 1 else hc

        def run(first, last, early, got, level, piece):
            if piece is None:
                parts, mats, base = sum((p for p, _ in pieces), ()), sum((m for _, m in pieces), ()), None
                outs = [shape(last - first, sum(heights), width_in, dtype=bf16)]
            else:
                (parts, mats), base = pieces[piece], sum(heights[:piece]) if early is not None else -1
                outs = [shape(heights[piece], width_in, dtype=bf16)] * (last - first)
            return call(
                functools.partial(shard_kernel, first, last, parts, base, block, len(got)),
                outs,
                [idx, *mats, *([] if early is None else [early]), *[x for one in got for x in one[first:last]]],
                clock=clock,
                name=names[0] + "0" if piece is None else f"{names[piece + 1]}{level}",
            )

        return ShardSum(run)

    levels = len(bits_of(nf))
    first, second = ("first_half",), ("second_half",)
    down = shard_sum(("d", "da", "db"), [(first, (gl, active)), (second, (gl, active))])
    down.start_by_pieces()
    down_got, down.got = tie(down_got, down.got)
    wd = gather([w_down, down_got], "fsdp")
    part_a, part_b = down.begin(0), down.begin(1)
    slope, part_a, part_b = tie(slope, part_a, part_b)
    down.send(part_a, 0)
    down.send(part_b, 1)
    gh, gnt, gh_sum = call(
        functools.partial(hidden_back_kernel, nf),
        [shape(rows, ff, dtype=bf16), wide(dtype=bf16), shape(1, ff)],
        [idx, gl, slope, *wd, *wu],
        [pltpu.VMEM((rows, width), f32)],
        clock=clock,
        name="hidden_back",
    )
    gnt_got = swap(gnt, "tp", 1)

    o = types.SimpleNamespace(lines={})
    clock.append(LATE)

    def back():
        o.gmid, o.gb, o.gq, o.gk, o.gv, o.sums, o.qv_sum = call(
            functools.partial(attend_back_kernel, nc, nf),
            [wide(), wide(dtype=bf16), *[shape(rows, hc, dtype=bf16)] * 3, shape(8, width), shape(8, hc)],
            [idx, gl, gnt, gnt_got, unit2, rate2, small, q, k, v, *aux],
            [pltpu.VMEM((rows, hc), bf16)],
            clock=clock,
            name="back",
        )

    def normed_back():
        o.gn, o.cross, o.pack = call(
            functools.partial(normed_back_kernel, nf, nt, n_up),
            [wide(dtype=bf16), wide(dtype=bf16), shape(nf, PACK, block, dtype=bf16)],
            [idx, o.gq, o.gk, o.gv, unit1, o.sums, o.qv_sum, gh_sum, o.ffn, *wq],
            clock=clock,
            name="normed",
        )
        o.cross_got = swap(o.cross, "tp", 1)

    def outputs():
        o.stay, o.pass_on, o.go = call(
            functools.partial(outputs_kernel, nc),
            [shape(n, width, dtype=bf16), shape(n, width, dtype=bf16), shape(2, n, width, dtype=bf16)],
            [idx, o.ffn, o.cross_got, middle, o.gn, unit1, rate1, o.gmid, small],
            [pltpu.VMEM((nf, n, block), f32)],
            clock=clock,
            name="outputs",
        )
        o.near = swap(o.go, "ctx", 1)

    def relay():
        (x,) = call(relay_kernel, [shape(2, n, width, dtype=bf16)], [idx, o.pass_on, o.near], clock=clock, name="relay")
        o.far = swap(x, "ctx", 2)

    def assemble():
        out, args = [shape(nc, n, width, dtype=bf16)], [idx, o.stay, o.near, o.far]
        (o.ours,) = call(assemble_kernel, out, args, clock=clock, name="assemble")
        o.theirs = swap(o.ours, "tp", 1)

    def split():
        out = [shape(nc, n, width, dtype=bf16), shape(nc, n, width)]
        o.result, o.grad_inputs = call(split_kernel, out, [idx, o.ours, o.theirs], clock=clock, name="split")

    def finish_down():
        args = [idx, *o.lines["da"].ends(), *o.lines["db"].ends()]
        (o.grad_down,) = call(finish_down_kernel, [shape(ff, block)], args, clock=clock, name="grad_down")

    def finish_up():
        args = [idx, *o.lines["ua"].ends(), *o.lines["ub"].ends()]
        (o.grad_up,) = call(finish_up_kernel, [shape(block, ff)], args, clock=clock, name="grad_up")

    def small_sums():
        out, args = [shape(PACK, block, dtype=bf16)], [idx, *o.lines["kv"].ends()]
        (x,) = call(functools.partial(small_kernel, block), out, args, clock=clock, name="small")
        o.total = x.astype(f32) + swap(x, "tp", 1).astype(f32)

    def finish():
        o.grad_qkv, o.grad_out = call(
            functools.partial(finish_kernel, block),
            [shape(3 * block, hc), shape(hc, block)],
            [idx, *o.lines["kv"].ends(), *o.lines["qo"].ends()],
            clock=clock,
            name="finish",
        )

    def ffn_out():
        (o.ffn,) = call(functools.partial(down_kernel, nf), [wide(dtype=bf16)], [idx, active, *wd], clock=clock, name="ffn")

    def start_up():
        o.up = shard_sum(("u", "ua", "ub"), [(first, (normed2, gh)), (second, (normed2, gh))])
        o.up.start()

    def start_rest():
        kv = (("all", "all", "small"), (normed, o.gk, normed, o.gv, o.pack))
        qo = (("all", "out"), (normed, o.gq, mixed, o.gb))
        o.rest = shard_sum(("t", "kv", "qo"), [kv, qo])
        o.rest.start()

    o.down = down
    places = {"da": ("down", 0), "db": ("down", 1), "ua": ("up", 0), "ub": ("up", 1), "kv": ("rest", 0), "qo": ("rest", 1)}
    steps = {
        "back": back,
        "normed": normed_back,
        "outputs": outputs,
        "relay": relay,
        "assemble": assemble,
        "split": split,
        "grad_down": finish_down,
        "grad_up": finish_up,
        "small": small_sums,
        "finish": finish,
        "ffn": ffn_out,
        "u0": start_up,
        "t0": start_rest,
    }
    for name in ORDER:
        if name in steps:
            steps[name]()
        elif name[-1] == "1":
            which, piece = places[name[:-1]]
            one = getattr(o, which)
            one.send(one.begin(piece), piece)
        elif name[-1] == "2":
            which, piece = places[name[:-1]]
            one = getattr(o, which)
            for _ in range(2, levels):
                one.send(one.begin(piece), piece)
            o.lines[name[:-1]] = Line(one.own(piece), idx, clock)
        else:
            o.lines[name].advance(name)
    total = o.total[:]
    return (
        o.result,
        o.grad_inputs,
        total[0],
        total[1],
        o.grad_qkv.reshape(3, block, hc).transpose(1, 0, 2),
        total[6:8],
        o.grad_out,
        total[4],
        total[2],
        total[3],
        o.grad_up,
        total[8 : 8 + n_up].reshape(-1),
        o.grad_down,
        total[5],
    )


def solution(mesh):
    in_specs = (
        P("fsdp", "ctx", None),
        P("fsdp"),
        P("fsdp"),
        P("fsdp"),
        P("fsdp", None, "tp"),
        P(None, "fsdp"),
        P("tp", "fsdp"),
        P("fsdp"),
        P("fsdp"),
        P("fsdp"),
        P("fsdp", "tp"),
        P("fsdp"),
        P("tp", "fsdp"),
        P("fsdp"),
        P("fsdp", "ctx", None),
    )
    out_specs = (
        P("fsdp", "ctx", None),
        P("fsdp", "ctx", None),
        P("fsdp"),
        P("fsdp"),
        P("fsdp", None, "tp"),
        P(None, "fsdp"),
        P("tp", "fsdp"),
        P("fsdp"),
        P("fsdp"),
        P("fsdp"),
        P("fsdp", "tp"),
        P("fsdp"),
        P("tp", "fsdp"),
        P("fsdp"),
    )
    return jax.shard_map(local, mesh=mesh, in_specs=in_specs, out_specs=out_specs, check_vma=False)
```

```python
import functools
import types

import jax
import jax.numpy as jnp
from jax import lax
from jax.experimental import pallas as pl
from jax.experimental.pallas import tpu as pltpu
from jax.sharding import PartitionSpec as P

HD = 64
epsilon = 1e-06
f32 = jnp.float32
bf16 = jnp.bfloat16
PACK = 16
CHUNK = 512
LATE = "late"
ORDER = (
    "u0", "da2", "ub1", "ffn", "back", "da", "db2", "normed", "ub2", "ua1", "da", "db", "outputs", "ua2",
    "ub", "db", "t0", "relay", "kv1", "grad_down", "ua", "qo1", "kv2", "ub", "assemble", "qo2", "kv", "ua",
    "split", "qo", "kv", "qo", "small", "grad_up", "finish",
)


def bits_of(n):
    out, bit = [], 1
    while bit < n:
        out.append(bit)
        bit *= 2
    return out


def bitrev(n):
    order = [0]
    for bit in reversed(bits_of(n)):
        order = order + [j | bit for j in order]
    return order


def place(x, n):
    bits = len(bits_of(n))
    out = 0
    for k in range(bits):
        out = out + ((x >> k) & 1) * (1 << (bits - 1 - k))
    return out


def swap(x, axis, bit):
    return lax.ppermute(x, axis, [(i, i ^ bit) for i in range(lax.axis_size(axis))])


def gather(pieces, axis):
    for bit in reversed(bits_of(lax.axis_size(axis) // len(pieces))):
        pieces = pieces + [swap(p, axis, bit) for p in pieces]
    return pieces


def first_swap(piece, axis):
    return swap(piece, axis, bits_of(lax.axis_size(axis))[-1])


class ShardSum:
    def __init__(self, run):
        self.run, self.n, self.first, self.got = run, lax.axis_size("fsdp"), None, [[], []]

    def start(self):
        (x,) = self.run(self.n // 2, self.n, None, [], 0, None)
        self.first = swap(x, "fsdp", 1)

    def start_by_pieces(self):
        for piece in range(2):
            self.send(self.begin(piece), piece)

    def level(self, piece):
        return len(self.got[piece]) + (self.first is not None)

    def begin(self, piece):
        level = self.level(piece)
        n = self.n >> level
        return self.run(n // 2, n, self.first, self.got[piece], level, piece)

    def send(self, blocks, piece):
        level = self.level(piece)
        self.got[piece].append([swap(x, "fsdp", 1 << level) for x in blocks])

    def own(self, piece):
        return self.run(0, 1, self.first, self.got[piece], self.level(piece), piece)[0]


def tie(*trees):
    flat, where = jax.tree.flatten(trees)
    return jax.tree.unflatten(where, lax.optimization_barrier(flat))


class Line:
    def __init__(self, x, idx, clock):
        assert lax.axis_size("ctx") == 4
        self.held, self.idx, self.clock, self.step = x, idx, clock, 0
        self.got = self.send()

    def send(self):
        pairs = ([(0, 1), (3, 2)], [(1, 2), (2, 1)], [(1, 0), (2, 3)])[self.step]
        return lax.ppermute(self.held, "ctx", pairs)

    def advance(self, name):
        self.step += 1
        out = [jax.ShapeDtypeStruct(self.held.shape, bf16)]
        args, name = [self.idx, self.held, self.got], f"{name}_{self.step}"
        (self.held,) = call(add_kernel, out, args, clock=self.clock, name=name)
        self.got = self.send()

    def ends(self):
        return [self.held, self.got]


NN = (((1,), (0,)), ((), ()))
NT = (((1,), (1,)), ((), ()))
TN = (((0,), (0,)), ((), ()))


def mm(a, b, dims=NN):
    return lax.dot_general(a, b, dims, preferred_element_type=f32)


def call(kernel, outs, args, scratch=(), mib=12, far=(), clock=None, name=None):
    vm = pl.BlockSpec(memory_space=pltpu.VMEM)
    near = len(args)
    last = [] if clock is None else [x for x in clock if x is not LATE]
    late = clock is not None and any(x is LATE for x in clock)
    args = [*args, *far, *last]
    count = len(args) - len(last)

    def body(*refs):
        kernel(*refs[:count], *refs[count + len(last) :])

    results = pl.pallas_call(
        body,
        out_shape=outs,
        in_specs=[pl.BlockSpec(memory_space=pltpu.SMEM)]
        + [vm] * (near - 1)
        + [pl.BlockSpec(memory_space=pl.ANY)] * (len(far) + len(last)),
        out_specs=[vm] * len(outs),
        scratch_shapes=list(scratch),
        compiler_params=pltpu.CompilerParams(vmem_limit_bytes=mib << 20),
        cost_estimate=pl.CostEstimate(flops=int(3e10) if late else 0, bytes_accessed=0, transcendentals=0),
        name=name,
    )(*args)
    if clock is not None:
        clock[:] = [results[-1], LATE] if late else [results[-1]]
    return results


def rows_of(small, r):
    return jnp.concatenate([small[p].astype(f32)[r : r + 1] for p in range(small.shape[0])], axis=1)


def live_rows(idx, s, n):
    return (idx[1] ^ s) * n + lax.broadcasted_iota(jnp.int32, (n, 1), 0) < idx[3]


def live_keys(idx, nc, n):
    col = lax.broadcasted_iota(jnp.int32, (1, nc * n), 1)
    slot = col
    for s in range(nc):
        slot = jnp.where((col >= s * n) & (col < (s + 1) * n), slot + ((idx[1] ^ s) - s) * n, slot)
    return slot < idx[3]


def to_relative(idx, x, box):
    nf, _, block = box.shape
    for b in range(nf):
        box[place(idx[0] ^ b, nf)] = x[:, b * block : (b + 1) * block]
    return jnp.concatenate([box[p] for p in range(nf)], axis=1)


def from_relative(idx, x, box):
    nf, _, block = box.shape
    for p in range(nf):
        box[p] = x[:, p * block : (p + 1) * block]
    return jnp.concatenate([box[place(idx[0] ^ b, nf)] for b in range(nf)], axis=1)


def mean(x):
    return jnp.mean(x, axis=-1, keepdims=True)


def normalize(x):
    center = x - mean(x)
    rate = lax.rsqrt(mean(center * center) + epsilon)
    return center * rate, rate


def norm_back(grad, gain, unit, rate):
    e = grad * gain
    return rate * (e - mean(e) - unit * mean(e * unit))


def softmax_of(q, k, keep, scale):
    scores = jnp.where(keep, mm(q, k, NT) * scale, -1e30)
    expo = jnp.exp(scores - jnp.max(scores, axis=-1, keepdims=True))
    return expo * (1.0 / jnp.sum(expo, axis=-1, keepdims=True))


def sides(n):
    lane = lax.broadcasted_iota(jnp.int32, (1, n), 1)
    return [(lane >= h * HD) & (lane < (h + 1) * HD) for h in range(n // HD)]


def only(keep, x):
    return jnp.where(keep, x.astype(f32), 0.0).astype(x.dtype)


def merge(keeps, parts):
    out = parts[0]
    for keep, part in zip(keeps[1:], parts[1:]):
        out = jnp.where(keep, part, out)
    return out


def fold(x, block, width):
    k = width // block
    rows = x.shape[0] // k
    return jnp.concatenate([x[i * rows : (i + 1) * rows] for i in range(k)], axis=1)


def unfold(x, block):
    return jnp.concatenate([x[:, i * block : (i + 1) * block] for i in range(x.shape[1] // block)], axis=0)


def pack_kernel(_, wo, *refs):
    *vectors, qv, up, out = refs
    block = qv.shape[1]
    out[:block] = fold(wo[...], block, out.shape[1])
    lines = [x[...].astype(f32).reshape(1, block) for x in vectors] + [qv[...].astype(f32), up[...].astype(f32)]
    lines.append(jnp.zeros((PACK - 8 - up.shape[0], block), f32))
    out[block:, :block] = jnp.concatenate(lines, axis=0).astype(bf16)
    out[block:, block:] = jnp.zeros((PACK, out.shape[1] - block), bf16)


def attend_kernel(nc, nf, nt, n_up, *refs):
    idx, refs = refs[0], refs[1:]
    sources = refs[: nc + 2 * nf]
    masked, unit1, rate1, normed, q, k, v, mixed, *branch, up_shift, small, box, tok_all, w_all, aux_all, sems = refs[
        nc + 2 * nf :
    ]
    toks = [tok_all.at[s] for s in range(nc)]
    wq, aux = [w_all.at[p] for p in range(nf)], [aux_all.at[p] for p in range(nf)]
    places = [*toks, *wq, *aux]
    order = [*range(nc), *range(nc + nf, nc + 2 * nf), *range(nc, nc + nf)]
    copies = {i: pltpu.make_async_copy(sources[i], places[i], sems.at[i]) for i in order}
    for i in order:
        copies[i].start()
    for i in order[: nc + nf]:
        copies[i].wait()
    n = toks[0].shape[0]
    block = small.shape[2]
    for p in range(nf):
        small[p] = aux[p][block:, :block]
    hc = q.shape[1]
    gain, shift = rows_of(small, 0), rows_of(small, 1)
    for s in range(nc):
        here = slice(s * n, (s + 1) * n)
        x = jnp.where(live_rows(idx, s, n), toks[s][...].astype(f32), 0.0)
        x = to_relative(idx, x, box)
        masked[here, :] = x.astype(bf16)
        unit, rate = normalize(x)
        unit1[here, :] = unit
        rate1[here, :] = jnp.broadcast_to(rate, (n, 128))
        normed[here, :] = (unit * gain + shift).astype(bf16)
    shifts = []
    for i in range(nf // nt):
        mine = small[place(idx[0] ^ (idx[2] * (nf // nt) + i), nf)].astype(f32)
        shifts.append((mine[6:7], mine[7:8]))
        for r in range(n_up):
            up_shift[:, (i * n_up + r) * block : (i * n_up + r + 1) * block] = mine[8 + r : 9 + r]
    q_shift = jnp.concatenate([a for a, _ in shifts], axis=1)
    v_shift = jnp.concatenate([b for _, b in shifts], axis=1)
    for i in order[nc + nf :]:
        copies[i].wait()
    for j, (out, bias) in enumerate(((q, q_shift), (k, None), (v, v_shift))):
        acc = mm(normed[:, :block], wq[0][j * block : (j + 1) * block])
        for p in range(1, nf):
            acc = acc + mm(normed[:, p * block : (p + 1) * block], wq[p][j * block : (j + 1) * block])
        out[...] = (acc if bias is None else acc + bias).astype(bf16)
    keep = live_keys(idx, nc, n)
    halves = sides(128)

    def pair(i, _):
        at = pl.ds(pl.multiple_of(i * 128, 128), 128)
        qp, kp, vp = q[:, at], k[:, at], v[:, at]
        parts = [mm(softmax_of(only(h, qp), kp, keep, HD**-0.5).astype(bf16), vp) for h in halves]
        mixed[:, at] = merge(halves, parts).astype(bf16)
        return 0

    lax.fori_loop(0, hc // 128, pair, 0, unroll=True)
    for p in range(nf):
        out_w = unfold(aux[p][:block], block)
        for h, out in enumerate(branch):
            part = mixed[h * out.shape[0] : (h + 1) * out.shape[0]]
            out[:, p * block : (p + 1) * block] = mm(part, out_w).astype(bf16)


def up_kernel(nc, nf, *refs):
    idx, masked, own_a, own_b, got_a, got_b, small, up_shift = refs[:8]
    wu = refs[8 : 8 + nf]
    middle, unit2, rate2, normed2, active, slope = refs[8 + nf :]
    n = masked.shape[0] // nc
    block = small.shape[2]
    gain, shift, bias = rows_of(small, 2), rows_of(small, 3), rows_of(small, 4)
    for s in range(nc):
        here = slice(s * n, (s + 1) * n)
        own, got = (own_a, got_a) if s < nc // 2 else (own_b, got_b)
        part = slice(s % (nc // 2) * n, (s % (nc // 2) + 1) * n)
        x = masked[here, :].astype(f32) + (own[part, :].astype(f32) + got[part, :].astype(f32) + bias)
        middle[here, :] = x
        unit, rate = normalize(x)
        unit2[here, :] = unit
        rate2[here, :] = jnp.broadcast_to(rate, (n, 128))
        normed2[here, :] = (unit * gain + shift).astype(bf16)
    chunk = min(CHUNK, active.shape[1])

    def step(i, _):
        at = pl.ds(pl.multiple_of(i * chunk, chunk), chunk)
        acc = mm(normed2[:, :block], wu[0][:, at])
        for p in range(1, nf):
            acc = acc + mm(normed2[:, p * block : (p + 1) * block], wu[p][:, at])
        x = acc + up_shift[:, at]
        root = 0.7978845608028654
        tanh = jnp.tanh(root * (x + 0.044715 * (x * x * x)))
        half = 0.5 * (1.0 + tanh)
        active[:, at] = (x * half).astype(bf16)
        slope[:, at] = half + 0.5 * x * (1.0 - tanh * tanh) * (root * (1.0 + 3 * 0.044715 * (x * x)))
        return 0

    lax.fori_loop(0, active.shape[1] // chunk, step, 0)


def cotangent_kernel(idx, own, near, far, gl, box):
    n = own.shape[0]
    for s, x in enumerate((own, near.at[0], far.at[0], far.at[1])):
        c = jnp.where(live_rows(idx, s, n), x[...].astype(f32), 0.0)
        gl[s * n : (s + 1) * n, :] = to_relative(idx, c, box).astype(bf16)


def hidden_back_kernel(nf, *refs):
    _, gl, slope = refs[:3]
    wd, wu = refs[3 : 3 + nf], refs[3 + nf : 3 + 2 * nf]
    gh, gnt, gh_sum, acc = refs[3 + 2 * nf :]
    block = wd[0].shape[1]
    chunk = min(CHUNK, gh.shape[1])
    acc[...] = jnp.zeros_like(acc)

    def step(i, _):
        at = pl.ds(pl.multiple_of(i * chunk, chunk), chunk)
        ga = mm(gl[:, :block], wd[0][at, :], NT)
        for p in range(1, nf):
            ga = ga + mm(gl[:, p * block : (p + 1) * block], wd[p][at, :], NT)
        g = (ga * slope[:, at]).astype(bf16)
        gh[:, at] = g
        gh_sum[:, at] = jnp.sum(g.astype(f32), axis=0, keepdims=True)
        for p in range(nf):
            acc[:, p * block : (p + 1) * block] += mm(g, wu[p][:, at], NT)
        return 0

    lax.fori_loop(0, gh.shape[1] // chunk, step, 0)
    gnt[...] = acc[...].astype(bf16)


def down_kernel(nf, idx, active, *refs):
    out = refs[nf]
    block = refs[0].shape[1]
    for p in range(nf):
        out[:, p * block : (p + 1) * block] = mm(active[...], refs[p][...]).astype(bf16)


def attend_back_kernel(nc, nf, *refs):
    idx, gl, own, got, unit2, rate2, small, q, k, v = refs[:10]
    aux = refs[10 : 10 + nf]
    gmid, gb, gq, gk, gv, sums, qv_sum, gm = refs[10 + nf :]
    n = gl.shape[0] // nc
    block = small.shape[2]
    hc = q.shape[1]
    gain = rows_of(small, 2)
    totals = [0.0] * 4
    for s in range(nc):
        here = slice(s * n, (s + 1) * n)
        g = own[here, :].astype(f32) + got[here, :].astype(f32)
        u = unit2[here, :]
        c = gl[here, :].astype(f32)
        x = c + norm_back(g, gain, u, rate2[here, :1])
        gmid[here, :] = x
        low = x.astype(bf16)
        gb[here, :] = low
        for r, value in enumerate((g * u, g, low.astype(f32), c)):
            totals[r] = totals[r] + jnp.sum(value, axis=0, keepdims=True)
    sums[...] = jnp.concatenate(totals + [jnp.zeros((4, gl.shape[1]), f32)], axis=0)
    acc = mm(gb[:, :block], unfold(aux[0][:block], block), NT)
    for p in range(1, nf):
        acc = acc + mm(gb[:, p * block : (p + 1) * block], unfold(aux[p][:block], block), NT)
    gm[...] = acc.astype(bf16)
    keep = live_keys(idx, nc, n)
    halves = sides(128)
    scale = HD**-0.5

    def pair(i, _):
        at = pl.ds(pl.multiple_of(i * 128, 128), 128)
        qp, kp, vp, gp = q[:, at], k[:, at], v[:, at], gm[:, at]
        dq, dk, dv = [], [], []
        for h in halves:
            prob = softmax_of(only(h, qp), kp, keep, scale)
            grad = mm(only(h, gp), vp, NT)
            dv.append(mm(prob.astype(bf16), gp, TN))
            ds = (prob * (grad - jnp.sum(prob * grad, axis=-1, keepdims=True))).astype(bf16)
            dq.append(mm(ds, kp))
            dk.append(mm(ds, qp, TN))
        a = (merge(halves, dq) * scale).astype(bf16)
        b = merge(halves, dv).astype(bf16)
        gq[:, at] = a
        gk[:, at] = (merge(halves, dk) * scale).astype(bf16)
        gv[:, at] = b
        total = [jnp.sum(x.astype(f32), axis=0, keepdims=True) for x in (a, b)]
        qv_sum[:, at] = jnp.concatenate(total + [jnp.zeros((6, 128), f32)], axis=0)
        return 0

    lax.fori_loop(0, hc // 128, pair, 0, unroll=True)


def normed_back_kernel(nf, nt, n_up, idx, gq, gk, gv, unit1, sums, qv_sum, gh_sum, ffn, *refs):
    wq, (gn, cross, pack) = refs[:nf], refs[nf:]
    block = pack.shape[2]
    order = bitrev(nf)
    first = jnp.where(idx[2] == 0, 1.0, 0.0)
    held = nf // nt
    for p in range(nf):
        here = slice(p * block, (p + 1) * block)
        acc = mm(gq[...], wq[p][:block], NT) + mm(gk[...], wq[p][block : 2 * block], NT)
        acc = acc + mm(gv[...], wq[p][2 * block : 3 * block], NT)
        gn[:, here] = acc.astype(bf16)
        cross[:, here] = jnp.where(idx[2] == 0, acc, ffn[:, here].astype(f32)).astype(bf16)
        rows = [jnp.sum(acc * unit1[:, here], axis=0, keepdims=True), jnp.sum(acc, axis=0, keepdims=True)]
        rows += [sums[r : r + 1, here] * first for r in range(4)]
        which = (idx[0] ^ order[p]) - idx[2] * held

        def mine(of):
            out = jnp.zeros((1, block), f32)
            for i in range(held):
                out = jnp.where(which == i, of(i), out)
            return out

        rows += [mine(lambda i, r=r: qv_sum[r : r + 1, i * block : (i + 1) * block]) for r in range(2)]
        rows += [
            mine(lambda i, r=r: gh_sum[:, (i * n_up + r) * block : (i * n_up + r + 1) * block]) for r in range(n_up)
        ]
        rows.append(jnp.zeros((PACK - len(rows), block), f32))
        pack[p] = jnp.concatenate(rows, axis=0).astype(bf16)


def outputs_kernel(nc, idx, ffn, cross_got, middle, gn, unit1, rate1, gmid, small, stay, pass_on, go, box):
    n = gmid.shape[0] // nc
    outs = [stay, go.at[0], pass_on, go.at[1]]

    @pl.when(idx[2] == 0)
    def _():
        bias = rows_of(small, 5)
        for s in range(nc):
            here = slice(s * n, (s + 1) * n)
            x = middle[here, :] + (ffn[here, :].astype(f32) + cross_got[here, :].astype(f32) + bias)
            outs[s][...] = from_relative(idx, jnp.where(live_rows(idx, s, n), x, 0.0), box).astype(bf16)

    @pl.when(idx[2] != 0)
    def _():
        gain = rows_of(small, 0)
        for s in range(nc):
            here = slice(s * n, (s + 1) * n)
            g = gn[here, :].astype(f32) + cross_got[here, :].astype(f32)
            x = gmid[here, :] + norm_back(g, gain, unit1[here, :], rate1[here, :1])
            outs[s][...] = from_relative(idx, jnp.where(live_rows(idx, s, n), x, 0.0), box).astype(bf16)


def relay_kernel(_, own, got, out):
    out[0] = own[...]
    out[1] = got[1]


def assemble_kernel(idx, own, near, far, out):
    out[idx[1]] = own[...]
    out[idx[1] ^ 1] = near[0]
    out[idx[1] ^ 2] = far[0]
    out[idx[1] ^ 3] = far[1]


def split_kernel(idx, own, got, result, grad):
    @pl.when(idx[2] == 0)
    def _():
        result[...] = own[...]
        grad[...] = got[...].astype(f32)

    @pl.when(idx[2] != 0)
    def _():
        result[...] = got[...]
        grad[...] = own[...].astype(f32)


def shard_kernel(first, last, parts, base, block, levels, *refs):
    refs = list(refs[1:])
    mats = [refs.pop(0) for kind in parts for _ in range(1 if kind == "small" else 2)]
    early = [refs.pop(0)] if base is not None and base >= 0 else []
    gots = [[refs.pop(0) for _ in range(first, last)] for _ in range(levels)]
    outs = [refs[0].at[p] for p in range(last - first)] if base is None else refs
    for p, out in enumerate(outs):
        at, taken = 0, 0
        low = (first + p) * block
        for kind in parts:
            if kind == "small":
                x = mats[taken][first + p].astype(f32)
                x = jnp.concatenate([x, jnp.zeros((PACK, out.shape[1] - block), f32)], axis=1)
            elif kind == "out":
                x = fold(mm(mats[taken][...], mats[taken + 1][:, low : low + block], TN), block, out.shape[1])
            else:
                start = low + (block // 2 if kind == "second_half" else 0)
                size = block if kind == "all" else block // 2
                x = mm(mats[taken][:, start : start + size], mats[taken + 1][...], TN)
            size = x.shape[0]
            for got in early:
                x = x + got[first + p, base + at : base + at + size].astype(f32)
            for got in gots:
                x = x + got[p][at : at + size].astype(f32)
            out[at : at + size] = x.astype(bf16)
            at += size
            taken += 1 if kind == "small" else 2


def add_kernel(_, x, got, out):
    out[...] = (x[...].astype(f32) + got[...].astype(f32)).astype(bf16)


def picked(idx, own, got):
    return jnp.where(idx[4] == 1, got.astype(f32), own.astype(f32))


def finish_up_kernel(idx, *refs):
    out = refs[-1]
    rows = refs[0].shape[0]
    for i in range(len(refs) // 2):
        out[i * rows : (i + 1) * rows] = picked(idx, refs[2 * i][...], refs[2 * i + 1][...])


def finish_down_kernel(idx, *refs):
    out = refs[-1]
    rows = refs[0].shape[0]
    step = min(out.shape[0], 512)
    for i in range(len(refs) // 2):
        for j in range(0, out.shape[0], step):
            x = picked(idx, refs[2 * i][:, j : j + step], refs[2 * i + 1][:, j : j + step])
            out[j : j + step, i * rows : (i + 1) * rows] = x.T


def small_kernel(block, idx, own, got, out):
    out[...] = picked(idx, own[2 * block :, :block], got[2 * block :, :block]).astype(bf16)


def finish_kernel(block, idx, a, a_got, b, b_got, qkv, out_w):
    kv = picked(idx, a[: 2 * block], a_got[: 2 * block])
    qo = picked(idx, b[...], b_got[...])
    qkv[:block] = qo[:block]
    qkv[block:] = kv
    out_w[...] = unfold(qo[block:], block)


def shape(*dims, dtype=f32):
    return jax.ShapeDtypeStruct(dims, dtype)


def local(
    inputs,
    lengths,
    ln1_gain,
    ln1_bias,
    w_qkv,
    qv_bias,
    w_out,
    out_bias,
    ln2_gain,
    ln2_bias,
    w_up,
    up_bias,
    w_down,
    down_bias,
    cotangent,
):
    nf, nc, nt = (lax.axis_size(a) for a in ("fsdp", "ctx", "tp"))
    f, c, t = (lax.axis_index(a) for a in ("fsdp", "ctx", "tp"))
    images, n, width = inputs.shape
    assert images == nc == 4 and nt == 2
    rows = n * nc
    block = width // nf
    hc = w_qkv.shape[2]
    ff = w_up.shape[1]
    n_up = up_bias.shape[0] // block
    outer = (c == 0) | (c == nc - 1)
    idx = jnp.stack([f, c, t, lax.dynamic_index_in_dim(lengths, c, 0, False), outer.astype(jnp.int32)]).astype(jnp.int32)
    wide = functools.partial(shape, rows, width)

    def to_image(x):
        return [lax.dynamic_index_in_dim(x, c, 0, False)] + [
            swap(lax.dynamic_index_in_dim(x, c ^ s, 0, False), "ctx", s) for s in range(1, nc)
        ]

    clock = []

    w_proj = w_qkv.transpose(1, 0, 2).reshape(3 * block, hc)
    proj_got = first_swap(w_proj, "fsdp")
    toks = to_image(inputs)
    (packed,) = call(
        pack_kernel,
        [shape(block + PACK, hc, dtype=bf16)],
        [idx, w_out, ln1_gain, ln1_bias, ln2_gain, ln2_bias, out_bias, down_bias, qv_bias, up_bias.reshape(n_up, block)],
        name="pack",
    )
    packed_got = first_swap(packed, "fsdp")
    proj_got, packed_got, w_up_later, toks, cotangent = tie(proj_got, packed_got, w_up, toks, cotangent)
    own, pass_on = (lax.dynamic_index_in_dim(cotangent, c ^ s, 0, False) for s in (0, 2))
    near = swap(jnp.stack([lax.dynamic_index_in_dim(cotangent, c ^ s, 0, False) for s in (1, 3)]), "ctx", 1)
    wq = gather([w_proj, proj_got], "fsdp")
    aux = gather([packed, packed_got], "fsdp")
    up_got = first_swap(w_up_later, "fsdp")
    masked, unit1, rate1, normed, q, k, v, mixed, branch_a, branch_b, up_shift, small = call(
        functools.partial(attend_kernel, nc, nf, nt, n_up),
        [
            wide(dtype=bf16),
            wide(),
            shape(rows, 128),
            wide(dtype=bf16),
            *[shape(rows, hc, dtype=bf16)] * 4,
            *[shape(rows // 2, width, dtype=bf16)] * 2,
            shape(1, ff),
            shape(nf, PACK, block, dtype=bf16),
        ],
        [idx],
        [
            pltpu.VMEM((nf, n, block), f32),
            pltpu.VMEM((nc, n, width), bf16),
            pltpu.VMEM((nf, 3 * block, hc), bf16),
            pltpu.VMEM((nf, block + PACK, hc), bf16),
            pltpu.SemaphoreType.DMA((nc + 2 * nf,)),
        ],
        mib=24,
        far=[*toks, *wq, *aux],
        clock=clock,
        name="attend",
    )
    branch_a, near = tie(branch_a, near)
    got_a, got_b = swap(branch_a, "tp", 1), swap(branch_b, "tp", 1)
    got_a, up_got, w_down_later = tie(got_a, up_got, w_down)
    (relayed,) = call(relay_kernel, [shape(2, n, width, dtype=bf16)], [idx, pass_on, near], name="relay_in")
    cots = [own, near, swap(relayed, "ctx", 2)]
    wu = gather([w_up, up_got], "fsdp")
    down_got = first_swap(w_down_later, "fsdp")

    middle, unit2, rate2, normed2, active, slope = call(
        functools.partial(up_kernel, nc, nf),
        [
            wide(),
            wide(),
            shape(rows, 128),
            wide(dtype=bf16),
            shape(rows, ff, dtype=bf16),
            shape(rows, ff),
        ],
        [idx, masked, branch_a, branch_b, got_a, got_b, small, up_shift, *wu],
        clock=clock,
        name="hidden",
    )
    (gl,) = call(
        cotangent_kernel,
        [wide(dtype=bf16)],
        [idx, *cots],
        [pltpu.VMEM((nf, n, block), f32)],
        clock=clock,
        name="cotangent",
    )

    def shard_sum(names, pieces):
        kinds = {"small": PACK, "first_half": block // 2, "second_half": block // 2}
        heights = [sum(kinds.get(kind, block) for kind in parts) for parts, _ in pieces]
        width_in = ff if len(pieces[0][0]) == 1 else hc

        def run(first, last, early, got, level, piece):
            if piece is None:
                parts, mats, base = sum((p for p, _ in pieces), ()), sum((m for _, m in pieces), ()), None
                outs = [shape(last - first, sum(heights), width_in, dtype=bf16)]
            else:
                (parts, mats), base = pieces[piece], sum(heights[:piece]) if early is not None else -1
                outs = [shape(heights[piece], width_in, dtype=bf16)] * (last - first)
            return call(
                functools.partial(shard_kernel, first, last, parts, base, block, len(got)),
                outs,
                [idx, *mats, *([] if early is None else [early]), *[x for one in got for x in one[first:last]]],
                clock=clock,
                name=names[0] + "0" if piece is None else f"{names[piece + 1]}{level}",
            )

        return ShardSum(run)

    levels = len(bits_of(nf))
    first, second = ("first_half",), ("second_half",)
    down = shard_sum(("d", "da", "db"), [(first, (gl, active)), (second, (gl, active))])
    down.start_by_pieces()
    down_got, down.got = tie(down_got, down.got)
    wd = gather([w_down, down_got], "fsdp")
    part_a, part_b = down.begin(0), down.begin(1)
    slope, part_a, part_b = tie(slope, part_a, part_b)
    down.send(part_a, 0)
    down.send(part_b, 1)
    gh, gnt, gh_sum = call(
        functools.partial(hidden_back_kernel, nf),
        [shape(rows, ff, dtype=bf16), wide(dtype=bf16), shape(1, ff)],
        [idx, gl, slope, *wd, *wu],
        [pltpu.VMEM((rows, width), f32)],
        clock=clock,
        name="hidden_back",
    )
    gnt_got = swap(gnt, "tp", 1)

    o = types.SimpleNamespace(lines={})
    clock.append(LATE)

    def back():
        o.gmid, o.gb, o.gq, o.gk, o.gv, o.sums, o.qv_sum = call(
            functools.partial(attend_back_kernel, nc, nf),
            [wide(), wide(dtype=bf16), *[shape(rows, hc, dtype=bf16)] * 3, shape(8, width), shape(8, hc)],
            [idx, gl, gnt, gnt_got, unit2, rate2, small, q, k, v, *aux],
            [pltpu.VMEM((rows, hc), bf16)],
            clock=clock,
            name="back",
        )

    def normed_back():
        o.gn, o.cross, o.pack = call(
            functools.partial(normed_back_kernel, nf, nt, n_up),
            [wide(dtype=bf16), wide(dtype=bf16), shape(nf, PACK, block, dtype=bf16)],
            [idx, o.gq, o.gk, o.gv, unit1, o.sums, o.qv_sum, gh_sum, o.ffn, *wq],
            clock=clock,
            name="normed",
        )
        o.cross_got = swap(o.cross, "tp", 1)

    def outputs():
        o.stay, o.pass_on, o.go = call(
            functools.partial(outputs_kernel, nc),
            [shape(n, width, dtype=bf16), shape(n, width, dtype=bf16), shape(2, n, width, dtype=bf16)],
            [idx, o.ffn, o.cross_got, middle, o.gn, unit1, rate1, o.gmid, small],
            [pltpu.VMEM((nf, n, block), f32)],
            clock=clock,
            name="outputs",
        )
        o.near = swap(o.go, "ctx", 1)

    def relay():
        (x,) = call(relay_kernel, [shape(2, n, width, dtype=bf16)], [idx, o.pass_on, o.near], clock=clock, name="relay")
        o.far = swap(x, "ctx", 2)

    def assemble():
        out, args = [shape(nc, n, width, dtype=bf16)], [idx, o.stay, o.near, o.far]
        (o.ours,) = call(assemble_kernel, out, args, clock=clock, name="assemble")
        o.theirs = swap(o.ours, "tp", 1)

    def split():
        out = [shape(nc, n, width, dtype=bf16), shape(nc, n, width)]
        o.result, o.grad_inputs = call(split_kernel, out, [idx, o.ours, o.theirs], clock=clock, name="split")

    def finish_down():
        args = [idx, *o.lines["da"].ends(), *o.lines["db"].ends()]
        (o.grad_down,) = call(finish_down_kernel, [shape(ff, block)], args, clock=clock, name="grad_down")

    def finish_up():
        args = [idx, *o.lines["ua"].ends(), *o.lines["ub"].ends()]
        (o.grad_up,) = call(finish_up_kernel, [shape(block, ff)], args, clock=clock, name="grad_up")

    def small_sums():
        out, args = [shape(PACK, block, dtype=bf16)], [idx, *o.lines["kv"].ends()]
        (x,) = call(functools.partial(small_kernel, block), out, args, clock=clock, name="small")
        o.total = x.astype(f32) + swap(x, "tp", 1).astype(f32)

    def finish():
        o.grad_qkv, o.grad_out = call(
            functools.partial(finish_kernel, block),
            [shape(3 * block, hc), shape(hc, block)],
            [idx, *o.lines["kv"].ends(), *o.lines["qo"].ends()],
            clock=clock,
            name="finish",
        )

    def ffn_out():
        (o.ffn,) = call(functools.partial(down_kernel, nf), [wide(dtype=bf16)], [idx, active, *wd], clock=clock, name="ffn")

    def start_up():
        o.up = shard_sum(("u", "ua", "ub"), [(first, (normed2, gh)), (second, (normed2, gh))])
        o.up.start()

    def start_rest():
        kv = (("all", "all", "small"), (normed, o.gk, normed, o.gv, o.pack))
        qo = (("all", "out"), (normed, o.gq, mixed, o.gb))
        o.rest = shard_sum(("t", "kv", "qo"), [kv, qo])
        o.rest.start()

    o.down = down
    places = {"da": ("down", 0), "db": ("down", 1), "ua": ("up", 0), "ub": ("up", 1), "kv": ("rest", 0), "qo": ("rest", 1)}
    steps = {
        "back": back,
        "normed": normed_back,
        "outputs": outputs,
        "relay": relay,
        "assemble": assemble,
        "split": split,
        "grad_down": finish_down,
        "grad_up": finish_up,
        "small": small_sums,
        "finish": finish,
        "ffn": ffn_out,
        "u0": start_up,
        "t0": start_rest,
    }
    for name in ORDER:
        if name in steps:
            steps[name]()
        elif name[-1] == "1":
            which, piece = places[name[:-1]]
            one = getattr(o, which)
            one.send(one.begin(piece), piece)
        elif name[-1] == "2":
            which, piece = places[name[:-1]]
            one = getattr(o, which)
            for _ in range(2, levels):
                one.send(one.begin(piece), piece)
            o.lines[name[:-1]] = Line(one.own(piece), idx, clock)
        else:
            o.lines[name].advance(name)
    total = o.total[:]
    return (
        o.result,
        o.grad_inputs,
        total[0],
        total[1],
        o.grad_qkv.reshape(3, block, hc).transpose(1, 0, 2),
        total[6:8],
        o.grad_out,
        total[4],
        total[2],
        total[3],
        o.grad_up,
        total[8 : 8 + n_up].reshape(-1),
        o.grad_down,
        total[5],
    )


def solution(mesh):
    in_specs = (
        P("fsdp", "ctx", None),
        P("fsdp"),
        P("fsdp"),
        P("fsdp"),
        P("fsdp", None, "tp"),
        P(None, "fsdp"),
        P("tp", "fsdp"),
        P("fsdp"),
        P("fsdp"),
        P("fsdp"),
        P("fsdp", "tp"),
        P("fsdp"),
        P("tp", "fsdp"),
        P("fsdp"),
        P("fsdp", "ctx", None),
    )
    out_specs = (
        P("fsdp", "ctx", None),
        P("fsdp", "ctx", None),
        P("fsdp"),
        P("fsdp"),
        P("fsdp", None, "tp"),
        P(None, "fsdp"),
        P("tp", "fsdp"),
        P("fsdp"),
        P("fsdp"),
        P("fsdp"),
        P("fsdp", "tp"),
        P("fsdp"),
        P("tp", "fsdp"),
        P("fsdp"),
    )
    return jax.shard_map(local, mesh=mesh, in_specs=in_specs, out_specs=out_specs, check_vma=False)
```

```python
import functools
import types

import jax
import jax.numpy as jnp
from jax import lax
from jax.experimental import pallas as pl
from jax.experimental.pallas import tpu as pltpu
from jax.sharding import PartitionSpec as P

HD = 64
epsilon = 1e-06
f32 = jnp.float32
bf16 = jnp.bfloat16
PACK = 16
CHUNK = 512
LATE = "late"
ORDER = (
    "u0", "da2", "ub1", "ffn", "back", "da", "db2", "normed", "ub2", "ua1", "da", "db", "outputs", "ua2",
    "ub", "db", "t0", "relay", "kv1", "grad_down", "ua", "qo1", "kv2", "ub", "assemble", "qo2", "kv", "ua",
    "split", "qo", "kv", "qo", "small", "grad_up", "finish",
)


def bits_of(n):
    out, bit = [], 1
    while bit < n:
        out.append(bit)
        bit *= 2
    return out


def bitrev(n):
    order = [0]
    for bit in reversed(bits_of(n)):
        order = order + [j | bit for j in order]
    return order


def place(x, n):
    bits = len(bits_of(n))
    out = 0
    for k in range(bits):
        out = out + ((x >> k) & 1) * (1 << (bits - 1 - k))
    return out


def swap(x, axis, bit):
    return lax.ppermute(x, axis, [(i, i ^ bit) for i in range(lax.axis_size(axis))])


def gather(pieces, axis):
    for bit in reversed(bits_of(lax.axis_size(axis) // len(pieces))):
        pieces = pieces + [swap(p, axis, bit) for p in pieces]
    return pieces


def first_swap(piece, axis):
    return swap(piece, axis, bits_of(lax.axis_size(axis))[-1])


class ShardSum:
    def __init__(self, run):
        self.run, self.n, self.first, self.got = run, lax.axis_size("fsdp"), None, [[], []]

    def start(self):
        (x,) = self.run(self.n // 2, self.n, None, [], 0, None)
        self.first = swap(x, "fsdp", 1)

    def start_by_pieces(self):
        for piece in range(2):
            self.send(self.begin(piece), piece)

    def level(self, piece):
        return len(self.got[piece]) + (self.first is not None)

    def begin(self, piece):
        level = self.level(piece)
        n = self.n >> level
        return self.run(n // 2, n, self.first, self.got[piece], level, piece)

    def send(self, blocks, piece):
        level = self.level(piece)
        self.got[piece].append([swap(x, "fsdp", 1 << level) for x in blocks])

    def own(self, piece):
        return self.run(0, 1, self.first, self.got[piece], self.level(piece), piece)[0]


def tie(*trees):
    flat, where = jax.tree.flatten(trees)
    return jax.tree.unflatten(where, lax.optimization_barrier(flat))


class Line:
    def __init__(self, x, idx, clock):
        assert lax.axis_size("ctx") == 4
        self.held, self.idx, self.clock, self.step = x, idx, clock, 0
        self.got = self.send()

    def send(self):
        pairs = ([(0, 1), (3, 2)], [(1, 2), (2, 1)], [(1, 0), (2, 3)])[self.step]
        return lax.ppermute(self.held, "ctx", pairs)

    def advance(self, name):
        self.step += 1
        out = [jax.ShapeDtypeStruct(self.held.shape, bf16)]
        args, name = [self.idx, self.held, self.got], f"{name}_{self.step}"
        (self.held,) = call(add_kernel, out, args, clock=self.clock, name=name)
        self.got = self.send()

    def ends(self):
        return [self.held, self.got]


NN = (((1,), (0,)), ((), ()))
NT = (((1,), (1,)), ((), ()))
TN = (((0,), (0,)), ((), ()))


def mm(a, b, dims=NN):
    return lax.dot_general(a, b, dims, preferred_element_type=f32)


def call(kernel, outs, args, scratch=(), mib=12, far=(), clock=None, name=None):
    vm = pl.BlockSpec(memory_space=pltpu.VMEM)
    near = len(args)
    last = [] if clock is None else [x for x in clock if x is not LATE]
    late = clock is not None and any(x is LATE for x in clock)
    args = [*args, *far, *last]
    count = len(args) - len(last)

    def body(*refs):
        kernel(*refs[:count], *refs[count + len(last) :])

    results = pl.pallas_call(
        body,
        out_shape=outs,
        in_specs=[pl.BlockSpec(memory_space=pltpu.SMEM)]
        + [vm] * (near - 1)
        + [pl.BlockSpec(memory_space=pl.ANY)] * (len(far) + len(last)),
        out_specs=[vm] * len(outs),
        scratch_shapes=list(scratch),
        compiler_params=pltpu.CompilerParams(vmem_limit_bytes=mib << 20),
        cost_estimate=pl.CostEstimate(flops=int(3e10) if late else 0, bytes_accessed=0, transcendentals=0),
        name=name,
    )(*args)
    if clock is not None:
        clock[:] = [results[-1], LATE] if late else [results[-1]]
    return results


def rows_of(small, r):
    return jnp.concatenate([small[p].astype(f32)[r : r + 1] for p in range(small.shape[0])], axis=1)


def live_rows(idx, s, n):
    return (idx[1] ^ s) * n + lax.broadcasted_iota(jnp.int32, (n, 1), 0) < idx[3]


def live_keys(idx, nc, n):
    col = lax.broadcasted_iota(jnp.int32, (1, nc * n), 1)
    slot = col
    for s in range(nc):
        slot = jnp.where((col >= s * n) & (col < (s + 1) * n), slot + ((idx[1] ^ s) - s) * n, slot)
    return slot < idx[3]


def to_relative(idx, x, box):
    nf, _, block = box.shape
    for b in range(nf):
        box[place(idx[0] ^ b, nf)] = x[:, b * block : (b + 1) * block]
    return jnp.concatenate([box[p] for p in range(nf)], axis=1)


def from_relative(idx, x, box):
    nf, _, block = box.shape
    for p in range(nf):
        box[p] = x[:, p * block : (p + 1) * block]
    return jnp.concatenate([box[place(idx[0] ^ b, nf)] for b in range(nf)], axis=1)


def mean(x):
    return jnp.mean(x, axis=-1, keepdims=True)


def normalize(x):
    center = x - mean(x)
    rate = lax.rsqrt(mean(center * center) + epsilon)
    return center * rate, rate


def norm_back(grad, gain, unit, rate):
    e = grad * gain
    return rate * (e - mean(e) - unit * mean(e * unit))


def softmax_of(q, k, keep, scale):
    scores = jnp.where(keep, mm(q, k, NT) * scale, -1e30)
    expo = jnp.exp(scores - jnp.max(scores, axis=-1, keepdims=True))
    return expo * (1.0 / jnp.sum(expo, axis=-1, keepdims=True))


def sides(n):
    lane = lax.broadcasted_iota(jnp.int32, (1, n), 1)
    return [(lane >= h * HD) & (lane < (h + 1) * HD) for h in range(n // HD)]


def only(keep, x):
    return jnp.where(keep, x.astype(f32), 0.0).astype(x.dtype)


def merge(keeps, parts):
    out = parts[0]
    for keep, part in zip(keeps[1:], parts[1:]):
        out = jnp.where(keep, part, out)
    return out


def fold(x, block, width):
    k = width // block
    rows = x.shape[0] // k
    return jnp.concatenate([x[i * rows : (i + 1) * rows] for i in range(k)], axis=1)


def unfold(x, block):
    return jnp.concatenate([x[:, i * block : (i + 1) * block] for i in range(x.shape[1] // block)], axis=0)


def pack_kernel(_, wo, *refs):
    *vectors, qv, up, out = refs
    block = qv.shape[1]
    out[:block] = fold(wo[...], block, out.shape[1])
    lines = [x[...].astype(f32).reshape(1, block) for x in vectors] + [qv[...].astype(f32), up[...].astype(f32)]
    lines.append(jnp.zeros((PACK - 8 - up.shape[0], block), f32))
    out[block:, :block] = jnp.concatenate(lines, axis=0).astype(bf16)
    out[block:, block:] = jnp.zeros((PACK, out.shape[1] - block), bf16)


def attend_kernel(nc, nf, nt, n_up, *refs):
    idx, refs = refs[0], refs[1:]
    sources = refs[: nc + 2 * nf]
    masked, unit1, rate1, normed, q, k, v, mixed, *branch, up_shift, small, box, tok_all, w_all, aux_all, sems = refs[
        nc + 2 * nf :
    ]
    toks = [tok_all.at[s] for s in range(nc)]
    wq, aux = [w_all.at[p] for p in range(nf)], [aux_all.at[p] for p in range(nf)]
    places = [*toks, *wq, *aux]
    order = [*range(nc), *range(nc + nf, nc + 2 * nf), *range(nc, nc + nf)]
    copies = {i: pltpu.make_async_copy(sources[i], places[i], sems.at[i]) for i in order}
    for i in order:
        copies[i].start()
    for i in order[: nc + nf]:
        copies[i].wait()
    n = toks[0].shape[0]
    block = small.shape[2]
    for p in range(nf):
        small[p] = aux[p][block:, :block]
    hc = q.shape[1]
    gain, shift = rows_of(small, 0), rows_of(small, 1)
    for s in range(nc):
        here = slice(s * n, (s + 1) * n)
        x = jnp.where(live_rows(idx, s, n), toks[s][...].astype(f32), 0.0)
        x = to_relative(idx, x, box)
        masked[here, :] = x.astype(bf16)
        unit, rate = normalize(x)
        unit1[here, :] = unit
        rate1[here, :] = jnp.broadcast_to(rate, (n, 128))
        normed[here, :] = (unit * gain + shift).astype(bf16)
    shifts = []
    for i in range(nf // nt):
        mine = small[place(idx[0] ^ (idx[2] * (nf // nt) + i), nf)].astype(f32)
        shifts.append((mine[6:7], mine[7:8]))
        for r in range(n_up):
            up_shift[:, (i * n_up + r) * block : (i * n_up + r + 1) * block] = mine[8 + r : 9 + r]
    q_shift = jnp.concatenate([a for a, _ in shifts], axis=1)
    v_shift = jnp.concatenate([b for _, b in shifts], axis=1)
    for i in order[nc + nf :]:
        copies[i].wait()
    for j, (out, bias) in enumerate(((q, q_shift), (k, None), (v, v_shift))):
        acc = mm(normed[:, :block], wq[0][j * block : (j + 1) * block])
        for p in range(1, nf):
            acc = acc + mm(normed[:, p * block : (p + 1) * block], wq[p][j * block : (j + 1) * block])
        out[...] = (acc if bias is None else acc + bias).astype(bf16)
    keep = live_keys(idx, nc, n)
    halves = sides(128)

    def pair(i, _):
        at = pl.ds(pl.multiple_of(i * 128, 128), 128)
        qp, kp, vp = q[:, at], k[:, at], v[:, at]
        parts = [mm(softmax_of(only(h, qp), kp, keep, HD**-0.5).astype(bf16), vp) for h in halves]
        mixed[:, at] = merge(halves, parts).astype(bf16)
        return 0

    lax.fori_loop(0, hc // 128, pair, 0, unroll=True)
    for p in range(nf):
        out_w = unfold(aux[p][:block], block)
        for h, out in enumerate(branch):
            part = mixed[h * out.shape[0] : (h + 1) * out.shape[0]]
            out[:, p * block : (p + 1) * block] = mm(part, out_w).astype(bf16)


def up_kernel(nc, nf, *refs):
    idx, masked, own_a, own_b, got_a, got_b, small, up_shift = refs[:8]
    wu = refs[8 : 8 + nf]
    middle, unit2, rate2, normed2, active, slope = refs[8 + nf :]
    n = masked.shape[0] // nc
    block = small.shape[2]
    gain, shift, bias = rows_of(small, 2), rows_of(small, 3), rows_of(small, 4)
    for s in range(nc):
        here = slice(s * n, (s + 1) * n)
        own, got = (own_a, got_a) if s < nc // 2 else (own_b, got_b)
        part = slice(s % (nc // 2) * n, (s % (nc // 2) + 1) * n)
        x = masked[here, :].astype(f32) + (own[part, :].astype(f32) + got[part, :].astype(f32) + bias)
        middle[here, :] = x
        unit, rate = normalize(x)
        unit2[here, :] = unit
        rate2[here, :] = jnp.broadcast_to(rate, (n, 128))
        normed2[here, :] = (unit * gain + shift).astype(bf16)
    chunk = min(CHUNK, active.shape[1])

    def step(i, _):
        at = pl.ds(pl.multiple_of(i * chunk, chunk), chunk)
        acc = mm(normed2[:, :block], wu[0][:, at])
        for p in range(1, nf):
            acc = acc + mm(normed2[:, p * block : (p + 1) * block], wu[p][:, at])
        x = acc + up_shift[:, at]
        root = 0.7978845608028654
        tanh = jnp.tanh(root * (x + 0.044715 * (x * x * x)))
        half = 0.5 * (1.0 + tanh)
        active[:, at] = (x * half).astype(bf16)
        slope[:, at] = half + 0.5 * x * (1.0 - tanh * tanh) * (root * (1.0 + 3 * 0.044715 * (x * x)))
        return 0

    lax.fori_loop(0, active.shape[1] // chunk, step, 0, unroll=True)


def cotangent_kernel(idx, own, near, far, gl, box):
    n = own.shape[0]
    for s, x in enumerate((own, near.at[0], far.at[0], far.at[1])):
        c = jnp.where(live_rows(idx, s, n), x[...].astype(f32), 0.0)
        gl[s * n : (s + 1) * n, :] = to_relative(idx, c, box).astype(bf16)


def hidden_back_kernel(nf, *refs):
    _, gl, slope = refs[:3]
    wd, wu = refs[3 : 3 + nf], refs[3 + nf : 3 + 2 * nf]
    gh, gnt, gh_sum, acc = refs[3 + 2 * nf :]
    block = wd[0].shape[1]
    chunk = min(CHUNK, gh.shape[1])
    acc[...] = jnp.zeros_like(acc)

    def step(i, _):
        at = pl.ds(pl.multiple_of(i * chunk, chunk), chunk)
        ga = mm(gl[:, :block], wd[0][at, :], NT)
        for p in range(1, nf):
            ga = ga + mm(gl[:, p * block : (p + 1) * block], wd[p][at, :], NT)
        g = (ga * slope[:, at]).astype(bf16)
        gh[:, at] = g
        gh_sum[:, at] = jnp.sum(g.astype(f32), axis=0, keepdims=True)
        for p in range(nf):
            acc[:, p * block : (p + 1) * block] += mm(g, wu[p][:, at], NT)
        return 0

    lax.fori_loop(0, gh.shape[1] // chunk, step, 0, unroll=True)
    gnt[...] = acc[...].astype(bf16)


def down_kernel(nf, idx, active, *refs):
    out = refs[nf]
    block = refs[0].shape[1]
    for p in range(nf):
        out[:, p * block : (p + 1) * block] = mm(active[...], refs[p][...]).astype(bf16)


def attend_back_kernel(nc, nf, *refs):
    idx, gl, own, got, unit2, rate2, small, q, k, v = refs[:10]
    aux = refs[10 : 10 + nf]
    gmid, gb, gq, gk, gv, sums, qv_sum, gm = refs[10 + nf :]
    n = gl.shape[0] // nc
    block = small.shape[2]
    hc = q.shape[1]
    gain = rows_of(small, 2)
    totals = [0.0] * 4
    for s in range(nc):
        here = slice(s * n, (s + 1) * n)
        g = own[here, :].astype(f32) + got[here, :].astype(f32)
        u = unit2[here, :]
        c = gl[here, :].astype(f32)
        x = c + norm_back(g, gain, u, rate2[here, :1])
        gmid[here, :] = x
        low = x.astype(bf16)
        gb[here, :] = low
        for r, value in enumerate((g * u, g, low.astype(f32), c)):
            totals[r] = totals[r] + jnp.sum(value, axis=0, keepdims=True)
    sums[...] = jnp.concatenate(totals + [jnp.zeros((4, gl.shape[1]), f32)], axis=0)
    acc = mm(gb[:, :block], unfold(aux[0][:block], block), NT)
    for p in range(1, nf):
        acc = acc + mm(gb[:, p * block : (p + 1) * block], unfold(aux[p][:block], block), NT)
    gm[...] = acc.astype(bf16)
    keep = live_keys(idx, nc, n)
    halves = sides(128)
    scale = HD**-0.5

    def pair(i, _):
        at = pl.ds(pl.multiple_of(i * 128, 128), 128)
        qp, kp, vp, gp = q[:, at], k[:, at], v[:, at], gm[:, at]
        dq, dk, dv = [], [], []
        for h in halves:
            prob = softmax_of(only(h, qp), kp, keep, scale)
            grad = mm(only(h, gp), vp, NT)
            dv.append(mm(prob.astype(bf16), gp, TN))
            ds = (prob * (grad - jnp.sum(prob * grad, axis=-1, keepdims=True))).astype(bf16)
            dq.append(mm(ds, kp))
            dk.append(mm(ds, qp, TN))
        a = (merge(halves, dq) * scale).astype(bf16)
        b = merge(halves, dv).astype(bf16)
        gq[:, at] = a
        gk[:, at] = (merge(halves, dk) * scale).astype(bf16)
        gv[:, at] = b
        total = [jnp.sum(x.astype(f32), axis=0, keepdims=True) for x in (a, b)]
        qv_sum[:, at] = jnp.concatenate(total + [jnp.zeros((6, 128), f32)], axis=0)
        return 0

    lax.fori_loop(0, hc // 128, pair, 0, unroll=True)


def normed_back_kernel(nf, nt, n_up, idx, gq, gk, gv, unit1, sums, qv_sum, gh_sum, ffn, *refs):
    wq, (gn, cross, pack) = refs[:nf], refs[nf:]
    block = pack.shape[2]
    order = bitrev(nf)
    first = jnp.where(idx[2] == 0, 1.0, 0.0)
    held = nf // nt
    for p in range(nf):
        here = slice(p * block, (p + 1) * block)
        acc = mm(gq[...], wq[p][:block], NT) + mm(gk[...], wq[p][block : 2 * block], NT)
        acc = acc + mm(gv[...], wq[p][2 * block : 3 * block], NT)
        gn[:, here] = acc.astype(bf16)
        cross[:, here] = jnp.where(idx[2] == 0, acc, ffn[:, here].astype(f32)).astype(bf16)
        rows = [jnp.sum(acc * unit1[:, here], axis=0, keepdims=True), jnp.sum(acc, axis=0, keepdims=True)]
        rows += [sums[r : r + 1, here] * first for r in range(4)]
        which = (idx[0] ^ order[p]) - idx[2] * held

        def mine(of):
            out = jnp.zeros((1, block), f32)
            for i in range(held):
                out = jnp.where(which == i, of(i), out)
            return out

        rows += [mine(lambda i, r=r: qv_sum[r : r + 1, i * block : (i + 1) * block]) for r in range(2)]
        rows += [
            mine(lambda i, r=r: gh_sum[:, (i * n_up + r) * block : (i * n_up + r + 1) * block]) for r in range(n_up)
        ]
        rows.append(jnp.zeros((PACK - len(rows), block), f32))
        pack[p] = jnp.concatenate(rows, axis=0).astype(bf16)


def outputs_kernel(nc, idx, ffn, cross_got, middle, gn, unit1, rate1, gmid, small, stay, pass_on, go, box):
    n = gmid.shape[0] // nc
    outs = [stay, go.at[0], pass_on, go.at[1]]

    @pl.when(idx[2] == 0)
    def _():
        bias = rows_of(small, 5)
        for s in range(nc):
            here = slice(s * n, (s + 1) * n)
            x = middle[here, :] + (ffn[here, :].astype(f32) + cross_got[here, :].astype(f32) + bias)
            outs[s][...] = from_relative(idx, jnp.where(live_rows(idx, s, n), x, 0.0), box).astype(bf16)

    @pl.when(idx[2] != 0)
    def _():
        gain = rows_of(small, 0)
        for s in range(nc):
            here = slice(s * n, (s + 1) * n)
            g = gn[here, :].astype(f32) + cross_got[here, :].astype(f32)
            x = gmid[here, :] + norm_back(g, gain, unit1[here, :], rate1[here, :1])
            outs[s][...] = from_relative(idx, jnp.where(live_rows(idx, s, n), x, 0.0), box).astype(bf16)


def relay_kernel(_, own, got, out):
    out[0] = own[...]
    out[1] = got[1]


def assemble_kernel(idx, own, near, far, out):
    out[idx[1]] = own[...]
    out[idx[1] ^ 1] = near[0]
    out[idx[1] ^ 2] = far[0]
    out[idx[1] ^ 3] = far[1]


def split_kernel(idx, own, got, result, grad):
    @pl.when(idx[2] == 0)
    def _():
        result[...] = own[...]
        grad[...] = got[...].astype(f32)

    @pl.when(idx[2] != 0)
    def _():
        result[...] = got[...]
        grad[...] = own[...].astype(f32)


def shard_kernel(first, last, parts, base, block, levels, *refs):
    refs = list(refs[1:])
    mats = [refs.pop(0) for kind in parts for _ in range(1 if kind == "small" else 2)]
    early = [refs.pop(0)] if base is not None and base >= 0 else []
    gots = [[refs.pop(0) for _ in range(first, last)] for _ in range(levels)]
    outs = [refs[0].at[p] for p in range(last - first)] if base is None else refs
    for p, out in enumerate(outs):
        at, taken = 0, 0
        low = (first + p) * block
        for kind in parts:
            if kind == "small":
                x = mats[taken][first + p].astype(f32)
                x = jnp.concatenate([x, jnp.zeros((PACK, out.shape[1] - block), f32)], axis=1)
            elif kind == "out":
                x = fold(mm(mats[taken][...], mats[taken + 1][:, low : low + block], TN), block, out.shape[1])
            else:
                start = low + (block // 2 if kind == "second_half" else 0)
                size = block if kind == "all" else block // 2
                x = mm(mats[taken][:, start : start + size], mats[taken + 1][...], TN)
            size = x.shape[0]
            for got in early:
                x = x + got[first + p, base + at : base + at + size].astype(f32)
            for got in gots:
                x = x + got[p][at : at + size].astype(f32)
            out[at : at + size] = x.astype(bf16)
            at += size
            taken += 1 if kind == "small" else 2


def add_kernel(_, x, got, out):
    out[...] = (x[...].astype(f32) + got[...].astype(f32)).astype(bf16)


def picked(idx, own, got):
    return jnp.where(idx[4] == 1, got.astype(f32), own.astype(f32))


def finish_up_kernel(idx, *refs):
    out = refs[-1]
    rows = refs[0].shape[0]
    for i in range(len(refs) // 2):
        out[i * rows : (i + 1) * rows] = picked(idx, refs[2 * i][...], refs[2 * i + 1][...])


def finish_down_kernel(idx, *refs):
    out = refs[-1]
    rows = refs[0].shape[0]
    step = min(out.shape[0], 512)
    for i in range(len(refs) // 2):
        for j in range(0, out.shape[0], step):
            x = picked(idx, refs[2 * i][:, j : j + step], refs[2 * i + 1][:, j : j + step])
            out[j : j + step, i * rows : (i + 1) * rows] = x.T


def small_kernel(block, idx, own, got, out):
    out[...] = picked(idx, own[2 * block :, :block], got[2 * block :, :block]).astype(bf16)


def finish_kernel(block, idx, a, a_got, b, b_got, qkv, out_w):
    kv = picked(idx, a[: 2 * block], a_got[: 2 * block])
    qo = picked(idx, b[...], b_got[...])
    qkv[:block] = qo[:block]
    qkv[block:] = kv
    out_w[...] = unfold(qo[block:], block)


def shape(*dims, dtype=f32):
    return jax.ShapeDtypeStruct(dims, dtype)


def local(
    inputs,
    lengths,
    ln1_gain,
    ln1_bias,
    w_qkv,
    qv_bias,
    w_out,
    out_bias,
    ln2_gain,
    ln2_bias,
    w_up,
    up_bias,
    w_down,
    down_bias,
    cotangent,
):
    nf, nc, nt = (lax.axis_size(a) for a in ("fsdp", "ctx", "tp"))
    f, c, t = (lax.axis_index(a) for a in ("fsdp", "ctx", "tp"))
    images, n, width = inputs.shape
    assert images == nc == 4 and nt == 2
    rows = n * nc
    block = width // nf
    hc = w_qkv.shape[2]
    ff = w_up.shape[1]
    n_up = up_bias.shape[0] // block
    outer = (c == 0) | (c == nc - 1)
    idx = jnp.stack([f, c, t, lax.dynamic_index_in_dim(lengths, c, 0, False), outer.astype(jnp.int32)]).astype(jnp.int32)
    wide = functools.partial(shape, rows, width)

    def to_image(x):
        return [lax.dynamic_index_in_dim(x, c, 0, False)] + [
            swap(lax.dynamic_index_in_dim(x, c ^ s, 0, False), "ctx", s) for s in range(1, nc)
        ]

    clock = []

    w_proj = w_qkv.transpose(1, 0, 2).reshape(3 * block, hc)
    proj_got = first_swap(w_proj, "fsdp")
    toks = to_image(inputs)
    (packed,) = call(
        pack_kernel,
        [shape(block + PACK, hc, dtype=bf16)],
        [idx, w_out, ln1_gain, ln1_bias, ln2_gain, ln2_bias, out_bias, down_bias, qv_bias, up_bias.reshape(n_up, block)],
        name="pack",
    )
    packed_got = first_swap(packed, "fsdp")
    proj_got, packed_got, w_up_later, toks, cotangent = tie(proj_got, packed_got, w_up, toks, cotangent)
    own, pass_on = (lax.dynamic_index_in_dim(cotangent, c ^ s, 0, False) for s in (0, 2))
    near = swap(jnp.stack([lax.dynamic_index_in_dim(cotangent, c ^ s, 0, False) for s in (1, 3)]), "ctx", 1)
    wq = gather([w_proj, proj_got], "fsdp")
    aux = gather([packed, packed_got], "fsdp")
    up_got = first_swap(w_up_later, "fsdp")
    masked, unit1, rate1, normed, q, k, v, mixed, branch_a, branch_b, up_shift, small = call(
        functools.partial(attend_kernel, nc, nf, nt, n_up),
        [
            wide(dtype=bf16),
            wide(),
            shape(rows, 128),
            wide(dtype=bf16),
            *[shape(rows, hc, dtype=bf16)] * 4,
            *[shape(rows // 2, width, dtype=bf16)] * 2,
            shape(1, ff),
            shape(nf, PACK, block, dtype=bf16),
        ],
        [idx],
        [
            pltpu.VMEM((nf, n, block), f32),
            pltpu.VMEM((nc, n, width), bf16),
            pltpu.VMEM((nf, 3 * block, hc), bf16),
            pltpu.VMEM((nf, block + PACK, hc), bf16),
            pltpu.SemaphoreType.DMA((nc + 2 * nf,)),
        ],
        mib=24,
        far=[*toks, *wq, *aux],
        clock=clock,
        name="attend",
    )
    branch_a, near = tie(branch_a, near)
    got_a, got_b = swap(branch_a, "tp", 1), swap(branch_b, "tp", 1)
    got_a, up_got, w_down_later = tie(got_a, up_got, w_down)
    (relayed,) = call(relay_kernel, [shape(2, n, width, dtype=bf16)], [idx, pass_on, near], name="relay_in")
    cots = [own, near, swap(relayed, "ctx", 2)]
    wu = gather([w_up, up_got], "fsdp")
    down_got = first_swap(w_down_later, "fsdp")

    middle, unit2, rate2, normed2, active, slope = call(
        functools.partial(up_kernel, nc, nf),
        [
            wide(),
            wide(),
            shape(rows, 128),
            wide(dtype=bf16),
            shape(rows, ff, dtype=bf16),
            shape(rows, ff),
        ],
        [idx, masked, branch_a, branch_b, got_a, got_b, small, up_shift, *wu],
        clock=clock,
        name="hidden",
    )
    (gl,) = call(
        cotangent_kernel,
        [wide(dtype=bf16)],
        [idx, *cots],
        [pltpu.VMEM((nf, n, block), f32)],
        clock=clock,
        name="cotangent",
    )

    def shard_sum(names, pieces):
        kinds = {"small": PACK, "first_half": block // 2, "second_half": block // 2}
        heights = [sum(kinds.get(kind, block) for kind in parts) for parts, _ in pieces]
        width_in = ff if len(pieces[0][0]) == 1 else hc

        def run(first, last, early, got, level, piece):
            if piece is None:
                parts, mats, base = sum((p for p, _ in pieces), ()), sum((m for _, m in pieces), ()), None
                outs = [shape(last - first, sum(heights), width_in, dtype=bf16)]
            else:
                (parts, mats), base = pieces[piece], sum(heights[:piece]) if early is not None else -1
                outs = [shape(heights[piece], width_in, dtype=bf16)] * (last - first)
            return call(
                functools.partial(shard_kernel, first, last, parts, base, block, len(got)),
                outs,
                [idx, *mats, *([] if early is None else [early]), *[x for one in got for x in one[first:last]]],
                clock=clock,
                name=names[0] + "0" if piece is None else f"{names[piece + 1]}{level}",
            )

        return ShardSum(run)

    levels = len(bits_of(nf))
    first, second = ("first_half",), ("second_half",)
    down = shard_sum(("d", "da", "db"), [(first, (gl, active)), (second, (gl, active))])
    down.start_by_pieces()
    down_got, down.got = tie(down_got, down.got)
    wd = gather([w_down, down_got], "fsdp")
    part_a, part_b = down.begin(0), down.begin(1)
    slope, part_a, part_b = tie(slope, part_a, part_b)
    down.send(part_a, 0)
    down.send(part_b, 1)
    gh, gnt, gh_sum = call(
        functools.partial(hidden_back_kernel, nf),
        [shape(rows, ff, dtype=bf16), wide(dtype=bf16), shape(1, ff)],
        [idx, gl, slope, *wd, *wu],
        [pltpu.VMEM((rows, width), f32)],
        clock=clock,
        name="hidden_back",
    )
    gnt_got = swap(gnt, "tp", 1)

    o = types.SimpleNamespace(lines={})
    clock.append(LATE)

    def back():
        o.gmid, o.gb, o.gq, o.gk, o.gv, o.sums, o.qv_sum = call(
            functools.partial(attend_back_kernel, nc, nf),
            [wide(), wide(dtype=bf16), *[shape(rows, hc, dtype=bf16)] * 3, shape(8, width), shape(8, hc)],
            [idx, gl, gnt, gnt_got, unit2, rate2, small, q, k, v, *aux],
            [pltpu.VMEM((rows, hc), bf16)],
            clock=clock,
            name="back",
        )

    def normed_back():
        o.gn, o.cross, o.pack = call(
            functools.partial(normed_back_kernel, nf, nt, n_up),
            [wide(dtype=bf16), wide(dtype=bf16), shape(nf, PACK, block, dtype=bf16)],
            [idx, o.gq, o.gk, o.gv, unit1, o.sums, o.qv_sum, gh_sum, o.ffn, *wq],
            clock=clock,
            name="normed",
        )
        o.cross_got = swap(o.cross, "tp", 1)

    def outputs():
        o.stay, o.pass_on, o.go = call(
            functools.partial(outputs_kernel, nc),
            [shape(n, width, dtype=bf16), shape(n, width, dtype=bf16), shape(2, n, width, dtype=bf16)],
            [idx, o.ffn, o.cross_got, middle, o.gn, unit1, rate1, o.gmid, small],
            [pltpu.VMEM((nf, n, block), f32)],
            clock=clock,
            name="outputs",
        )
        o.near = swap(o.go, "ctx", 1)

    def relay():
        (x,) = call(relay_kernel, [shape(2, n, width, dtype=bf16)], [idx, o.pass_on, o.near], clock=clock, name="relay")
        o.far = swap(x, "ctx", 2)

    def assemble():
        out, args = [shape(nc, n, width, dtype=bf16)], [idx, o.stay, o.near, o.far]
        (o.ours,) = call(assemble_kernel, out, args, clock=clock, name="assemble")
        o.theirs = swap(o.ours, "tp", 1)

    def split():
        out = [shape(nc, n, width, dtype=bf16), shape(nc, n, width)]
        o.result, o.grad_inputs = call(split_kernel, out, [idx, o.ours, o.theirs], clock=clock, name="split")

    def finish_down():
        args = [idx, *o.lines["da"].ends(), *o.lines["db"].ends()]
        (o.grad_down,) = call(finish_down_kernel, [shape(ff, block)], args, clock=clock, name="grad_down")

    def finish_up():
        args = [idx, *o.lines["ua"].ends(), *o.lines["ub"].ends()]
        (o.grad_up,) = call(finish_up_kernel, [shape(block, ff)], args, clock=clock, name="grad_up")

    def small_sums():
        out, args = [shape(PACK, block, dtype=bf16)], [idx, *o.lines["kv"].ends()]
        (x,) = call(functools.partial(small_kernel, block), out, args, clock=clock, name="small")
        o.total = x.astype(f32) + swap(x, "tp", 1).astype(f32)

    def finish():
        o.grad_qkv, o.grad_out = call(
            functools.partial(finish_kernel, block),
            [shape(3 * block, hc), shape(hc, block)],
            [idx, *o.lines["kv"].ends(), *o.lines["qo"].ends()],
            clock=clock,
            name="finish",
        )

    def ffn_out():
        (o.ffn,) = call(functools.partial(down_kernel, nf), [wide(dtype=bf16)], [idx, active, *wd], clock=clock, name="ffn")

    def start_up():
        o.up = shard_sum(("u", "ua", "ub"), [(first, (normed2, gh)), (second, (normed2, gh))])
        o.up.start()

    def start_rest():
        kv = (("all", "all", "small"), (normed, o.gk, normed, o.gv, o.pack))
        qo = (("all", "out"), (normed, o.gq, mixed, o.gb))
        o.rest = shard_sum(("t", "kv", "qo"), [kv, qo])
        o.rest.start()

    o.down = down
    places = {"da": ("down", 0), "db": ("down", 1), "ua": ("up", 0), "ub": ("up", 1), "kv": ("rest", 0), "qo": ("rest", 1)}
    steps = {
        "back": back,
        "normed": normed_back,
        "outputs": outputs,
        "relay": relay,
        "assemble": assemble,
        "split": split,
        "grad_down": finish_down,
        "grad_up": finish_up,
        "small": small_sums,
        "finish": finish,
        "ffn": ffn_out,
        "u0": start_up,
        "t0": start_rest,
    }
    for name in ORDER:
        if name in steps:
            steps[name]()
        elif name[-1] == "1":
            which, piece = places[name[:-1]]
            one = getattr(o, which)
            one.send(one.begin(piece), piece)
        elif name[-1] == "2":
            which, piece = places[name[:-1]]
            one = getattr(o, which)
            for _ in range(2, levels):
                one.send(one.begin(piece), piece)
            o.lines[name[:-1]] = Line(one.own(piece), idx, clock)
        else:
            o.lines[name].advance(name)
    total = o.total[:]
    return (
        o.result,
        o.grad_inputs,
        total[0],
        total[1],
        o.grad_qkv.reshape(3, block, hc).transpose(1, 0, 2),
        total[6:8],
        o.grad_out,
        total[4],
        total[2],
        total[3],
        o.grad_up,
        total[8 : 8 + n_up].reshape(-1),
        o.grad_down,
        total[5],
    )


def solution(mesh):
    in_specs = (
        P("fsdp", "ctx", None),
        P("fsdp"),
        P("fsdp"),
        P("fsdp"),
        P("fsdp", None, "tp"),
        P(None, "fsdp"),
        P("tp", "fsdp"),
        P("fsdp"),
        P("fsdp"),
        P("fsdp"),
        P("fsdp", "tp"),
        P("fsdp"),
        P("tp", "fsdp"),
        P("fsdp"),
        P("fsdp", "ctx", None),
    )
    out_specs = (
        P("fsdp", "ctx", None),
        P("fsdp", "ctx", None),
        P("fsdp"),
        P("fsdp"),
        P("fsdp", None, "tp"),
        P(None, "fsdp"),
        P("tp", "fsdp"),
        P("fsdp"),
        P("fsdp"),
        P("fsdp"),
        P("fsdp", "tp"),
        P("fsdp"),
        P("tp", "fsdp"),
        P("fsdp"),
    )
    return jax.shard_map(local, mesh=mesh, in_specs=in_specs, out_specs=out_specs, check_vma=False)
```
